32 devices in a mesh: wa: 4 (over y, x), ha: 4 (over z), row: 2 (over core).
Axes of the slice: x: 2, y: 2, z: 4, core: 2. Of those that a mesh axis runs over, the one named last changes fastest.
Arguments:
- tokens: bfloat16 [160, 5120], P(('row', 'ha'), 'wa'), may hold values from -6 to 6
- cotangent: bfloat16 [160, 5120], P(('row', 'ha'), 'wa'), may hold values from -6 to 6
- gate_weight: bfloat16 [5120, 13824], P('wa', 'ha'), may hold values from -0.078125 to 0.078125
- up_weight: bfloat16 [5120, 13824], P('wa', 'ha'), may hold values from -0.078125 to 0.078125
- down_weight: bfloat16 [13824, 5120], P('ha', 'wa'), may hold values from -0.0546875 to 0.0546875
Outputs:
- grad_tokens: bfloat16 [160, 5120], P(('row', 'ha'), 'wa')
- grad_gate: bfloat16 [5120, 13824], P('wa', 'ha')
- grad_up: bfloat16 [5120, 13824], P('wa', 'ha')
- grad_down: bfloat16 [13824, 5120], P('ha', 'wa')
The draws below stay inside these ranges and needn't reach their ends.
All inputs are finite; a program needn't handle non-finite values.
Results may differ from the reference program's by a relative error of at most 0.0059.
Values may be sent and summed in bfloat16 or wider, within the bound.
No kernel may reach another device: no remote copies, remote signals or barrier semaphores. Data moves between devices by JAX's collectives and lax.ppermute only.
A program may use at most 128 MiB of HBM per device.

```python
import jax
import jax.numpy as jnp
from jax import lax

D = 5120
FF = 13824
TOK_DEV = 20
TOKENS = 160
N_HA = 4
N_ROW = 2


def level_of(key, shape, shards, least, top_value):
    def one(axis_at, shards_of):
        draws = jax.random.uniform(jax.random.fold_in(jax.random.fold_in(key, 6), axis_at), (shards_of,), jnp.float32, least / len(shards), top_value / len(shards))
        return jnp.repeat(jnp.exp(draws), shape[axis_at] // shards_of).reshape((-1,) + (1,) * (len(shape) - axis_at - 1))

    level = one(*shards[0])
    for cut in shards[1:]:
        level = level * one(*cut)
    return level


def scatter_about(own_key, extent, scale, most, cuts=(), kind=jnp.bfloat16):
    drawn = jax.random.normal(own_key, extent, jnp.float32) * scale
    if len(cuts) > 0:
        drawn = level_of(own_key, extent, cuts, -0.22, 0.18) * drawn
    return jnp.clip(drawn, min=-most, max=most).astype(kind)


def setup_inputs(seed: int = 0) -> dict:
    splits = jax.random.split(jax.random.key(seed), 6)
    tokens = scatter_about(splits[0], (TOKENS, D), 1.0, 6.0, ((0, 8), (1, 4)))
    cotangent = scatter_about(splits[1], (TOKENS, D), 0.5, 6.0, ((0, 8), (1, 4)))
    gate_weight = scatter_about(splits[2], (D, FF), D ** -0.5, 0.078125, ((0, 4), (1, 4)))
    up_weight = scatter_about(splits[3], (D, FF), D ** -0.5, 0.078125, ((0, 4), (1, 4)))
    down_weight = scatter_about(splits[4], (FF, D), FF ** -0.5, 0.0546875, ((0, 4), (1, 4)))
    return dict(tokens=tokens, cotangent=cotangent, gate_weight=gate_weight, up_weight=up_weight, down_weight=down_weight)


def rounded(value):
    return lax.optimization_barrier(value.astype(jnp.bfloat16)).astype(jnp.float32)


def reference(tokens, cotangent, gate_weight, up_weight, down_weight):
    group_rows = TOK_DEV * N_HA
    grad_rows = []
    total_gate = jnp.zeros((D, FF), jnp.float32)
    total_up = jnp.zeros((D, FF), jnp.float32)
    total_down = jnp.zeros((FF, D), jnp.float32)
    for replica in range(N_ROW):
        rows_in = tokens[replica * group_rows:(replica + 1) * group_rows]
        grads_in = cotangent[replica * group_rows:(replica + 1) * group_rows]
        gate_sum = jnp.dot(rows_in, gate_weight, preferred_element_type=jnp.float32)
        up_sum = jnp.dot(rows_in, up_weight, preferred_element_type=jnp.float32)
        dh_sum = jnp.dot(grads_in, down_weight.T, preferred_element_type=jnp.float32)
        sig = jax.nn.sigmoid(gate_sum)
        active = gate_sum * sig
        hidden = (active * up_sum).astype(jnp.bfloat16)
        d_up = (dh_sum * active).astype(jnp.bfloat16)
        d_gate = (dh_sum * up_sum * sig * (1.0 + gate_sum * (1.0 - sig))).astype(jnp.bfloat16)
        grad_x = jnp.dot(d_gate, gate_weight.T, preferred_element_type=jnp.float32) + jnp.dot(d_up, up_weight.T, preferred_element_type=jnp.float32)
        grad_rows.append(grad_x.astype(jnp.bfloat16))
        total_gate = total_gate + rounded(jnp.dot(rows_in.T, d_gate, preferred_element_type=jnp.float32))
        total_up = total_up + rounded(jnp.dot(rows_in.T, d_up, preferred_element_type=jnp.float32))
        total_down = total_down + rounded(jnp.dot(hidden.T, grads_in, preferred_element_type=jnp.float32))
    grad_tokens = jnp.concatenate(grad_rows, axis=0)
    return (grad_tokens, total_gate.astype(jnp.bfloat16), total_up.astype(jnp.bfloat16), total_down.astype(jnp.bfloat16))
```

```python
import functools

import jax
import jax.numpy as jnp
from jax import lax
from jax.experimental import pallas as pl
from jax.experimental.pallas import tpu as pltpu
from jax.sharding import PartitionSpec as P

BF16 = jnp.bfloat16
F32 = jnp.float32
NT = (((1,), (1,)), ((), ()))
TN = (((0,), (0,)), ((), ()))
LANES = 128
CHUNKS = 3
VMEM_LIMIT = 48 * 1024 * 1024


def pointwise(gate_sum, up_sum, dh_sum):
    sig = jax.nn.sigmoid(gate_sum)
    active = gate_sum * sig
    hidden = (active * up_sum).astype(BF16)
    d_up = (dh_sum * active).astype(BF16)
    d_gate = (dh_sum * up_sum * sig * (1.0 + gate_sum * (1.0 - sig))).astype(BF16)
    return (hidden, d_gate, d_up)


def call(kernel, grid, in_specs, out_specs, out_shape, flops, moved, scratch=(), aliases=None):
    return pl.pallas_call(
        kernel,
        grid=grid,
        in_specs=in_specs,
        out_specs=out_specs,
        out_shape=out_shape,
        scratch_shapes=list(scratch),
        input_output_aliases=aliases or {},
        cost_estimate=pl.CostEstimate(flops=flops, bytes_accessed=moved, transcendentals=0),
        compiler_params=pltpu.CompilerParams(vmem_limit_bytes=VMEM_LIMIT),
    )


def whole(shape):
    return pl.BlockSpec(shape, lambda i: (0,) * len(shape))


SCALAR = pl.BlockSpec(memory_space=pltpu.SMEM)


def order_kernel(parts, rows, wa_ref, *refs):
    pieces = [ref[...].astype(F32) for ref in refs[:parts]]
    x_ref, y_ref = refs[parts:]
    wa = wa_ref[0]
    xs, ys = [], []
    for slot in range(parts):
        at = wa ^ slot
        piece = pieces[0]
        for other in range(1, parts):
            piece = jnp.where(at == other, pieces[other], piece)
        xs.append(piece[:rows])
        ys.append(piece[rows:])
    x_ref[...] = jnp.concatenate(xs, axis=0).astype(BF16)
    y_ref[...] = jnp.concatenate(ys, axis=0).astype(BF16)


def order_rows(wa, pieces):
    parts = len(pieces)
    rows, width = pieces[0].shape[0] // 2, pieces[0].shape[1]
    shape = (parts * rows, width)
    return call(
        functools.partial(order_kernel, parts, rows),
        (1,),
        [SCALAR] + [whole((2 * rows, width))] * parts,
        [whole(shape)] * 2,
        [jax.ShapeDtypeStruct(shape, BF16)] * 2,
        0,
        8 * shape[0] * width,
    )(wa, *pieces)


def forward_kernel(parts, rows, x_ref, y_ref, gate_ref, up_ref, down_ref, own_ref, *send_refs):
    gate = jnp.dot(x_ref[...], gate_ref[...], preferred_element_type=F32)
    up = jnp.dot(x_ref[...], up_ref[...], preferred_element_type=F32)
    dh = lax.dot_general(y_ref[...], down_ref[...], NT, preferred_element_type=F32)
    for slot in range(parts):
        cut = slice(slot * rows, (slot + 1) * rows)
        block = jnp.concatenate([gate[cut], up[cut], dh[cut]], axis=0)
        if slot == 0:
            own_ref[...] = block
        else:
            send_refs[slot - 1][...] = block.astype(BF16)


def forward(parts, first, count, tile, x, y, gate_weight, up_weight, down_weight):
    group, width = x.shape
    rows = group // parts
    columns = count * tile
    return call(
        functools.partial(forward_kernel, parts, rows),
        (count,),
        [
            whole((group, width)),
            whole((group, width)),
            pl.BlockSpec((width, tile), lambda i: (0, first + i)),
            pl.BlockSpec((width, tile), lambda i: (0, first + i)),
            pl.BlockSpec((tile, width), lambda i: (first + i, 0)),
        ],
        [pl.BlockSpec((3 * rows, tile), lambda i: (0, i))] * parts,
        [jax.ShapeDtypeStruct((3 * rows, columns), F32)]
        + [jax.ShapeDtypeStruct((3 * rows, columns), BF16)] * (parts - 1),
        6 * group * width * columns,
        6 * width * columns,
    )(x, y, gate_weight, up_weight, down_weight)


def middle_kernel(rows, own_ref, *refs):
    total = own_ref[...]
    for ref in refs[:-1]:
        total = total + ref[...].astype(F32)
    hidden, d_gate, d_up = pointwise(total[:rows], total[rows : 2 * rows], total[2 * rows :])
    refs[-1][...] = jnp.concatenate(
        [d_gate.astype(F32), d_up.astype(F32), hidden.astype(F32)], axis=0
    ).astype(BF16)


def middle(own, received):
    shape = own.shape
    return call(
        functools.partial(middle_kernel, shape[0] // 3),
        (1,),
        [whole(shape)] * (1 + len(received)),
        whole(shape),
        jax.ShapeDtypeStruct(shape, BF16),
        20 * shape[0] * shape[1],
        12 * shape[0] * shape[1],
    )(own, *received)


def stack_kernel(rows, *refs):
    blocks = [ref[...].astype(F32) for ref in refs[:-1]]
    cuts = [
        block[at * rows : (at + 1) * rows] for at in range(3) for block in blocks
    ]
    refs[-1][...] = jnp.concatenate(cuts, axis=0).astype(BF16)


def stack(blocks):
    parts = len(blocks)
    rows, columns = blocks[0].shape[0] // 3, blocks[0].shape[1]
    shape = (3 * parts * rows, columns)
    return call(
        functools.partial(stack_kernel, rows),
        (1,),
        [whole(blocks[0].shape)] * parts,
        whole(shape),
        jax.ShapeDtypeStruct(shape, BF16),
        0,
        4 * shape[0] * columns,
    )(*blocks)


def input_grad_kernel(group, start_ref, d_gate_ref, d_up_ref, gate_ref, up_ref, out_ref):
    @pl.when(pl.program_id(0) == 0)
    def _():
        out_ref[...] = start_ref[...]

    out_ref[...] += lax.dot_general(
        d_gate_ref[...], gate_ref[...], NT, preferred_element_type=F32
    ) + lax.dot_general(d_up_ref[...], up_ref[...], NT, preferred_element_type=F32)


def input_grad(first, count, tile, start, stacked, gate_weight, up_weight):
    group = stacked.shape[0] // 3
    width = gate_weight.shape[0]
    return call(
        functools.partial(input_grad_kernel, group),
        (count,),
        [
            whole((group, width)),
            pl.BlockSpec((group, tile), lambda i: (0, i)),
            pl.BlockSpec((group, tile), lambda i: (1, i)),
            pl.BlockSpec((width, tile), lambda i: (0, first + i)),
            pl.BlockSpec((width, tile), lambda i: (0, first + i)),
        ],
        whole((group, width)),
        jax.ShapeDtypeStruct((group, width), F32),
        4 * group * width * count * tile,
        4 * width * count * tile,
    )(start, stacked, stacked, gate_weight, up_weight)


def weight_grad_kernel(group, has_start, row_ref, xt_ref, y_ref, mine_ref, other_ref, *refs):
    gate_ref, up_ref, down_ref, both = refs[3 * has_start :]
    first = row_ref[0] == 0
    for at in range(3):
        cut = slice(at * group, (at + 1) * group)
        both[at, :group] = jnp.where(first, mine_ref[cut], other_ref[cut])
        both[at, group:] = jnp.where(first, other_ref[cut], mine_ref[cut])
    gate_ref[...] = jnp.dot(xt_ref[...], both[0], preferred_element_type=F32).astype(BF16)
    up_ref[...] = jnp.dot(xt_ref[...], both[1], preferred_element_type=F32).astype(BF16)
    down_ref[...] = lax.dot_general(
        both[2], y_ref[...], TN, preferred_element_type=F32
    ).astype(BF16)


def weight_grad(first, count, tile, hidden_width, row, xt, y, mine, other, start):
    width = xt.shape[0]
    group = mine.shape[0] // 3
    has_start = start is not None
    start = start or ()
    return call(
        functools.partial(weight_grad_kernel, group, has_start),
        (count,),
        [
            SCALAR,
            whole((width, 2 * group)),
            whole((2 * group, width)),
            pl.BlockSpec((3 * group, tile), lambda i: (0, i)),
            pl.BlockSpec((3 * group, tile), lambda i: (0, i)),
        ]
        + [pl.BlockSpec(memory_space=pl.ANY)] * len(start),
        [
            pl.BlockSpec((width, tile), lambda i: (0, first + i)),
            pl.BlockSpec((width, tile), lambda i: (0, first + i)),
            pl.BlockSpec((tile, width), lambda i: (first + i, 0)),
        ],
        [
            jax.ShapeDtypeStruct((width, hidden_width), BF16),
            jax.ShapeDtypeStruct((width, hidden_width), BF16),
            jax.ShapeDtypeStruct((hidden_width, width), BF16),
        ],
        12 * group * width * count * tile,
        6 * width * count * tile,
        scratch=[pltpu.VMEM((3, 2 * group, tile), BF16)],
        aliases={5 + i: i for i in range(len(start))},
    )(row, xt, y, mine, other, *start)


def last_kernel(parts, rows, wa_ref, grad_ref, own_ref, *send_refs):
    grad = grad_ref[...]
    cuts = [grad[slot * rows : (slot + 1) * rows] for slot in range(parts)]
    wa = wa_ref[0]
    for step in range(parts):
        at = wa ^ step
        piece = cuts[0]
        for slot in range(1, parts):
            piece = jnp.where(at == slot, cuts[slot], piece)
        if step == 0:
            own_ref[...] = piece
        else:
            send_refs[step - 1][...] = piece.astype(BF16)


def last_pieces(parts, wa, grad):
    rows, width = grad.shape[0] // parts, grad.shape[1]
    return call(
        functools.partial(last_kernel, parts, rows),
        (1,),
        [SCALAR, whole(grad.shape)],
        [whole((rows, width))] * parts,
        [jax.ShapeDtypeStruct((rows, width), F32)]
        + [jax.ShapeDtypeStruct((rows, width), BF16)] * (parts - 1),
        0,
        8 * grad.shape[0] * width,
    )(wa, grad)


def swap(value, axis, size, step):
    return lax.ppermute(value, axis, [(at, at ^ step) for at in range(size)])


def fast_body(n_wa, n_ha, n_row, tokens, cotangent, gate_weight, up_weight, down_weight):
    rows, width = tokens.shape
    hidden_width = gate_weight.shape[1]
    columns = hidden_width // CHUNKS
    tile = max(t for t in range(LANES, 513, LANES) if columns % t == 0)
    count = columns // tile
    group = n_ha * rows
    wa = lax.axis_index("wa").astype(jnp.int32).reshape(1)
    row = lax.axis_index("row").astype(jnp.int32).reshape(1)

    both = jnp.concatenate([tokens, cotangent], axis=0)
    pieces = [both] + [swap(both, "ha", n_ha, step) for step in range(1, n_ha)]
    x, y = order_rows(wa, pieces)

    blocks = []
    for chunk in range(CHUNKS):
        own, *sends = forward(
            n_wa, chunk * count, count, tile, x, y, gate_weight, up_weight, down_weight
        )
        blocks.append((own, [swap(s, "wa", n_wa, k + 1) for k, s in enumerate(sends)]))

    xy = jnp.concatenate([x, y], axis=0)
    xy_other = swap(xy, "row", n_row, 1)
    first = row[0] == 0
    x_low, x_high = jnp.where(first, xy[:group], xy_other[:group]), jnp.where(first, xy_other[:group], xy[:group])
    y_low, y_high = jnp.where(first, xy[group:], xy_other[group:]), jnp.where(first, xy_other[group:], xy[group:])
    xt = jnp.concatenate([x_low, x_high], axis=0).T
    y_all = jnp.concatenate([y_low, y_high], axis=0)

    gathered = []
    for own, received in blocks:
        mine = middle(own, received)
        gathered.append([mine] + [swap(mine, "wa", n_wa, step) for step in range(1, n_wa)])

    grad = jnp.zeros((group, width), F32)
    stacks = []
    for chunk in range(CHUNKS):
        mine = stack(gathered[chunk])
        stacks.append((mine, swap(mine, "row", n_row, 1)))
        grad = input_grad(chunk * count, count, tile, grad, mine, gate_weight, up_weight)
    own, *sends = last_pieces(n_ha, wa, grad)
    for step, sent in enumerate(sends):
        own = own + swap(sent, "ha", n_ha, step + 1).astype(F32)

    grads = None
    for chunk, (mine, other) in enumerate(stacks):
        grads = weight_grad(
            chunk * count, count, tile, hidden_width, row, xt, y_all, mine, other, grads
        )
    return (own.astype(BF16), *grads)


def plain_body(tokens, cotangent, gate_weight, up_weight, down_weight):
    hidden_width = gate_weight.shape[1]
    x = lax.all_gather(tokens, "ha", axis=0, tiled=True)
    y = lax.all_gather(cotangent, "ha", axis=0, tiled=True)
    gate_part = jnp.dot(x, gate_weight, preferred_element_type=F32)
    up_part = jnp.dot(x, up_weight, preferred_element_type=F32)
    dh_part = lax.dot_general(y, down_weight, NT, preferred_element_type=F32)
    summed = lax.psum(jnp.concatenate([gate_part, up_part, dh_part], axis=1), "wa")
    hidden, d_gate, d_up = pointwise(
        summed[:, :hidden_width],
        summed[:, hidden_width : 2 * hidden_width],
        summed[:, 2 * hidden_width :],
    )
    partial = lax.dot_general(
        d_gate, gate_weight, NT, preferred_element_type=F32
    ) + lax.dot_general(d_up, up_weight, NT, preferred_element_type=F32)
    grad_tokens = lax.psum_scatter(partial, "ha", scatter_dimension=0, tiled=True)
    grads = (
        lax.dot_general(x, d_gate, TN, preferred_element_type=F32),
        lax.dot_general(x, d_up, TN, preferred_element_type=F32),
        lax.dot_general(hidden, y, TN, preferred_element_type=F32),
    )
    return (
        grad_tokens.astype(BF16),
        *(lax.psum(g.astype(BF16), "row").astype(BF16) for g in grads),
    )


def solution(mesh):
    n_wa, n_ha, n_row = (mesh.shape[name] for name in ("wa", "ha", "row"))

    def body(tokens, cotangent, gate_weight, up_weight, down_weight):
        width, hidden_width = gate_weight.shape
        fits = (
            n_wa == n_ha == 4
            and n_row == 2
            and width % LANES == 0
            and hidden_width % (LANES * CHUNKS) == 0
            and (tokens.shape[0] * n_ha) % 16 == 0
        )
        if fits:
            return fast_body(
                n_wa, n_ha, n_row, tokens, cotangent, gate_weight, up_weight, down_weight
            )
        return plain_body(tokens, cotangent, gate_weight, up_weight, down_weight)

    return jax.shard_map(
        body,
        mesh=mesh,
        in_specs=(
            P(("row", "ha"), "wa"),
            P(("row", "ha"), "wa"),
            P("wa", "ha"),
            P("wa", "ha"),
            P("ha", "wa"),
        ),
        out_specs=(P(("row", "ha"), "wa"), P("wa", "ha"), P("wa", "ha"), P("ha", "wa")),
        check_vma=False,
    )
```

```python
import functools

import jax
import jax.numpy as jnp
from jax import lax
from jax.experimental import pallas as pl
from jax.experimental.pallas import tpu as pltpu
from jax.sharding import PartitionSpec as P

BF16 = jnp.bfloat16
F32 = jnp.float32
NT = (((1,), (1,)), ((), ()))
TN = (((0,), (0,)), ((), ()))
LANES = 128
CHUNKS = 3
MIB = 1024 * 1024


def pointwise(gate_sum, up_sum, dh_sum):
    sig = jax.nn.sigmoid(gate_sum)
    active = gate_sum * sig
    hidden = (active * up_sum).astype(BF16)
    d_up = (dh_sum * active).astype(BF16)
    d_gate = (dh_sum * up_sum * sig * (1.0 + gate_sum * (1.0 - sig))).astype(BF16)
    return (hidden, d_gate, d_up)


def call(
    kernel, grid, in_specs, out_specs, out_shape, flops, moved, scratch=(), aliases=None, limit=4
):
    return pl.pallas_call(
        kernel,
        grid=grid,
        in_specs=in_specs,
        out_specs=out_specs,
        out_shape=out_shape,
        scratch_shapes=list(scratch),
        input_output_aliases=aliases or {},
        cost_estimate=pl.CostEstimate(flops=flops, bytes_accessed=moved, transcendentals=0),
        compiler_params=pltpu.CompilerParams(vmem_limit_bytes=limit * MIB),
    )


def whole(shape):
    return pl.BlockSpec(shape, lambda i: (0,) * len(shape))


SCALAR = pl.BlockSpec(memory_space=pltpu.SMEM)
IN_VMEM = pl.BlockSpec(memory_space=pltpu.VMEM)
TOKEN = jax.ShapeDtypeStruct((8, LANES), F32)


def order_kernel(parts, rows, wa_ref, *refs):
    pieces = [ref[...].astype(F32) for ref in refs[:parts]]
    x_ref, y_ref = refs[parts:]
    wa = wa_ref[0]
    xs, ys = [], []
    for slot in range(parts):
        at = wa ^ slot
        piece = pieces[0]
        for other in range(1, parts):
            piece = jnp.where(at == other, pieces[other], piece)
        xs.append(piece[:rows])
        ys.append(piece[rows:])
    x_ref[...] = jnp.concatenate(xs, axis=0).astype(BF16)
    y_ref[...] = jnp.concatenate(ys, axis=0).astype(BF16)


def order_rows(wa, pieces):
    parts = len(pieces)
    rows, width = pieces[0].shape[0] // 2, pieces[0].shape[1]
    shape = (parts * rows, width)
    return call(
        functools.partial(order_kernel, parts, rows),
        (),
        [SCALAR] + [IN_VMEM] * parts,
        [IN_VMEM] * 2,
        [jax.ShapeDtypeStruct(shape, BF16)] * 2,
        0,
        8 * shape[0] * width,
    )(wa, *pieces)


def forward_kernel(parts, rows, begin, x_ref, y_ref, gate_ref, up_ref, down_ref, own_ref, *send_refs):
    there = pl.ds(begin, own_ref.shape[1])
    gate = jnp.dot(x_ref[...], gate_ref[:, there], preferred_element_type=F32)
    up = jnp.dot(x_ref[...], up_ref[:, there], preferred_element_type=F32)
    dh = lax.dot_general(y_ref[...], down_ref[there, :], NT, preferred_element_type=F32)
    for slot in range(parts):
        cut = slice(slot * rows, (slot + 1) * rows)
        block = jnp.concatenate([gate[cut], up[cut], dh[cut]], axis=0)
        if slot == 0:
            own_ref[...] = block
        else:
            send_refs[slot - 1][...] = block.astype(BF16)


def load_kernel(cuts, *refs):
    count = (len(refs) - 1) // 2
    sems = refs[-1]
    copies = []
    for at in range(count):
        rows = refs[at].shape[0] // cuts
        for cut in range(cuts):
            part = pl.ds(cut * rows, rows)
            copies.append(
                pltpu.make_async_copy(
                    refs[at].at[part], refs[count + at].at[part], sems.at[at, cut]
                )
            )
    for copy in copies:
        copy.start()
    for copy in copies:
        copy.wait()


def load(*weights):
    cuts = 4
    return pl.pallas_call(
        functools.partial(load_kernel, cuts),
        in_specs=[pl.BlockSpec(memory_space=pl.ANY)] * len(weights),
        out_specs=[IN_VMEM] * len(weights),
        out_shape=[pltpu.VMEM(w.shape, w.dtype) for w in weights],
        scratch_shapes=[pltpu.SemaphoreType.DMA((len(weights), cuts))],
        cost_estimate=pl.CostEstimate(
            flops=0, bytes_accessed=sum(2 * w.size for w in weights), transcendentals=0
        ),
        compiler_params=pltpu.CompilerParams(vmem_limit_bytes=34 * MIB),
    )(*weights)


def forward(parts, first, count, tile, x, y, gate_weight, up_weight, down_weight):
    group, width = x.shape
    rows = group // parts
    columns = count * tile
    return call(
        functools.partial(forward_kernel, parts, rows, first * tile),
        (),
        [IN_VMEM] * 5,
        [IN_VMEM] * parts,
        [jax.ShapeDtypeStruct((3 * rows, columns), F32)]
        + [jax.ShapeDtypeStruct((3 * rows, columns), BF16)] * (parts - 1),
        6 * group * width * columns,
        6 * width * columns,
    )(x, y, gate_weight, up_weight, down_weight)


def middle_kernel(rows, own_ref, *refs):
    total = own_ref[...]
    for ref in refs[:-1]:
        total = total + ref[...].astype(F32)
    hidden, d_gate, d_up = pointwise(total[:rows], total[rows : 2 * rows], total[2 * rows :])
    refs[-1][...] = jnp.concatenate(
        [d_gate.astype(F32), d_up.astype(F32), hidden.astype(F32)], axis=0
    ).astype(BF16)


def middle(own, received):
    shape = own.shape
    return call(
        functools.partial(middle_kernel, shape[0] // 3),
        (),
        [IN_VMEM] * (1 + len(received)),
        IN_VMEM,
        jax.ShapeDtypeStruct(shape, BF16),
        20 * shape[0] * shape[1],
        12 * shape[0] * shape[1],
    )(own, *received)


def stack_kernel(rows, *refs):
    blocks = [ref[...].astype(F32) for ref in refs[:-1]]
    cuts = [
        block[at * rows : (at + 1) * rows] for at in range(3) for block in blocks
    ]
    refs[-1][...] = jnp.concatenate(cuts, axis=0).astype(BF16)


def stack(blocks):
    parts = len(blocks)
    rows, columns = blocks[0].shape[0] // 3, blocks[0].shape[1]
    shape = (3 * parts * rows, columns)
    return call(
        functools.partial(stack_kernel, rows),
        (),
        [IN_VMEM] * parts,
        IN_VMEM,
        jax.ShapeDtypeStruct(shape, BF16),
        0,
        4 * shape[0] * columns,
    )(*blocks)


def input_grad_kernel(group, begin, after, stack_ref, gate_ref, up_ref, *refs):
    there = pl.ds(begin, stack_ref.shape[1])
    grad = lax.dot_general(
        stack_ref[:group], gate_ref[:, there], NT, preferred_element_type=F32
    ) + lax.dot_general(
        stack_ref[group : 2 * group], up_ref[:, there], NT, preferred_element_type=F32
    )
    refs[-1][...] = grad + refs[0][...] if after else grad


def input_grad(begin, stacked, gate_weight, up_weight, after):
    group, columns = stacked.shape[0] // 3, stacked.shape[1]
    width = gate_weight.shape[0]
    return call(
        functools.partial(input_grad_kernel, group, begin, bool(after)),
        (),
        [IN_VMEM] * (3 + len(after)),
        IN_VMEM,
        jax.ShapeDtypeStruct((group, width), F32),
        4 * group * width * columns,
        4 * width * columns,
    )(stacked, gate_weight, up_weight, *after)


def factors_kernel(group, row_ref, x_ref, y_ref, other_ref, xt_ref, y_all_ref):
    first = row_ref[0] == 0
    x, y = x_ref[...], y_ref[...]
    x_other, y_other = other_ref[:group], other_ref[group:]
    y_all_ref[:group] = jnp.where(first, y, y_other)
    y_all_ref[group:] = jnp.where(first, y_other, y)
    x_all = jnp.concatenate([jnp.where(first, x, x_other), jnp.where(first, x_other, x)], axis=0)
    xt_ref[...] = x_all.T


def factors(row, x, y, other):
    group, width = x.shape
    return call(
        functools.partial(factors_kernel, group),
        (),
        [SCALAR] + [IN_VMEM] * 3,
        [IN_VMEM] * 2,
        [
            jax.ShapeDtypeStruct((width, 2 * group), BF16),
            jax.ShapeDtypeStruct((2 * group, width), BF16),
        ],
        0,
        8 * group * width,
    )(row, x, y, other)


def join_kernel(first_ref, second_ref, out_ref):
    out_ref[...] = jnp.concatenate(
        [first_ref[...].astype(F32), second_ref[...].astype(F32)], axis=0
    ).astype(BF16)


def join(first, second):
    shape = (first.shape[0] + second.shape[0], first.shape[1])
    return call(
        join_kernel,
        (),
        [IN_VMEM] * 2,
        IN_VMEM,
        jax.ShapeDtypeStruct(shape, BF16),
        0,
        4 * shape[0] * shape[1],
    )(first, second)


def total_kernel(own_ref, *refs):
    total = own_ref[...]
    for ref in refs[:-1]:
        total = total + ref[...].astype(F32)
    refs[-1][...] = total.astype(BF16)


def total(own, received):
    return call(
        total_kernel,
        (),
        [IN_VMEM] * (1 + len(received)),
        IN_VMEM,
        jax.ShapeDtypeStruct(own.shape, BF16),
        4 * own.size,
        12 * own.size,
    )(own, *received)


def weight_grad_kernel(group, has_start, row_ref, xt_ref, y_ref, mine_ref, other_ref, *refs):
    gate_ref, up_ref, down_ref, token_ref, both = refs[3 * has_start :]
    token_ref[...] = jnp.zeros_like(token_ref)
    first = row_ref[0] == 0
    for at in range(3):
        cut = slice(at * group, (at + 1) * group)
        both[at, :group] = jnp.where(first, mine_ref[cut], other_ref[cut])
        both[at, group:] = jnp.where(first, other_ref[cut], mine_ref[cut])
    gate_ref[...] = jnp.dot(xt_ref[...], both[0], preferred_element_type=F32).astype(BF16)
    up_ref[...] = jnp.dot(xt_ref[...], both[1], preferred_element_type=F32).astype(BF16)
    down_ref[...] = lax.dot_general(
        both[2], y_ref[...], TN, preferred_element_type=F32
    ).astype(BF16)


def weight_grad(first, count, tile, hidden_width, row, xt, y, mine, other, start):
    width = xt.shape[0]
    group = mine.shape[0] // 3
    has_start = start is not None
    start = start or ()
    return call(
        functools.partial(weight_grad_kernel, group, has_start),
        (count,),
        [
            SCALAR,
            whole((width, 2 * group)),
            whole((2 * group, width)),
            pl.BlockSpec((3 * group, tile), lambda i: (0, i)),
            pl.BlockSpec((3 * group, tile), lambda i: (0, i)),
        ]
        + [pl.BlockSpec(memory_space=pl.ANY)] * len(start),
        [
            pl.BlockSpec((width, tile), lambda i: (0, first + i)),
            pl.BlockSpec((width, tile), lambda i: (0, first + i)),
            pl.BlockSpec((tile, width), lambda i: (first + i, 0)),
            whole(TOKEN.shape),
        ],
        [
            jax.ShapeDtypeStruct((width, hidden_width), BF16),
            jax.ShapeDtypeStruct((width, hidden_width), BF16),
            jax.ShapeDtypeStruct((hidden_width, width), BF16),
            TOKEN,
        ],
        12 * group * width * count * tile,
        6 * width * count * tile,
        scratch=[pltpu.VMEM((3, 2 * group, tile), BF16)],
        aliases={5 + i: i for i in range(len(start))},
        limit=16,
    )(row, xt, y, mine, other, *start)


def last_kernel(parts, rows, wa_ref, grad_ref, own_ref, *send_refs):
    grad = grad_ref[...]
    cuts = [grad[slot * rows : (slot + 1) * rows] for slot in range(parts)]
    wa = wa_ref[0]
    for step in range(parts):
        at = wa ^ step
        piece = cuts[0]
        for slot in range(1, parts):
            piece = jnp.where(at == slot, cuts[slot], piece)
        if step == 0:
            own_ref[...] = piece
        else:
            send_refs[step - 1][...] = piece.astype(BF16)


def last_pieces(parts, wa, grad):
    rows, width = grad.shape[0] // parts, grad.shape[1]
    return call(
        functools.partial(last_kernel, parts, rows),
        (),
        [SCALAR, IN_VMEM],
        [IN_VMEM] * parts,
        [jax.ShapeDtypeStruct((rows, width), F32)]
        + [jax.ShapeDtypeStruct((rows, width), BF16)] * (parts - 1),
        0,
        8 * grad.shape[0] * width,
    )(wa, grad)


def swap(value, axis, size, step):
    return lax.ppermute(value, axis, [(at, at ^ step) for at in range(size)])


def fast_body(n_wa, n_ha, n_row, tokens, cotangent, gate_weight, up_weight, down_weight):
    rows, width = tokens.shape
    hidden_width = gate_weight.shape[1]
    columns = hidden_width // CHUNKS
    tile = max(t for t in range(LANES, 513, LANES) if columns % t == 0)
    count = columns // tile
    group = n_ha * rows
    wa = lax.axis_index("wa").astype(jnp.int32).reshape(1)
    row = lax.axis_index("row").astype(jnp.int32).reshape(1)

    both = join(tokens, cotangent)
    gate_weight, up_weight, down_weight = load(gate_weight, up_weight, down_weight)
    pieces = [both] + [swap(both, "ha", n_ha, step) for step in range(1, n_ha)]
    x, y = order_rows(wa, pieces)

    blocks = []
    for chunk in range(CHUNKS):
        own, *sends = forward(
            n_wa, chunk * count, count, tile, x, y, gate_weight, up_weight, down_weight
        )
        blocks.append((own, [swap(s, "wa", n_wa, k + 1) for k, s in enumerate(sends)]))
    xt, y_all = factors(row, x, y, swap(join(x, y), "row", n_row, 1))

    gathered = []
    for own, received in blocks:
        mine = middle(own, received)
        gathered.append([mine] + [swap(mine, "wa", n_wa, step) for step in range(1, n_wa)])

    grads, after = None, ()
    for chunk in range(CHUNKS):
        mine = stack(gathered[chunk])
        other = swap(mine, "row", n_row, 1)
        grad = input_grad(chunk * columns, mine, gate_weight, up_weight, after)
        if chunk == CHUNKS - 1:
            own, *sends = last_pieces(n_ha, wa, grad)
            received = [swap(sent, "ha", n_ha, k + 1) for k, sent in enumerate(sends)]
        *grads, token = weight_grad(
            chunk * count, count, tile, hidden_width, row, xt, y_all, mine, other, grads
        )
        after = (grad, token)
    return (total(own, received), *grads)


def plain_body(tokens, cotangent, gate_weight, up_weight, down_weight):
    hidden_width = gate_weight.shape[1]
    x = lax.all_gather(tokens, "ha", axis=0, tiled=True)
    y = lax.all_gather(cotangent, "ha", axis=0, tiled=True)
    gate_part = jnp.dot(x, gate_weight, preferred_element_type=F32)
    up_part = jnp.dot(x, up_weight, preferred_element_type=F32)
    dh_part = lax.dot_general(y, down_weight, NT, preferred_element_type=F32)
    summed = lax.psum(jnp.concatenate([gate_part, up_part, dh_part], axis=1), "wa")
    hidden, d_gate, d_up = pointwise(
        summed[:, :hidden_width],
        summed[:, hidden_width : 2 * hidden_width],
        summed[:, 2 * hidden_width :],
    )
    partial = lax.dot_general(
        d_gate, gate_weight, NT, preferred_element_type=F32
    ) + lax.dot_general(d_up, up_weight, NT, preferred_element_type=F32)
    grad_tokens = lax.psum_scatter(partial, "ha", scatter_dimension=0, tiled=True)
    grads = (
        lax.dot_general(x, d_gate, TN, preferred_element_type=F32),
        lax.dot_general(x, d_up, TN, preferred_element_type=F32),
        lax.dot_general(hidden, y, TN, preferred_element_type=F32),
    )
    return (
        grad_tokens.astype(BF16),
        *(lax.psum(g.astype(BF16), "row").astype(BF16) for g in grads),
    )


def solution(mesh):
    n_wa, n_ha, n_row = (mesh.shape[name] for name in ("wa", "ha", "row"))

    def body(tokens, cotangent, gate_weight, up_weight, down_weight):
        width, hidden_width = gate_weight.shape
        fits = (
            n_wa == n_ha == 4
            and n_row == 2
            and width % LANES == 0
            and hidden_width % (LANES * CHUNKS) == 0
            and (tokens.shape[0] * n_ha) % 16 == 0
        )
        if fits:
            return fast_body(
                n_wa, n_ha, n_row, tokens, cotangent, gate_weight, up_weight, down_weight
            )
        return plain_body(tokens, cotangent, gate_weight, up_weight, down_weight)

    return jax.shard_map(
        body,
        mesh=mesh,
        in_specs=(
            P(("row", "ha"), "wa"),
            P(("row", "ha"), "wa"),
            P("wa", "ha"),
            P("wa", "ha"),
            P("ha", "wa"),
        ),
        out_specs=(P(("row", "ha"), "wa"), P("wa", "ha"), P("wa", "ha"), P("ha", "wa")),
        check_vma=False,
    )
```

```python
import functools

import jax
import jax.numpy as jnp
from jax import lax
from jax.experimental import pallas as pl
from jax.experimental.pallas import tpu as pltpu
from jax.sharding import PartitionSpec as P

BF16 = jnp.bfloat16
F32 = jnp.float32
NT = (((1,), (1,)), ((), ()))
TN = (((0,), (0,)), ((), ()))
LANES = 128
CHUNKS = 4
TILE = 256
MIB = 1024 * 1024


def pointwise(gate_sum, up_sum, dh_sum):
    sig = jax.nn.sigmoid(gate_sum)
    active = gate_sum * sig
    hidden = (active * up_sum).astype(BF16)
    d_up = (dh_sum * active).astype(BF16)
    d_gate = (dh_sum * up_sum * sig * (1.0 + gate_sum * (1.0 - sig))).astype(BF16)
    return (hidden, d_gate, d_up)


def call(
    kernel, grid, in_specs, out_specs, out_shape, flops, moved, scratch=(), aliases=None, limit=4
):
    return pl.pallas_call(
        kernel,
        grid=grid,
        in_specs=in_specs,
        out_specs=out_specs,
        out_shape=out_shape,
        scratch_shapes=list(scratch),
        input_output_aliases=aliases or {},
        cost_estimate=pl.CostEstimate(flops=flops, bytes_accessed=moved, transcendentals=0),
        compiler_params=pltpu.CompilerParams(vmem_limit_bytes=limit * MIB),
    )


def whole(shape):
    return pl.BlockSpec(shape, lambda i: (0,) * len(shape))


IN_VMEM = pl.BlockSpec(memory_space=pltpu.VMEM)
TOKEN = jax.ShapeDtypeStruct((8, LANES), F32)


def order_kernel(parts, rows, *refs):
    pieces = [ref[...].astype(F32) for ref in refs[:parts]]
    x_ref, y_ref = refs[parts:]
    wa = lax.axis_index("wa")
    xs, ys = [], []
    for slot in range(parts):
        at = wa ^ slot
        piece = pieces[0]
        for other in range(1, parts):
            piece = jnp.where(at == other, pieces[other], piece)
        xs.append(piece[:rows])
        ys.append(piece[rows:])
    x_ref[...] = jnp.concatenate(xs, axis=0).astype(BF16)
    y_ref[...] = jnp.concatenate(ys, axis=0).astype(BF16)


def order_rows(pieces):
    parts = len(pieces)
    rows, width = pieces[0].shape[0] // 2, pieces[0].shape[1]
    shape = (parts * rows, width)
    return call(
        functools.partial(order_kernel, parts, rows),
        (),
        [IN_VMEM] * parts,
        [IN_VMEM] * 2,
        [jax.ShapeDtypeStruct(shape, BF16)] * 2,
        0,
        8 * shape[0] * width,
    )(*pieces)


def forward_kernel(rows, begin, near, far, after, x_ref, y_ref, gate_ref, up_ref, down_ref, *refs):
    keep_ref, send_ref = refs[after:]
    there = pl.ds(begin, keep_ref.shape[1])
    gate = jnp.dot(x_ref[...], gate_ref[:, there], preferred_element_type=F32)
    up = jnp.dot(x_ref[...], up_ref[:, there], preferred_element_type=F32)
    dh = lax.dot_general(y_ref[...], down_ref[there, :], NT, preferred_element_type=F32)

    def slots(*which):
        cuts = [slice(slot * rows, (slot + 1) * rows) for slot in which]
        return jnp.concatenate([part[cut] for cut in cuts for part in (gate, up, dh)], axis=0)

    keep_ref[...] = slots(0, far)
    send_ref[...] = slots(near, near ^ far).astype(BF16)


def load_kernel(cuts, *refs):
    count = (len(refs) - 1) // 2
    sems = refs[-1]
    copies = []
    for at in range(count):
        rows = refs[at].shape[0] // cuts
        for cut in range(cuts):
            part = pl.ds(cut * rows, rows)
            copies.append(
                pltpu.make_async_copy(
                    refs[at].at[part], refs[count + at].at[part], sems.at[at, cut]
                )
            )
    for copy in copies:
        copy.start()
    for copy in copies:
        copy.wait()


def load(*weights):
    cuts = 4
    return pl.pallas_call(
        functools.partial(load_kernel, cuts),
        in_specs=[pl.BlockSpec(memory_space=pl.ANY)] * len(weights),
        out_specs=[IN_VMEM] * len(weights),
        out_shape=[pltpu.VMEM(w.shape, w.dtype) for w in weights],
        scratch_shapes=[pltpu.SemaphoreType.DMA((len(weights), cuts))],
        cost_estimate=pl.CostEstimate(
            flops=0, bytes_accessed=sum(2 * w.size for w in weights), transcendentals=0
        ),
        compiler_params=pltpu.CompilerParams(vmem_limit_bytes=34 * MIB),
    )(*weights)


def forward(begin, columns, near, far, x, y, gate_weight, up_weight, down_weight, after):
    group, width = x.shape
    rows = group // 4
    return call(
        functools.partial(forward_kernel, rows, begin, near, far, len(after)),
        (),
        [IN_VMEM] * (5 + len(after)),
        [IN_VMEM] * 2,
        [
            jax.ShapeDtypeStruct((6 * rows, columns), F32),
            jax.ShapeDtypeStruct((6 * rows, columns), BF16),
        ],
        6 * group * width * columns,
        6 * width * columns,
    )(x, y, gate_weight, up_weight, down_weight, *after)


def halve_kernel(keep_ref, received_ref, _, own_ref, send_ref):
    total = keep_ref[...] + received_ref[...].astype(F32)
    half = own_ref.shape[0]
    own_ref[...] = total[:half]
    send_ref[...] = total[half:].astype(BF16)


def halve(keep, received, after):
    shape = (keep.shape[0] // 2, keep.shape[1])
    return call(
        halve_kernel,
        (),
        [IN_VMEM] * 3,
        [IN_VMEM] * 2,
        [jax.ShapeDtypeStruct(shape, F32), jax.ShapeDtypeStruct(shape, BF16)],
        2 * keep.size,
        9 * keep.size,
    )(keep, received, after)


def middle_kernel(rows, own_ref, *refs):
    total = own_ref[...]
    for ref in refs[:-1]:
        total = total + ref[...].astype(F32)
    hidden, d_gate, d_up = pointwise(total[:rows], total[rows : 2 * rows], total[2 * rows :])
    refs[-1][...] = jnp.concatenate(
        [d_gate.astype(F32), d_up.astype(F32), hidden.astype(F32)], axis=0
    ).astype(BF16)


def middle(own, received):
    shape = own.shape
    return call(
        functools.partial(middle_kernel, shape[0] // 3),
        (),
        [IN_VMEM] * (1 + len(received)),
        IN_VMEM,
        jax.ShapeDtypeStruct(shape, BF16),
        20 * shape[0] * shape[1],
        12 * shape[0] * shape[1],
    )(own, *received)


def stack_kernel(rows, near, far, mine_ref, other_ref, out_ref):
    mine, other = mine_ref[...].astype(F32), other_ref[...].astype(F32)
    slots = {0: mine[: 3 * rows], near: mine[3 * rows :]}
    slots |= {far: other[: 3 * rows], near ^ far: other[3 * rows :]}
    cuts = [slots[slot][at * rows : (at + 1) * rows] for at in range(3) for slot in range(4)]
    out_ref[...] = jnp.concatenate(cuts, axis=0).astype(BF16)


def stack(near, far, mine, other):
    rows, columns = mine.shape[0] // 6, mine.shape[1]
    shape = (12 * rows, columns)
    return call(
        functools.partial(stack_kernel, rows, near, far),
        (),
        [IN_VMEM] * 2,
        IN_VMEM,
        jax.ShapeDtypeStruct(shape, BF16),
        0,
        4 * shape[0] * columns,
    )(mine, other)


def input_grad_kernel(group, begin, has_start, stack_ref, gate_ref, up_ref, *refs):
    there = pl.ds(begin, stack_ref.shape[1])
    grad = lax.dot_general(
        stack_ref[:group], gate_ref[:, there], NT, preferred_element_type=F32
    ) + lax.dot_general(
        stack_ref[group : 2 * group], up_ref[:, there], NT, preferred_element_type=F32
    )
    refs[-1][...] = grad + refs[0][...] if has_start else grad


def input_grad(begin, stacked, gate_weight, up_weight, after):
    group, columns = stacked.shape[0] // 3, stacked.shape[1]
    width = gate_weight.shape[0]
    return call(
        functools.partial(input_grad_kernel, group, begin, bool(after)),
        (),
        [IN_VMEM] * (3 + len(after)),
        IN_VMEM,
        jax.ShapeDtypeStruct((group, width), F32),
        4 * group * width * columns,
        4 * width * columns,
    )(stacked, gate_weight, up_weight, *after)


def factors_kernel(group, x_ref, y_ref, other_ref, xt_ref, y_all_ref):
    first = lax.axis_index("row") == 0
    x, y = x_ref[...], y_ref[...]
    x_other, y_other = other_ref[:group], other_ref[group:]
    y_all_ref[:group] = jnp.where(first, y, y_other)
    y_all_ref[group:] = jnp.where(first, y_other, y)
    x_all = jnp.concatenate([jnp.where(first, x, x_other), jnp.where(first, x_other, x)], axis=0)
    xt_ref[...] = x_all.T


def factors(x, y, other):
    group, width = x.shape
    return call(
        functools.partial(factors_kernel, group),
        (),
        [IN_VMEM] * 3,
        [IN_VMEM] * 2,
        [
            jax.ShapeDtypeStruct((width, 2 * group), BF16),
            jax.ShapeDtypeStruct((2 * group, width), BF16),
        ],
        0,
        8 * group * width,
    )(x, y, other)


def join_kernel(first_ref, second_ref, out_ref):
    out_ref[...] = jnp.concatenate(
        [first_ref[...].astype(F32), second_ref[...].astype(F32)], axis=0
    ).astype(BF16)


def join(first, second, from_hbm=False):
    shape = (first.shape[0] + second.shape[0], first.shape[1])
    return call(
        join_kernel,
        (1,) if from_hbm else (),
        [whole(first.shape), whole(second.shape)] if from_hbm else [IN_VMEM] * 2,
        whole(shape) if from_hbm else IN_VMEM,
        jax.ShapeDtypeStruct(shape, BF16),
        0,
        4 * shape[0] * shape[1],
    )(first, second)


def total_kernel(own_ref, *refs):
    total = own_ref[...]
    for ref in refs[:-1]:
        total = total + ref[...].astype(F32)
    refs[-1][...] = total.astype(BF16)


def total(own, received):
    return call(
        total_kernel,
        (),
        [IN_VMEM] * (1 + len(received)),
        IN_VMEM,
        jax.ShapeDtypeStruct(own.shape, BF16),
        4 * own.size,
        12 * own.size,
    )(own, *received)


def weight_grad_kernel(group, begin, skip, xt_ref, y_ref, mine_ref, other_ref, *refs):
    *outs, token_ref, both, gate, up, down, sems = refs[skip:]
    columns = mine_ref.shape[1]
    first = lax.axis_index("row") == 0
    for at in range(3):
        cut = slice(at * group, (at + 1) * group)
        both[at, :group] = jnp.where(first, mine_ref[cut], other_ref[cut])
        both[at, group:] = jnp.where(first, other_ref[cut], mine_ref[cut])
    copies = []

    def send(at, source, target):
        copies.append(pltpu.make_async_copy(source, target, sems.at[at, len(copies) // 3]))
        copies[-1].start()

    for start in range(0, columns, TILE):
        size = min(TILE, columns - start)
        here, there = pl.ds(start, size), pl.ds(begin + start, size)
        gate[:, here] = jnp.dot(
            xt_ref[...], both[0, :, here], preferred_element_type=F32
        ).astype(BF16)
        send(0, gate.at[:, here], outs[0].at[:, there])
        up[:, here] = jnp.dot(
            xt_ref[...], both[1, :, here], preferred_element_type=F32
        ).astype(BF16)
        send(1, up.at[:, here], outs[1].at[:, there])
        down[here, :] = lax.dot_general(
            both[2, :, here], y_ref[...], TN, preferred_element_type=F32
        ).astype(BF16)
        send(2, down.at[here], outs[2].at[there])
    token_ref[...] = jnp.zeros_like(token_ref)
    for copy in copies:
        copy.wait()


def weight_grad(begin, hidden_width, xt, y, mine, other, grads, after):
    width = xt.shape[0]
    group, columns = mine.shape[0] // 3, mine.shape[1]
    in_hbm = pl.BlockSpec(memory_space=pl.ANY)
    return call(
        functools.partial(weight_grad_kernel, group, begin, len(grads) + len(after)),
        (),
        [IN_VMEM] * 4 + [in_hbm] * len(grads) + [IN_VMEM] * len(after),
        [in_hbm] * 3 + [IN_VMEM],
        [
            jax.ShapeDtypeStruct((width, hidden_width), BF16),
            jax.ShapeDtypeStruct((width, hidden_width), BF16),
            jax.ShapeDtypeStruct((hidden_width, width), BF16),
            TOKEN,
        ],
        12 * group * width * columns,
        6 * width * columns,
        scratch=[
            pltpu.VMEM((3, 2 * group, columns), BF16),
            pltpu.VMEM((width, columns), BF16),
            pltpu.VMEM((width, columns), BF16),
            pltpu.VMEM((columns, width), BF16),
            pltpu.SemaphoreType.DMA((3, pl.cdiv(columns, TILE))),
        ],
        aliases={4 + i: i for i in range(len(grads))},
        limit=16,
    )(xt, y, mine, other, *grads, *after)


def last_kernel(parts, rows, grad_ref, own_ref, *send_refs):
    grad = grad_ref[...]
    cuts = [grad[slot * rows : (slot + 1) * rows] for slot in range(parts)]
    wa = lax.axis_index("wa")
    for step in range(parts):
        at = wa ^ step
        piece = cuts[0]
        for slot in range(1, parts):
            piece = jnp.where(at == slot, cuts[slot], piece)
        if step == 0:
            own_ref[...] = piece
        else:
            send_refs[step - 1][...] = piece.astype(BF16)


def last_pieces(parts, grad):
    rows, width = grad.shape[0] // parts, grad.shape[1]
    return call(
        functools.partial(last_kernel, parts, rows),
        (),
        [IN_VMEM],
        [IN_VMEM] * parts,
        [jax.ShapeDtypeStruct((rows, width), F32)]
        + [jax.ShapeDtypeStruct((rows, width), BF16)] * (parts - 1),
        0,
        8 * grad.shape[0] * width,
    )(grad)


def swap(value, axis, size, step):
    return lax.ppermute(value, axis, [(at, at ^ step) for at in range(size)])


def fast_body(n_wa, n_ha, n_row, tokens, cotangent, gate_weight, up_weight, down_weight):
    hidden_width = gate_weight.shape[1]
    tiles = hidden_width // LANES
    ends = [-(-tiles * (at + 1) // CHUNKS) * LANES for at in range(CHUNKS)]
    chunks = [(begin, end - begin) for begin, end in zip([0] + ends, ends)]
    axes = [((1, 2), (2, 1))[at % 2] for at in range(CHUNKS)]

    both = join(tokens, cotangent, from_hbm=True)
    gate_weight, up_weight, down_weight = load(gate_weight, up_weight, down_weight)
    pieces = [both] + [swap(both, "ha", n_ha, step) for step in range(1, n_ha)]
    x, y = order_rows(pieces)

    sums, after = [], ()
    for (begin, columns), (near, far) in zip(chunks, axes):
        keep, send = forward(
            begin, columns, near, far, x, y, gate_weight, up_weight, down_weight, after
        )
        sums.append((keep, swap(send, "wa", n_wa, near)))
        after = (send,)
    sums = [halve(keep, received, send) for keep, received in sums]
    sums = [(own, swap(send, "wa", n_wa, far)) for (own, send), (_, far) in zip(sums, axes)]
    xt, y_all = factors(x, y, swap(join(x, y), "row", n_row, 1))
    mine = [middle(own, [received]) for own, received in sums]
    mine = [join(m, swap(m, "wa", n_wa, near)) for m, (near, _) in zip(mine, axes)]
    mine = [(m, swap(m, "wa", n_wa, far)) for m, (_, far) in zip(mine, axes)]
    mine = [stack(*axis, *m) for axis, m in zip(axes, mine)]
    other = [swap(m, "row", n_row, 1) for m in mine]

    grad, grads, token = (), (), ()
    for at, (begin, columns) in enumerate(chunks):
        grad = (input_grad(begin, mine[at], gate_weight, up_weight, grad + token),)
        if at < CHUNKS - 2:
            *grads, token = weight_grad(
                begin, hidden_width, xt, y_all, mine[at], other[at], grads, ()
            )
            token = (token,)
        else:
            token = ()
    own, *sends = last_pieces(n_ha, grad[0])
    received = [swap(sent, "ha", n_ha, k + 1) for k, sent in enumerate(sends)]
    for at in range(CHUNKS - 2, CHUNKS):
        *grads, _ = weight_grad(
            chunks[at][0], hidden_width, xt, y_all, mine[at], other[at], grads, (own,)
        )
    return (total(own, received), *grads)


def plain_body(tokens, cotangent, gate_weight, up_weight, down_weight):
    hidden_width = gate_weight.shape[1]
    x = lax.all_gather(tokens, "ha", axis=0, tiled=True)
    y = lax.all_gather(cotangent, "ha", axis=0, tiled=True)
    gate_part = jnp.dot(x, gate_weight, preferred_element_type=F32)
    up_part = jnp.dot(x, up_weight, preferred_element_type=F32)
    dh_part = lax.dot_general(y, down_weight, NT, preferred_element_type=F32)
    summed = lax.psum(jnp.concatenate([gate_part, up_part, dh_part], axis=1), "wa")
    hidden, d_gate, d_up = pointwise(
        summed[:, :hidden_width],
        summed[:, hidden_width : 2 * hidden_width],
        summed[:, 2 * hidden_width :],
    )
    partial = lax.dot_general(
        d_gate, gate_weight, NT, preferred_element_type=F32
    ) + lax.dot_general(d_up, up_weight, NT, preferred_element_type=F32)
    grad_tokens = lax.psum_scatter(partial, "ha", scatter_dimension=0, tiled=True)
    grads = (
        lax.dot_general(x, d_gate, TN, preferred_element_type=F32),
        lax.dot_general(x, d_up, TN, preferred_element_type=F32),
        lax.dot_general(hidden, y, TN, preferred_element_type=F32),
    )
    return (
        grad_tokens.astype(BF16),
        *(lax.psum(g.astype(BF16), "row").astype(BF16) for g in grads),
    )


def solution(mesh):
    n_wa, n_ha, n_row = (mesh.shape[name] for name in ("wa", "ha", "row"))

    def body(tokens, cotangent, gate_weight, up_weight, down_weight):
        width, hidden_width = gate_weight.shape
        fits = (
            n_wa == n_ha == 4
            and n_row == 2
            and width % LANES == 0
            and hidden_width % LANES == 0
            and hidden_width >= LANES * CHUNKS
            and (tokens.shape[0] * n_ha) % 16 == 0
        )
        if fits:
            return fast_body(
                n_wa, n_ha, n_row, tokens, cotangent, gate_weight, up_weight, down_weight
            )
        return plain_body(tokens, cotangent, gate_weight, up_weight, down_weight)

    return jax.shard_map(
        body,
        mesh=mesh,
        in_specs=(
            P(("row", "ha"), "wa"),
            P(("row", "ha"), "wa"),
            P("wa", "ha"),
            P("wa", "ha"),
            P("ha", "wa"),
        ),
        out_specs=(P(("row", "ha"), "wa"), P("wa", "ha"), P("wa", "ha"), P("ha", "wa")),
        check_vma=False,
    )
```

```python
import functools

import jax
import jax.numpy as jnp
from jax import lax
from jax.experimental import pallas as pl
from jax.experimental.pallas import tpu as pltpu
from jax.sharding import PartitionSpec as P

BF16 = jnp.bfloat16
F32 = jnp.float32
NT = (((1,), (1,)), ((), ()))
TN = (((0,), (0,)), ((), ()))
LANES = 128
CHUNKS = 4
TILE = 256
CUTS = 4
MIB = 1024 * 1024
IN_VMEM = pl.BlockSpec(memory_space=pltpu.VMEM)
IN_HBM = pl.BlockSpec(memory_space=pl.ANY)


def shaped(rows, columns, dtype=BF16):
    return jax.ShapeDtypeStruct((rows, columns), dtype)


def joined(*blocks):
    return jnp.concatenate([block.astype(F32) for block in blocks], axis=0)


def pointwise(gate_sum, up_sum, dh_sum):
    sig = jax.nn.sigmoid(gate_sum)
    active = gate_sum * sig
    hidden = (active * up_sum).astype(BF16)
    d_up = (dh_sum * active).astype(BF16)
    d_gate = (dh_sum * up_sum * sig * (1.0 + gate_sum * (1.0 - sig))).astype(BF16)
    return (hidden, d_gate, d_up)


class Line:
    def __init__(self):
        self.token = ()

    def call(self, kernel, args, out_shape, in_specs=None, out_specs=None, scratch=(), limit=4):
        count, outs, tokens = len(args), len(out_shape), len(self.token)

        def body(*refs):
            rest = refs[count + tokens :]
            rest[outs][...] = jnp.zeros_like(rest[outs])
            kernel(*refs[:count], *rest[:outs], *rest[outs + 1 :])

        *results, token = pl.pallas_call(
            body,
            in_specs=(in_specs or [IN_VMEM] * count) + [IN_VMEM] * tokens,
            out_specs=(out_specs or [IN_VMEM] * outs) + [IN_VMEM],
            out_shape=[*out_shape, shaped(8, LANES, F32)],
            scratch_shapes=list(scratch),
            cost_estimate=pl.CostEstimate(flops=1, bytes_accessed=1, transcendentals=0),
            compiler_params=pltpu.CompilerParams(vmem_limit_bytes=limit * MIB),
        )(*args, *self.token)
        self.token = (token,)
        return results


def load_kernel(*refs):
    count = len(refs) // 2
    sems = refs[-1]
    copies = []
    for cut in range(CUTS):
        for at, (source, target) in enumerate(zip(refs[:count], refs[count:-1])):
            rows = source.shape[0] // CUTS
            part = pl.ds(cut * rows, rows)
            copies.append(
                pltpu.make_async_copy(source.at[part], target.at[part], sems.at[at, cut])
            )
    for copy in copies:
        copy.start()
    for copy in copies:
        copy.wait()


def load(line, *weights):
    return line.call(
        load_kernel,
        weights,
        [pltpu.VMEM(weight.shape, BF16) for weight in weights],
        in_specs=[IN_HBM] * len(weights),
        scratch=[pltpu.SemaphoreType.DMA((len(weights), CUTS))],
        limit=34,
    )


def order_kernel(*refs):
    *piece_refs, out_ref = refs
    pieces = [ref[...].astype(F32) for ref in piece_refs]
    rows = pieces[0].shape[0] // 2
    wa = lax.axis_index("wa")
    slots = []
    for slot in range(len(pieces)):
        at = wa ^ slot
        piece = pieces[0]
        for other in range(1, len(pieces)):
            piece = jnp.where(at == other, pieces[other], piece)
        slots.append(piece)
    out_ref[...] = joined(
        *(slot[:rows] for slot in slots), *(slot[rows:] for slot in slots)
    ).astype(BF16)


def order_rows(line, pieces):
    rows, width = pieces[0].shape
    return line.call(order_kernel, pieces, [shaped(4 * rows, width)])[0]


def forward_kernel(begin, near, far, xy_ref, gate_ref, up_ref, down_ref, *refs):
    keep_ref, send_ref = refs
    group = xy_ref.shape[0] // 2
    rows = group // 4
    x, y = xy_ref[:group], xy_ref[group:]
    there = pl.ds(begin, keep_ref.shape[1])
    gate = jnp.dot(x, gate_ref[:, there], preferred_element_type=F32)
    up = jnp.dot(x, up_ref[:, there], preferred_element_type=F32)
    dh = lax.dot_general(y, down_ref[there], NT, preferred_element_type=F32)

    def slots(*which):
        cuts = [slice(slot * rows, (slot + 1) * rows) for slot in which]
        return joined(*(part[cut] for cut in cuts for part in (gate, up, dh)))

    keep_ref[...] = slots(0, far)
    send_ref[...] = slots(near, near ^ far).astype(BF16)


def forward(line, begin, columns, axes, xy, gate_weight, up_weight, down_weight):
    rows = 6 * (xy.shape[0] // 8)
    return line.call(
        functools.partial(forward_kernel, begin, *axes),
        (xy, gate_weight, up_weight, down_weight),
        [shaped(rows, columns, F32), shaped(rows, columns)],
    )


def halve_kernel(keep_ref, received_ref, own_ref, send_ref):
    total = keep_ref[...] + received_ref[...].astype(F32)
    half = own_ref.shape[0]
    own_ref[...] = total[:half]
    send_ref[...] = total[half:].astype(BF16)


def halve(line, keep, received):
    shape = (keep.shape[0] // 2, keep.shape[1])
    return line.call(halve_kernel, (keep, received), [shaped(*shape, F32), shaped(*shape)])


def middle_kernel(own_ref, received_ref, out_ref):
    total = own_ref[...] + received_ref[...].astype(F32)
    rows = total.shape[0] // 3
    hidden, d_gate, d_up = pointwise(total[:rows], total[rows : 2 * rows], total[2 * rows :])
    out_ref[...] = joined(d_gate, d_up, hidden).astype(BF16)


def middle(line, own, received):
    return line.call(middle_kernel, (own, received), [shaped(*own.shape)])[0]


def join_kernel(first_ref, second_ref, out_ref):
    out_ref[...] = joined(first_ref[...], second_ref[...]).astype(BF16)


def join(line, first, second):
    rows = first.shape[0] + second.shape[0]
    return line.call(join_kernel, (first, second), [shaped(rows, first.shape[1])])[0]


def stack_kernel(axes, *refs):
    out_ref = refs[-1]
    begin = 0
    for at, (near, far) in enumerate(axes):
        mine, other = refs[2 * at][...].astype(F32), refs[2 * at + 1][...].astype(F32)
        columns = mine.shape[1]
        half, rows = mine.shape[0] // 2, mine.shape[0] // 6
        slots = {0: mine[:half], near: mine[half:]}
        slots |= {far: other[:half], near ^ far: other[half:]}
        cuts = [slots[slot][k * rows : (k + 1) * rows] for k in range(3) for slot in range(4)]
        out_ref[:, begin : begin + columns] = joined(*cuts).astype(BF16)
        begin += columns


def stack(line, axes, blocks):
    rows = 2 * blocks[0][0].shape[0]
    columns = sum(mine.shape[1] for mine, _ in blocks)
    return line.call(
        functools.partial(stack_kernel, axes),
        [block for pair in blocks for block in pair],
        [shaped(rows, columns)],
    )[0]


def input_grad_kernel(begin, stack_ref, gate_ref, up_ref, *refs):
    there = pl.ds(begin, stack_ref.shape[1])
    group = stack_ref.shape[0] // 3
    grad = lax.dot_general(
        stack_ref[:group], gate_ref[:, there], NT, preferred_element_type=F32
    ) + lax.dot_general(
        stack_ref[group : 2 * group], up_ref[:, there], NT, preferred_element_type=F32
    )
    refs[-1][...] = grad + refs[0][...] if len(refs) > 1 else grad


def input_grad(line, begin, stacked, gate_weight, up_weight, start):
    shape = (stacked.shape[0] // 3, gate_weight.shape[0])
    return line.call(
        functools.partial(input_grad_kernel, begin),
        (stacked, gate_weight, up_weight, *start),
        [shaped(*shape, F32)],
    )


def factors_kernel(mine_ref, other_ref, xt_ref, y_all_ref):
    group = mine_ref.shape[0] // 2
    first = lax.axis_index("row") == 0
    x, y = mine_ref[:group], mine_ref[group:]
    x_other, y_other = other_ref[:group], other_ref[group:]
    y_all_ref[:group] = jnp.where(first, y, y_other)
    y_all_ref[group:] = jnp.where(first, y_other, y)
    x_all = jnp.concatenate([jnp.where(first, x, x_other), jnp.where(first, x_other, x)], axis=0)
    xt_ref[...] = x_all.T


def factors(line, xy, other):
    rows, width = xy.shape
    return line.call(factors_kernel, (xy, other), [shaped(width, rows), shaped(rows, width)])


def weight_grad_kernel(parts, xt_ref, y_ref, *refs):
    mine_refs, other_refs = refs[:parts], refs[parts : 2 * parts]
    *outs, both, gate, up, down, sems = refs[2 * parts :]
    group = y_ref.shape[0] // 2
    first = lax.axis_index("row") == 0
    copies = []

    def send(at, source, target):
        copies.append(pltpu.make_async_copy(source, target, sems.at[at, len(copies) // 3]))
        copies[-1].start()

    begin = 0
    for mine_ref, other_ref in zip(mine_refs, other_refs):
        columns = mine_ref.shape[1]
        for start in range(0, columns, TILE):
            size = min(TILE, columns - start)
            source, here = pl.ds(start, size), pl.ds(begin + start, size)
            for at in range(3):
                cut = slice(at * group, (at + 1) * group)
                mine, other = mine_ref[cut, source], other_ref[cut, source]
                both[at, :group, here] = jnp.where(first, mine, other)
                both[at, group:, here] = jnp.where(first, other, mine)
            gate[:, here] = jnp.dot(
                xt_ref[...], both[0, :, here], preferred_element_type=F32
            ).astype(BF16)
            send(0, gate.at[:, here], outs[0].at[:, here])
            up[:, here] = jnp.dot(
                xt_ref[...], both[1, :, here], preferred_element_type=F32
            ).astype(BF16)
            send(1, up.at[:, here], outs[1].at[:, here])
            down[here, :] = lax.dot_general(
                both[2, :, here], y_ref[...], TN, preferred_element_type=F32
            ).astype(BF16)
            send(2, down.at[here], outs[2].at[here])
        begin += columns
    for copy in copies:
        copy.wait()


def weight_grad(line, xt, y, mine, other):
    width = xt.shape[0]
    hidden_width = sum(m.shape[1] for m in mine)
    shapes = [(width, hidden_width), (width, hidden_width), (hidden_width, width)]
    steps = sum(pl.cdiv(m.shape[1], TILE) for m in mine)
    return line.call(
        functools.partial(weight_grad_kernel, len(mine)),
        (xt, y, *mine, *other),
        [shaped(*shape) for shape in shapes],
        out_specs=[IN_HBM] * 3,
        scratch=[
            pltpu.VMEM((3, y.shape[0], hidden_width), BF16),
            *(pltpu.VMEM(shape, BF16) for shape in shapes),
            pltpu.SemaphoreType.DMA((3, steps)),
        ],
        limit=40,
    )


def last_kernel(grad_ref, *out_refs):
    grad = grad_ref[...]
    rows = out_refs[0].shape[0]
    cuts = [grad[slot * rows : (slot + 1) * rows] for slot in range(len(out_refs))]
    wa = lax.axis_index("wa")
    for step, out_ref in enumerate(out_refs):
        at = wa ^ step
        piece = cuts[0]
        for slot in range(1, len(cuts)):
            piece = jnp.where(at == slot, cuts[slot], piece)
        out_ref[...] = piece.astype(out_ref.dtype)


def last_pieces(line, parts, grad):
    shape = (grad.shape[0] // parts, grad.shape[1])
    return line.call(
        last_kernel, (grad,), [shaped(*shape, F32)] + [shaped(*shape)] * (parts - 1)
    )


def total_kernel(own_ref, *refs):
    total = own_ref[...]
    for ref in refs[:-1]:
        total = total + ref[...].astype(F32)
    refs[-1][...] = total.astype(BF16)


def total(line, own, received):
    return line.call(total_kernel, (own, *received), [shaped(*own.shape)])[0]


def swap(value, axis, size, step):
    return lax.ppermute(value, axis, [(at, at ^ step) for at in range(size)])


def fast_body(n_wa, n_ha, n_row, tokens, cotangent, gate_weight, up_weight, down_weight):
    hidden_width = gate_weight.shape[1]
    tiles = hidden_width // LANES
    ends = [-(-tiles * (at + 1) // CHUNKS) * LANES for at in range(CHUNKS)]
    chunks = [(begin, end - begin) for begin, end in zip([0] + ends, ends)]
    axes = [((1, 2), (2, 1))[at % 2] for at in range(CHUNKS)]
    line = Line()

    both = jnp.concatenate([tokens, cotangent], axis=0)
    pieces = [both] + [swap(both, "ha", n_ha, step) for step in range(1, n_ha)]
    gate_weight, up_weight, down_weight = load(Line(), gate_weight, up_weight, down_weight)
    xy = order_rows(line, pieces)
    xy_other = swap(xy, "row", n_row, 1)

    kept, got = [], []
    for (begin, columns), axis in zip(chunks, axes):
        keep, send = forward(
            line, begin, columns, axis, xy, gate_weight, up_weight, down_weight
        )
        kept.append(keep)
        got.append(swap(send, "wa", n_wa, axis[0]))
    for at, (_, far) in enumerate(axes):
        kept[at], send = halve(line, kept[at], got[at])
        got[at] = swap(send, "wa", n_wa, far)
    order = [pair + 1 - at for pair in range(0, CHUNKS, 2) for at in range(2)]
    for at in order:
        kept[at] = middle(line, kept[at], got[at])
        got[at] = swap(kept[at], "wa", n_wa, axes[at][0])
    xt, y_all = factors(line, xy, xy_other)
    for at, (_, far) in enumerate(axes):
        kept[at] = join(line, kept[at], got[at])
        got[at] = swap(kept[at], "wa", n_wa, far)

    mine, other, grad = [], [], ()
    for at in range(0, CHUNKS, 2):
        pair = slice(at, at + 2)
        mine.append(stack(line, axes[pair], list(zip(kept, got))[pair]))
        other.append(swap(mine[-1], "row", n_row, 1))
        grad = input_grad(line, chunks[at][0], mine[-1], gate_weight, up_weight, grad)
    own, *sends = last_pieces(line, n_ha, grad[0])
    received = [swap(sent, "ha", n_ha, k + 1) for k, sent in enumerate(sends)]
    grads = weight_grad(line, xt, y_all, mine, other)
    return (total(line, own, received), *grads)


def plain_body(tokens, cotangent, gate_weight, up_weight, down_weight):
    hidden_width = gate_weight.shape[1]
    x = lax.all_gather(tokens, "ha", axis=0, tiled=True)
    y = lax.all_gather(cotangent, "ha", axis=0, tiled=True)
    gate_part = jnp.dot(x, gate_weight, preferred_element_type=F32)
    up_part = jnp.dot(x, up_weight, preferred_element_type=F32)
    dh_part = lax.dot_general(y, down_weight, NT, preferred_element_type=F32)
    summed = lax.psum(jnp.concatenate([gate_part, up_part, dh_part], axis=1), "wa")
    hidden, d_gate, d_up = pointwise(
        summed[:, :hidden_width],
        summed[:, hidden_width : 2 * hidden_width],
        summed[:, 2 * hidden_width :],
    )
    partial = lax.dot_general(
        d_gate, gate_weight, NT, preferred_element_type=F32
    ) + lax.dot_general(d_up, up_weight, NT, preferred_element_type=F32)
    grad_tokens = lax.psum_scatter(partial, "ha", scatter_dimension=0, tiled=True)
    grads = (
        lax.dot_general(x, d_gate, TN, preferred_element_type=F32),
        lax.dot_general(x, d_up, TN, preferred_element_type=F32),
        lax.dot_general(hidden, y, TN, preferred_element_type=F32),
    )
    return (
        grad_tokens.astype(BF16),
        *(lax.psum(g.astype(BF16), "row").astype(BF16) for g in grads),
    )


def solution(mesh):
    n_wa, n_ha, n_row = (mesh.shape[name] for name in ("wa", "ha", "row"))

    def body(tokens, cotangent, gate_weight, up_weight, down_weight):
        width, hidden_width = gate_weight.shape
        fits = (
            n_wa == n_ha == 4
            and n_row == 2
            and width % LANES == 0
            and hidden_width % LANES == 0
            and hidden_width >= LANES * CHUNKS
            and (tokens.shape[0] * n_ha) % 16 == 0
        )
        if fits:
            return fast_body(
                n_wa, n_ha, n_row, tokens, cotangent, gate_weight, up_weight, down_weight
            )
        return plain_body(tokens, cotangent, gate_weight, up_weight, down_weight)

    return jax.shard_map(
        body,
        mesh=mesh,
        in_specs=(
            P(("row", "ha"), "wa"),
            P(("row", "ha"), "wa"),
            P("wa", "ha"),
            P("wa", "ha"),
            P("ha", "wa"),
        ),
        out_specs=(P(("row", "ha"), "wa"), P("wa", "ha"), P("wa", "ha"), P("ha", "wa")),
        check_vma=False,
    )
```

```python
import functools

import jax
import jax.numpy as jnp
from jax import lax
from jax.experimental import pallas as pl
from jax.experimental.pallas import tpu as pltpu
from jax.sharding import PartitionSpec as P

BF16 = jnp.bfloat16
F32 = jnp.float32
NT = (((1,), (1,)), ((), ()))
TN = (((0,), (0,)), ((), ()))
LANES = 128
CHUNKS = 4
TILE = 256
CUTS = 4
MIB = 1024 * 1024
IN_VMEM = pl.BlockSpec(memory_space=pltpu.VMEM)
IN_HBM = pl.BlockSpec(memory_space=pl.ANY)


def shaped(rows, columns, dtype=BF16):
    return jax.ShapeDtypeStruct((rows, columns), dtype)


def joined(*blocks):
    return jnp.concatenate([block.astype(F32) for block in blocks], axis=0)


def pointwise(gate_sum, up_sum, dh_sum):
    sig = jax.nn.sigmoid(gate_sum)
    active = gate_sum * sig
    hidden = (active * up_sum).astype(BF16)
    d_up = (dh_sum * active).astype(BF16)
    d_gate = (dh_sum * up_sum * sig * (1.0 + gate_sum * (1.0 - sig))).astype(BF16)
    return (hidden, d_gate, d_up)


class Line:
    def __init__(self):
        self.token = ()

    def call(
        self,
        kernel,
        args,
        out_shape,
        in_specs=None,
        out_specs=None,
        scratch=(),
        aliases=None,
        limit=4,
    ):
        count, outs, tokens = len(args), len(out_shape), len(self.token)

        def body(*refs):
            rest = refs[count + tokens :]
            rest[outs][...] = jnp.zeros_like(rest[outs])
            kernel(*refs[:count], *rest[:outs], *rest[outs + 1 :])

        *results, token = pl.pallas_call(
            body,
            in_specs=(in_specs or [IN_VMEM] * count) + [IN_VMEM] * tokens,
            out_specs=(out_specs or [IN_VMEM] * outs) + [IN_VMEM],
            out_shape=[*out_shape, shaped(8, LANES, F32)],
            scratch_shapes=list(scratch),
            input_output_aliases=aliases or {},
            cost_estimate=pl.CostEstimate(flops=1, bytes_accessed=1, transcendentals=0),
            compiler_params=pltpu.CompilerParams(vmem_limit_bytes=limit * MIB),
            name=getattr(kernel, "func", kernel).__name__,
        )(*args, *self.token)
        self.token = (token,)
        return results


def copy_rows(sems, source, target, begin=0):
    rows = target.shape[0] // CUTS
    copies = []
    for cut in range(CUTS):
        there, here = pl.ds(begin + cut * rows, rows), pl.ds(cut * rows, rows)
        copies.append(pltpu.make_async_copy(source.at[there], target.at[here], sems.at[cut]))
        copies[-1].start()
    return copies


def load_kernel(gate_ref, up_ref, down_ref, gate_out, up_out, down_out, sems):
    copies = copy_rows(sems.at[0], gate_ref, gate_out)
    copies += copy_rows(sems.at[1], up_ref, up_out)
    copies += copy_rows(sems.at[2], down_ref, down_out)
    for copy in copies:
        copy.wait()


def load(line, gate_weight, up_weight, down_weight, rows):
    shapes = [gate_weight.shape, up_weight.shape, (rows, down_weight.shape[1])]
    return line.call(
        load_kernel,
        (gate_weight, up_weight, down_weight),
        [pltpu.VMEM(shape, BF16) for shape in shapes],
        in_specs=[IN_HBM] * 3,
        scratch=[pltpu.SemaphoreType.DMA((3, CUTS))],
        limit=30,
    )


def order_kernel(*refs):
    *piece_refs, out_ref = refs
    pieces = [ref[...].astype(F32) for ref in piece_refs]
    rows = pieces[0].shape[0] // 2
    wa = lax.axis_index("wa")
    slots = []
    for slot in range(len(pieces)):
        at = wa ^ slot
        piece = pieces[0]
        for other in range(1, len(pieces)):
            piece = jnp.where(at == other, pieces[other], piece)
        slots.append(piece)
    out_ref[...] = joined(
        *(slot[:rows] for slot in slots), *(slot[rows:] for slot in slots)
    ).astype(BF16)


def order_rows(line, pieces):
    rows, width = pieces[0].shape
    return line.call(order_kernel, pieces, [shaped(4 * rows, width)])[0]


def forward_kernel(begin, down_begin, near, far, later, *refs):
    xy_ref, gate_ref, up_ref, down_ref, *refs = refs
    copies = []
    if later is not None:
        all_ref, keep_ref, send_ref, later_ref, sems = refs
        copies = copy_rows(sems, all_ref, later_ref, later)
    else:
        keep_ref, send_ref = refs
    columns = keep_ref.shape[1]
    group = xy_ref.shape[0] // 2
    rows = group // 4
    x, y = xy_ref[:group], xy_ref[group:]
    there = pl.ds(begin, columns)
    gate = jnp.dot(x, gate_ref[:, there], preferred_element_type=F32)
    up = jnp.dot(x, up_ref[:, there], preferred_element_type=F32)
    dh = lax.dot_general(
        y, down_ref[pl.ds(down_begin, columns)], NT, preferred_element_type=F32
    )

    def slots(*which):
        cuts = [slice(slot * rows, (slot + 1) * rows) for slot in which]
        return joined(*(part[cut] for cut in cuts for part in (gate, up, dh)))

    keep_ref[...] = slots(0, far)
    send_ref[...] = slots(near, near ^ far).astype(BF16)
    for copy in copies:
        copy.wait()


def forward(line, begin, columns, axes, xy, gate, up, down, down_begin, rest=None):
    rows = 6 * (xy.shape[0] // 8)
    args, specs = [xy, gate, up, down], [IN_VMEM] * 4
    shapes = [shaped(rows, columns, F32), shaped(rows, columns)]
    later = None
    if rest is not None:
        weight, later = rest
        args.append(weight)
        specs.append(IN_HBM)
        shapes.append(pltpu.VMEM((weight.shape[0] - later, weight.shape[1]), BF16))
    return line.call(
        functools.partial(forward_kernel, begin, down_begin, *axes, later),
        args,
        shapes,
        in_specs=specs,
        scratch=[pltpu.SemaphoreType.DMA((CUTS,))] if rest is not None else [],
        limit=25 if rest is not None else 4,
    )


def halve_kernel(keep_ref, received_ref, own_ref, send_ref):
    total = keep_ref[...] + received_ref[...].astype(F32)
    half = own_ref.shape[0]
    own_ref[...] = total[:half]
    send_ref[...] = total[half:].astype(BF16)


def halve(line, keep, received):
    shape = (keep.shape[0] // 2, keep.shape[1])
    return line.call(halve_kernel, (keep, received), [shaped(*shape, F32), shaped(*shape)])


def middle_kernel(own_ref, received_ref, out_ref):
    total = own_ref[...] + received_ref[...].astype(F32)
    rows = total.shape[0] // 3
    hidden, d_gate, d_up = pointwise(total[:rows], total[rows : 2 * rows], total[2 * rows :])
    out_ref[...] = joined(d_gate, d_up, hidden).astype(BF16)


def middle(line, own, received):
    return line.call(middle_kernel, (own, received), [shaped(*own.shape)])[0]


def join_kernel(first_ref, second_ref, out_ref):
    out_ref[...] = joined(first_ref[...], second_ref[...]).astype(BF16)


def join(line, first, second):
    rows = first.shape[0] + second.shape[0]
    return line.call(join_kernel, (first, second), [shaped(rows, first.shape[1])])[0]


def stack_kernel(axes, *refs):
    out_ref = refs[-1]
    begin = 0
    for at, (near, far) in enumerate(axes):
        mine, other = refs[2 * at][...].astype(F32), refs[2 * at + 1][...].astype(F32)
        columns = mine.shape[1]
        half, rows = mine.shape[0] // 2, mine.shape[0] // 6
        slots = {0: mine[:half], near: mine[half:]}
        slots |= {far: other[:half], near ^ far: other[half:]}
        cuts = [slots[slot][k * rows : (k + 1) * rows] for k in range(3) for slot in range(4)]
        out_ref[:, begin : begin + columns] = joined(*cuts).astype(BF16)
        begin += columns


def stack(line, axes, blocks):
    rows = 2 * blocks[0][0].shape[0]
    columns = sum(mine.shape[1] for mine, _ in blocks)
    return line.call(
        functools.partial(stack_kernel, axes),
        [block for pair in blocks for block in pair],
        [shaped(rows, columns)],
    )[0]


def input_grad_kernel(begin, stack_ref, gate_ref, up_ref, *refs):
    there = pl.ds(begin, stack_ref.shape[1])
    group = stack_ref.shape[0] // 3
    grad = lax.dot_general(
        stack_ref[:group], gate_ref[:, there], NT, preferred_element_type=F32
    ) + lax.dot_general(
        stack_ref[group : 2 * group], up_ref[:, there], NT, preferred_element_type=F32
    )
    refs[-1][...] = grad + refs[0][...] if len(refs) > 1 else grad


def input_grad(line, begin, stacked, gate_weight, up_weight, start):
    shape = (stacked.shape[0] // 3, gate_weight.shape[0])
    return line.call(
        functools.partial(input_grad_kernel, begin),
        (stacked, gate_weight, up_weight, *start),
        [shaped(*shape, F32)],
    )


def factors_kernel(mine_ref, other_ref, xt_ref, y_all_ref):
    group = mine_ref.shape[0] // 2
    first = lax.axis_index("row") == 0
    x, y = mine_ref[:group], mine_ref[group:]
    x_other, y_other = other_ref[:group], other_ref[group:]
    y_all_ref[:group] = jnp.where(first, y, y_other)
    y_all_ref[group:] = jnp.where(first, y_other, y)
    x_all = jnp.concatenate([jnp.where(first, x, x_other), jnp.where(first, x_other, x)], axis=0)
    xt_ref[...] = x_all.T


def factors(line, xy, other):
    rows, width = xy.shape
    return line.call(factors_kernel, (xy, other), [shaped(width, rows), shaped(rows, width)])


def weight_grad_kernel(parts, xt_ref, y_ref, *refs):
    mine_refs, other_refs = refs[:parts], refs[parts : 2 * parts]
    *outs, both, gate, up, down, sems = refs[2 * parts :]
    group = y_ref.shape[0] // 2
    first = lax.axis_index("row") == 0
    copies = []

    def send(at, source, target):
        copies.append(pltpu.make_async_copy(source, target, sems.at[at, len(copies) // 3]))
        copies[-1].start()

    begin = 0
    for mine_ref, other_ref in zip(mine_refs, other_refs):
        columns = mine_ref.shape[1]
        for start in range(0, columns, TILE):
            size = min(TILE, columns - start)
            source, here = pl.ds(start, size), pl.ds(begin + start, size)
            for at in range(3):
                cut = slice(at * group, (at + 1) * group)
                mine, other = mine_ref[cut, source], other_ref[cut, source]
                both[at, :group, here] = jnp.where(first, mine, other)
                both[at, group:, here] = jnp.where(first, other, mine)
            gate[:, here] = jnp.dot(
                xt_ref[...], both[0, :, here], preferred_element_type=F32
            ).astype(BF16)
            send(0, gate.at[:, here], outs[0].at[:, here])
            up[:, here] = jnp.dot(
                xt_ref[...], both[1, :, here], preferred_element_type=F32
            ).astype(BF16)
            send(1, up.at[:, here], outs[1].at[:, here])
            down[here, :] = lax.dot_general(
                both[2, :, here], y_ref[...], TN, preferred_element_type=F32
            ).astype(BF16)
            send(2, down.at[here], outs[2].at[here])
        begin += columns
    for copy in copies:
        copy.wait()


def weight_grad(line, xt, y, mine, other):
    width = xt.shape[0]
    hidden_width = sum(m.shape[1] for m in mine)
    shapes = [(width, hidden_width), (width, hidden_width), (hidden_width, width)]
    steps = sum(pl.cdiv(m.shape[1], TILE) for m in mine)
    return line.call(
        functools.partial(weight_grad_kernel, len(mine)),
        (xt, y, *mine, *other),
        [shaped(*shape) for shape in shapes],
        out_specs=[IN_HBM] * 3,
        scratch=[
            pltpu.VMEM((3, y.shape[0], hidden_width), BF16),
            *(pltpu.VMEM(shape, BF16) for shape in shapes),
            pltpu.SemaphoreType.DMA((3, steps)),
        ],
        limit=40,
    )


def last_kernel(grad_ref, *out_refs):
    grad = grad_ref[...]
    rows = out_refs[0].shape[0]
    cuts = [grad[slot * rows : (slot + 1) * rows] for slot in range(len(out_refs))]
    wa = lax.axis_index("wa")
    for step, out_ref in enumerate(out_refs):
        at = wa ^ step
        piece = cuts[0]
        for slot in range(1, len(cuts)):
            piece = jnp.where(at == slot, cuts[slot], piece)
        out_ref[...] = piece.astype(out_ref.dtype)


def last_pieces(line, parts, grad):
    shape = (grad.shape[0] // parts, grad.shape[1])
    return line.call(
        last_kernel, (grad,), [shaped(*shape, F32)] + [shaped(*shape)] * (parts - 1)
    )


def total_kernel(own_ref, *refs):
    total = own_ref[...]
    for ref in refs[:-1]:
        total = total + ref[...].astype(F32)
    refs[-1][...] = total.astype(BF16)


def total(line, own, received):
    return line.call(total_kernel, (own, *received), [shaped(*own.shape)])[0]


def swap(value, axis, size, step):
    return lax.ppermute(value, axis, [(at, at ^ step) for at in range(size)])


def fast_body(n_wa, n_ha, n_row, tokens, cotangent, gate_weight, up_weight, down_weight):
    hidden_width = gate_weight.shape[1]
    tiles = hidden_width // LANES
    ends = [-(-tiles * (at + 1) // CHUNKS) * LANES for at in range(CHUNKS)]
    chunks = [(begin, end - begin) for begin, end in zip([0] + ends, ends)]
    axes = [((1, 2), (2, 1))[at % 2] for at in range(CHUNKS)]
    line = Line()

    both = jnp.concatenate([tokens, cotangent], axis=0)
    pieces = [both] + [swap(both, "ha", n_ha, step) for step in range(1, n_ha)]
    half = chunks[CHUNKS // 2][0]
    gate, up, down = load(Line(), gate_weight, up_weight, down_weight, half)
    xy = order_rows(line, pieces)
    xy_other = swap(xy, "row", n_row, 1)

    kept, got = [], []
    later = None
    for at, ((begin, columns), axis) in enumerate(zip(chunks, axes)):
        if at == 0:
            keep, send, later = forward(
                line, begin, columns, axis, xy, gate, up, down, begin, (down_weight, half)
            )
        elif begin < half:
            keep, send = forward(line, begin, columns, axis, xy, gate, up, down, begin)
        else:
            keep, send = forward(line, begin, columns, axis, xy, gate, up, later, begin - half)
        kept.append(keep)
        got.append(swap(send, "wa", n_wa, axis[0]))
    for at, (_, far) in enumerate(axes):
        kept[at], send = halve(line, kept[at], got[at])
        got[at] = swap(send, "wa", n_wa, far)
    order = [pair + 1 - at for pair in range(0, CHUNKS, 2) for at in range(2)]
    for at in order:
        kept[at] = middle(line, kept[at], got[at])
        got[at] = swap(kept[at], "wa", n_wa, axes[at][0])
    xt, y_all = factors(line, xy, xy_other)
    for at, (_, far) in enumerate(axes):
        kept[at] = join(line, kept[at], got[at])
        got[at] = swap(kept[at], "wa", n_wa, far)

    mine, other, grad = [], [], ()
    for at in range(0, CHUNKS, 2):
        pair = slice(at, at + 2)
        mine.append(stack(line, axes[pair], list(zip(kept, got))[pair]))
        other.append(swap(mine[-1], "row", n_row, 1))
        grad = input_grad(line, chunks[at][0], mine[-1], gate, up, grad)
    own, *sends = last_pieces(line, n_ha, grad[0])
    received = [swap(sent, "ha", n_ha, k + 1) for k, sent in enumerate(sends)]
    grads = weight_grad(line, xt, y_all, mine, other)
    return (total(line, own, received), *grads)


def plain_body(tokens, cotangent, gate_weight, up_weight, down_weight):
    hidden_width = gate_weight.shape[1]
    x = lax.all_gather(tokens, "ha", axis=0, tiled=True)
    y = lax.all_gather(cotangent, "ha", axis=0, tiled=True)
    gate_part = jnp.dot(x, gate_weight, preferred_element_type=F32)
    up_part = jnp.dot(x, up_weight, preferred_element_type=F32)
    dh_part = lax.dot_general(y, down_weight, NT, preferred_element_type=F32)
    summed = lax.psum(jnp.concatenate([gate_part, up_part, dh_part], axis=1), "wa")
    hidden, d_gate, d_up = pointwise(
        summed[:, :hidden_width],
        summed[:, hidden_width : 2 * hidden_width],
        summed[:, 2 * hidden_width :],
    )
    partial = lax.dot_general(
        d_gate, gate_weight, NT, preferred_element_type=F32
    ) + lax.dot_general(d_up, up_weight, NT, preferred_element_type=F32)
    grad_tokens = lax.psum_scatter(partial, "ha", scatter_dimension=0, tiled=True)
    grads = (
        lax.dot_general(x, d_gate, TN, preferred_element_type=F32),
        lax.dot_general(x, d_up, TN, preferred_element_type=F32),
        lax.dot_general(hidden, y, TN, preferred_element_type=F32),
    )
    return (
        grad_tokens.astype(BF16),
        *(lax.psum(g.astype(BF16), "row").astype(BF16) for g in grads),
    )


def solution(mesh):
    n_wa, n_ha, n_row = (mesh.shape[name] for name in ("wa", "ha", "row"))

    def body(tokens, cotangent, gate_weight, up_weight, down_weight):
        width, hidden_width = gate_weight.shape
        fits = (
            n_wa == n_ha == 4
            and n_row == 2
            and width % LANES == 0
            and hidden_width % LANES == 0
            and hidden_width >= LANES * CHUNKS
            and width % (16 * CUTS) == 0
            and (tokens.shape[0] * n_ha) % 16 == 0
        )
        if fits:
            return fast_body(
                n_wa, n_ha, n_row, tokens, cotangent, gate_weight, up_weight, down_weight
            )
        return plain_body(tokens, cotangent, gate_weight, up_weight, down_weight)

    return jax.shard_map(
        body,
        mesh=mesh,
        in_specs=(
            P(("row", "ha"), "wa"),
            P(("row", "ha"), "wa"),
            P("wa", "ha"),
            P("wa", "ha"),
            P("ha", "wa"),
        ),
        out_specs=(P(("row", "ha"), "wa"), P("wa", "ha"), P("wa", "ha"), P("ha", "wa")),
        check_vma=False,
    )
```

```python
import functools

import jax
import jax.numpy as jnp
from jax import lax
from jax.experimental import pallas as pl
from jax.experimental.pallas import tpu as pltpu
from jax.sharding import PartitionSpec as P

BF16 = jnp.bfloat16
F32 = jnp.float32
NT = (((1,), (1,)), ((), ()))
TN = (((0,), (0,)), ((), ()))
LANES = 128
CHUNKS = 4
TILE = 256
CUTS = 4
MIB = 1024 * 1024
IN_VMEM = pl.BlockSpec(memory_space=pltpu.VMEM)
IN_HBM = pl.BlockSpec(memory_space=pl.ANY)


def shaped(rows, columns, dtype=BF16):
    return jax.ShapeDtypeStruct((rows, columns), dtype)


def joined(*blocks):
    return jnp.concatenate([block.astype(F32) for block in blocks], axis=0)


def pointwise(gate_sum, up_sum, dh_sum):
    sig = jax.nn.sigmoid(gate_sum)
    active = gate_sum * sig
    hidden = (active * up_sum).astype(BF16)
    d_up = (dh_sum * active).astype(BF16)
    d_gate = (dh_sum * up_sum * sig * (1.0 + gate_sum * (1.0 - sig))).astype(BF16)
    return (hidden, d_gate, d_up)


class Line:
    def __init__(self):
        self.token = ()

    def call(
        self,
        kernel,
        args,
        out_shape,
        in_specs=None,
        out_specs=None,
        scratch=(),
        aliases=None,
        limit=4,
    ):
        count, outs, tokens = len(args), len(out_shape), len(self.token)

        def body(*refs):
            rest = refs[count + tokens :]
            rest[outs][...] = jnp.zeros_like(rest[outs])
            kernel(*refs[:count], *rest[:outs], *rest[outs + 1 :])

        *results, token = pl.pallas_call(
            body,
            in_specs=(in_specs or [IN_VMEM] * count) + [IN_VMEM] * tokens,
            out_specs=(out_specs or [IN_VMEM] * outs) + [IN_VMEM],
            out_shape=[*out_shape, shaped(8, LANES, F32)],
            scratch_shapes=list(scratch),
            input_output_aliases=aliases or {},
            cost_estimate=pl.CostEstimate(flops=1, bytes_accessed=1, transcendentals=0),
            compiler_params=pltpu.CompilerParams(vmem_limit_bytes=limit * MIB),
            name=getattr(kernel, "func", kernel).__name__,
        )(*args, *self.token)
        self.token = (token,)
        return results


def copy_rows(sems, source, target, begin=0):
    rows = target.shape[0] // CUTS
    copies = []
    for cut in range(CUTS):
        there, here = pl.ds(begin + cut * rows, rows), pl.ds(cut * rows, rows)
        copies.append(pltpu.make_async_copy(source.at[there], target.at[here], sems.at[cut]))
        copies[-1].start()
    return copies


def load_kernel(gate_ref, up_ref, down_ref, gate_out, up_out, down_out, sems):
    copies = copy_rows(sems.at[0], gate_ref, gate_out)
    copies += copy_rows(sems.at[1], up_ref, up_out)
    copies += copy_rows(sems.at[2], down_ref, down_out)
    for copy in copies:
        copy.wait()


def load(line, gate_weight, up_weight, down_weight, rows):
    shapes = [gate_weight.shape, up_weight.shape, (rows, down_weight.shape[1])]
    return line.call(
        load_kernel,
        (gate_weight, up_weight, down_weight),
        [pltpu.VMEM(shape, BF16) for shape in shapes],
        in_specs=[IN_HBM] * 3,
        scratch=[pltpu.SemaphoreType.DMA((3, CUTS))],
        limit=30,
    )


def order_kernel(*refs):
    *piece_refs, out_ref = refs
    pieces = [ref[...].astype(F32) for ref in piece_refs]
    rows = pieces[0].shape[0] // 2
    wa = lax.axis_index("wa")
    slots = []
    for slot in range(len(pieces)):
        at = wa ^ slot
        piece = pieces[0]
        for other in range(1, len(pieces)):
            piece = jnp.where(at == other, pieces[other], piece)
        slots.append(piece)
    out_ref[...] = joined(
        *(slot[:rows] for slot in slots), *(slot[rows:] for slot in slots)
    ).astype(BF16)


def order_rows(line, pieces):
    rows, width = pieces[0].shape
    return line.call(order_kernel, pieces, [shaped(4 * rows, width)])[0]


def forward_kernel(begin, near, far, later, *refs):
    xy_ref, gate_ref, up_ref, down_ref, *refs = refs
    copies = []
    if later is not None:
        all_ref, keep_ref, send_ref, later_ref, sems = refs
        copies = copy_rows(sems, all_ref, later_ref, later)
    else:
        keep_ref, send_ref = refs
    columns = keep_ref.shape[1]
    group = xy_ref.shape[0] // 2
    rows = group // 4
    x, y = xy_ref[:group], xy_ref[group:]
    there = pl.ds(begin, columns)
    gate = jnp.dot(x, gate_ref[:, there], preferred_element_type=F32)
    up = jnp.dot(x, up_ref[:, there], preferred_element_type=F32)
    dh = lax.dot_general(y, down_ref[...], NT, preferred_element_type=F32)

    def slots(*which):
        cuts = [slice(slot * rows, (slot + 1) * rows) for slot in which]
        return joined(*(part[cut] for cut in cuts for part in (gate, up, dh)))

    keep_ref[...] = slots(0, far)
    send_ref[...] = slots(near, near ^ far).astype(BF16)
    for copy in copies:
        copy.wait()


def forward(line, begin, columns, axes, xy, gate, up, down, rest=None):
    rows = 6 * (xy.shape[0] // 8)
    args, specs = [xy, gate, up, down], [IN_VMEM] * 4
    shapes = [shaped(rows, columns, F32), shaped(rows, columns)]
    later = None
    if rest is not None:
        weight, later, size = rest
        args.append(weight)
        specs.append(IN_HBM)
        shapes.append(pltpu.VMEM((size, weight.shape[1]), BF16))
    return line.call(
        functools.partial(forward_kernel, begin, *axes, later),
        args,
        shapes,
        in_specs=specs,
        scratch=[pltpu.SemaphoreType.DMA((CUTS,))] if rest is not None else [],
        limit=25 if rest is not None else 4,
    )


def halve_kernel(keep_ref, received_ref, own_ref, send_ref):
    total = keep_ref[...] + received_ref[...].astype(F32)
    half = own_ref.shape[0]
    own_ref[...] = total[:half]
    send_ref[...] = total[half:].astype(BF16)


def halve(line, keep, received):
    shape = (keep.shape[0] // 2, keep.shape[1])
    return line.call(halve_kernel, (keep, received), [shaped(*shape, F32), shaped(*shape)])


def middle_kernel(own_ref, received_ref, out_ref):
    total = own_ref[...] + received_ref[...].astype(F32)
    rows = total.shape[0] // 3
    hidden, d_gate, d_up = pointwise(total[:rows], total[rows : 2 * rows], total[2 * rows :])
    out_ref[...] = joined(d_gate, d_up, hidden).astype(BF16)


def middle(line, own, received):
    return line.call(middle_kernel, (own, received), [shaped(*own.shape)])[0]


def join_kernel(first_ref, second_ref, out_ref):
    out_ref[...] = joined(first_ref[...], second_ref[...]).astype(BF16)


def join(line, first, second):
    rows = first.shape[0] + second.shape[0]
    return line.call(join_kernel, (first, second), [shaped(rows, first.shape[1])])[0]


def stack_kernel(axes, *refs):
    out_ref = refs[-1]
    begin = 0
    for at, (near, far) in enumerate(axes):
        mine, other = refs[2 * at][...].astype(F32), refs[2 * at + 1][...].astype(F32)
        columns = mine.shape[1]
        half, rows = mine.shape[0] // 2, mine.shape[0] // 6
        slots = {0: mine[:half], near: mine[half:]}
        slots |= {far: other[:half], near ^ far: other[half:]}
        cuts = [slots[slot][k * rows : (k + 1) * rows] for k in range(3) for slot in range(4)]
        out_ref[:, begin : begin + columns] = joined(*cuts).astype(BF16)
        begin += columns


def stack(line, axes, blocks):
    rows = 2 * blocks[0][0].shape[0]
    columns = sum(mine.shape[1] for mine, _ in blocks)
    return line.call(
        functools.partial(stack_kernel, axes),
        [block for pair in blocks for block in pair],
        [shaped(rows, columns)],
    )[0]


def input_grad_kernel(begin, stack_ref, gate_ref, up_ref, *refs):
    there = pl.ds(begin, stack_ref.shape[1])
    group = stack_ref.shape[0] // 3
    grad = lax.dot_general(
        stack_ref[:group], gate_ref[:, there], NT, preferred_element_type=F32
    ) + lax.dot_general(
        stack_ref[group : 2 * group], up_ref[:, there], NT, preferred_element_type=F32
    )
    refs[-1][...] = grad + refs[0][...] if len(refs) > 1 else grad


def input_grad(line, begin, stacked, gate_weight, up_weight, start):
    shape = (stacked.shape[0] // 3, gate_weight.shape[0])
    return line.call(
        functools.partial(input_grad_kernel, begin),
        (stacked, gate_weight, up_weight, *start),
        [shaped(*shape, F32)],
    )


def factors_kernel(mine_ref, other_ref, xt_ref, y_all_ref):
    group = mine_ref.shape[0] // 2
    first = lax.axis_index("row") == 0
    x, y = mine_ref[:group], mine_ref[group:]
    x_other, y_other = other_ref[:group], other_ref[group:]
    y_all_ref[:group] = jnp.where(first, y, y_other)
    y_all_ref[group:] = jnp.where(first, y_other, y)
    x_all = jnp.concatenate([jnp.where(first, x, x_other), jnp.where(first, x_other, x)], axis=0)
    xt_ref[...] = x_all.T


def factors(line, xy, other):
    rows, width = xy.shape
    return line.call(factors_kernel, (xy, other), [shaped(width, rows), shaped(rows, width)])


def weight_grad_kernel(parts, xt_ref, y_ref, *refs):
    mine_refs, other_refs = refs[:parts], refs[parts : 2 * parts]
    *outs, both, gate, up, down, sems = refs[2 * parts :]
    group = y_ref.shape[0] // 2
    first = lax.axis_index("row") == 0
    copies = []

    def send(at, source, target):
        copies.append(pltpu.make_async_copy(source, target, sems.at[at, len(copies) // 3]))
        copies[-1].start()

    begin = 0
    for mine_ref, other_ref in zip(mine_refs, other_refs):
        columns = mine_ref.shape[1]
        for start in range(0, columns, TILE):
            size = min(TILE, columns - start)
            source, here = pl.ds(start, size), pl.ds(begin + start, size)
            for at in range(3):
                cut = slice(at * group, (at + 1) * group)
                mine, other = mine_ref[cut, source], other_ref[cut, source]
                both[at, :group, here] = jnp.where(first, mine, other)
                both[at, group:, here] = jnp.where(first, other, mine)
            gate[:, here] = jnp.dot(
                xt_ref[...], both[0, :, here], preferred_element_type=F32
            ).astype(BF16)
            send(0, gate.at[:, here], outs[0].at[:, here])
            up[:, here] = jnp.dot(
                xt_ref[...], both[1, :, here], preferred_element_type=F32
            ).astype(BF16)
            send(1, up.at[:, here], outs[1].at[:, here])
            down[here, :] = lax.dot_general(
                both[2, :, here], y_ref[...], TN, preferred_element_type=F32
            ).astype(BF16)
            send(2, down.at[here], outs[2].at[here])
        begin += columns
    for copy in copies:
        copy.wait()


def weight_grad(line, xt, y, mine, other):
    width = xt.shape[0]
    hidden_width = sum(m.shape[1] for m in mine)
    shapes = [(width, hidden_width), (width, hidden_width), (hidden_width, width)]
    steps = sum(pl.cdiv(m.shape[1], TILE) for m in mine)
    return line.call(
        functools.partial(weight_grad_kernel, len(mine)),
        (xt, y, *mine, *other),
        [shaped(*shape) for shape in shapes],
        out_specs=[IN_HBM] * 3,
        scratch=[
            pltpu.VMEM((3, y.shape[0], hidden_width), BF16),
            *(pltpu.VMEM(shape, BF16) for shape in shapes),
            pltpu.SemaphoreType.DMA((3, steps)),
        ],
        limit=40,
    )


def last_kernel(grad_ref, *out_refs):
    grad = grad_ref[...]
    rows = out_refs[0].shape[0]
    cuts = [grad[slot * rows : (slot + 1) * rows] for slot in range(len(out_refs))]
    wa = lax.axis_index("wa")
    for step, out_ref in enumerate(out_refs):
        at = wa ^ step
        piece = cuts[0]
        for slot in range(1, len(cuts)):
            piece = jnp.where(at == slot, cuts[slot], piece)
        out_ref[...] = piece.astype(out_ref.dtype)


def last_pieces(line, parts, grad):
    shape = (grad.shape[0] // parts, grad.shape[1])
    return line.call(
        last_kernel, (grad,), [shaped(*shape, F32)] + [shaped(*shape)] * (parts - 1)
    )


def total_kernel(own_ref, *refs):
    total = own_ref[...]
    for ref in refs[:-1]:
        total = total + ref[...].astype(F32)
    refs[-1][...] = total.astype(BF16)


def total(line, own, received):
    return line.call(total_kernel, (own, *received), [shaped(*own.shape)])[0]


def swap(value, axis, size, step):
    return lax.ppermute(value, axis, [(at, at ^ step) for at in range(size)])


def fast_body(n_wa, n_ha, n_row, tokens, cotangent, gate_weight, up_weight, down_weight):
    hidden_width = gate_weight.shape[1]
    tiles = hidden_width // LANES
    ends = [-(-tiles * (at + 1) // CHUNKS) * LANES for at in range(CHUNKS)]
    chunks = [(begin, end - begin) for begin, end in zip([0] + ends, ends)]
    axes = [((1, 2), (2, 1))[at % 2] for at in range(CHUNKS)]
    line = Line()

    both = jnp.concatenate([tokens, cotangent], axis=0)
    pieces = [both] + [swap(both, "ha", n_ha, step) for step in range(1, n_ha)]
    gate, up, down = load(Line(), gate_weight, up_weight, down_weight, chunks[0][1])
    xy = order_rows(line, pieces)
    xy_other = swap(xy, "row", n_row, 1)

    kept, got = [], []
    for at, ((begin, columns), axis) in enumerate(zip(chunks, axes)):
        rest = (down_weight, *chunks[at + 1]) if at + 1 < CHUNKS else None
        keep, send, *down_next = forward(
            line, begin, columns, axis, xy, gate, up, down, rest
        )
        down = down_next[0] if down_next else None
        kept.append(keep)
        got.append(swap(send, "wa", n_wa, axis[0]))
    for at, (_, far) in enumerate(axes):
        kept[at], send = halve(line, kept[at], got[at])
        got[at] = swap(send, "wa", n_wa, far)
    order = [1, 0, 3, 2]
    for at in order:
        kept[at] = middle(line, kept[at], got[at])
        got[at] = swap(kept[at], "wa", n_wa, axes[at][0])
    for at in [1, 0, 3, 2]:
        far = axes[at][1]
        kept[at] = join(line, kept[at], got[at])
        got[at] = swap(kept[at], "wa", n_wa, far)

    xt, y_all = factors(line, xy, xy_other)
    mine, other, grad = [], [], ()
    for at in range(0, CHUNKS, 2):
        pair = slice(at, at + 2)
        mine.append(stack(line, axes[pair], list(zip(kept, got))[pair]))
        other.append(swap(mine[-1], "row", n_row, 1))
        grad = input_grad(line, chunks[at][0], mine[-1], gate, up, grad)
    own, *sends = last_pieces(line, n_ha, grad[0])
    received = [swap(sent, "ha", n_ha, k + 1) for k, sent in enumerate(sends)]
    grads = weight_grad(line, xt, y_all, mine, other)
    return (total(line, own, received), *grads)


def plain_body(tokens, cotangent, gate_weight, up_weight, down_weight):
    hidden_width = gate_weight.shape[1]
    x = lax.all_gather(tokens, "ha", axis=0, tiled=True)
    y = lax.all_gather(cotangent, "ha", axis=0, tiled=True)
    gate_part = jnp.dot(x, gate_weight, preferred_element_type=F32)
    up_part = jnp.dot(x, up_weight, preferred_element_type=F32)
    dh_part = lax.dot_general(y, down_weight, NT, preferred_element_type=F32)
    summed = lax.psum(jnp.concatenate([gate_part, up_part, dh_part], axis=1), "wa")
    hidden, d_gate, d_up = pointwise(
        summed[:, :hidden_width],
        summed[:, hidden_width : 2 * hidden_width],
        summed[:, 2 * hidden_width :],
    )
    partial = lax.dot_general(
        d_gate, gate_weight, NT, preferred_element_type=F32
    ) + lax.dot_general(d_up, up_weight, NT, preferred_element_type=F32)
    grad_tokens = lax.psum_scatter(partial, "ha", scatter_dimension=0, tiled=True)
    grads = (
        lax.dot_general(x, d_gate, TN, preferred_element_type=F32),
        lax.dot_general(x, d_up, TN, preferred_element_type=F32),
        lax.dot_general(hidden, y, TN, preferred_element_type=F32),
    )
    return (
        grad_tokens.astype(BF16),
        *(lax.psum(g.astype(BF16), "row").astype(BF16) for g in grads),
    )


def solution(mesh):
    n_wa, n_ha, n_row = (mesh.shape[name] for name in ("wa", "ha", "row"))

    def body(tokens, cotangent, gate_weight, up_weight, down_weight):
        width, hidden_width = gate_weight.shape
        fits = (
            n_wa == n_ha == 4
            and n_row == 2
            and width % LANES == 0
            and hidden_width % LANES == 0
            and hidden_width >= LANES * CHUNKS
            and width % (16 * CUTS) == 0
            and (tokens.shape[0] * n_ha) % 16 == 0
        )
        if fits:
            return fast_body(
                n_wa, n_ha, n_row, tokens, cotangent, gate_weight, up_weight, down_weight
            )
        return plain_body(tokens, cotangent, gate_weight, up_weight, down_weight)

    return jax.shard_map(
        body,
        mesh=mesh,
        in_specs=(
            P(("row", "ha"), "wa"),
            P(("row", "ha"), "wa"),
            P("wa", "ha"),
            P("wa", "ha"),
            P("ha", "wa"),
        ),
        out_specs=(P(("row", "ha"), "wa"), P("wa", "ha"), P("wa", "ha"), P("ha", "wa")),
        check_vma=False,
    )
```

```python
import functools

import jax
import jax.numpy as jnp
from jax import lax
from jax.experimental import pallas as pl
from jax.experimental.pallas import tpu as pltpu
from jax.sharding import PartitionSpec as P

BF16 = jnp.bfloat16
F32 = jnp.float32
NT = (((1,), (1,)), ((), ()))
TN = (((0,), (0,)), ((), ()))
LANES = 128
CHUNKS = 4
TILE = 256
CUTS = 4
MIB = 1024 * 1024
IN_VMEM = pl.BlockSpec(memory_space=pltpu.VMEM)
IN_HBM = pl.BlockSpec(memory_space=pl.ANY)


def shaped(rows, columns, dtype=BF16):
    return jax.ShapeDtypeStruct((rows, columns), dtype)


def joined(*blocks):
    return jnp.concatenate([block.astype(F32) for block in blocks], axis=0)


def pointwise(gate_sum, up_sum, dh_sum):
    sig = jax.nn.sigmoid(gate_sum)
    active = gate_sum * sig
    hidden = (active * up_sum).astype(BF16)
    d_up = (dh_sum * active).astype(BF16)
    d_gate = (dh_sum * up_sum * sig * (1.0 + gate_sum * (1.0 - sig))).astype(BF16)
    return (hidden, d_gate, d_up)


class Line:
    def __init__(self):
        self.token = ()

    def call(
        self,
        kernel,
        args,
        out_shape,
        in_specs=None,
        out_specs=None,
        scratch=(),
        aliases=None,
        limit=4,
    ):
        count, outs, tokens = len(args), len(out_shape), len(self.token)

        def body(*refs):
            rest = refs[count + tokens :]
            rest[outs][...] = jnp.zeros_like(rest[outs])
            kernel(*refs[:count], *rest[:outs], *rest[outs + 1 :])

        *results, token = pl.pallas_call(
            body,
            in_specs=(in_specs or [IN_VMEM] * count) + [IN_VMEM] * tokens,
            out_specs=(out_specs or [IN_VMEM] * outs) + [IN_VMEM],
            out_shape=[*out_shape, shaped(8, LANES, F32)],
            scratch_shapes=list(scratch),
            input_output_aliases=aliases or {},
            cost_estimate=pl.CostEstimate(flops=1, bytes_accessed=1, transcendentals=0),
            compiler_params=pltpu.CompilerParams(vmem_limit_bytes=limit * MIB),
            name=getattr(kernel, "func", kernel).__name__,
        )(*args, *self.token)
        self.token = (token,)
        return results


def copy_rows(sems, source, target, begin=0):
    rows = target.shape[0] // CUTS
    copies = []
    for cut in range(CUTS):
        there, here = pl.ds(begin + cut * rows, rows), pl.ds(cut * rows, rows)
        copies.append(pltpu.make_async_copy(source.at[there], target.at[here], sems.at[cut]))
        copies[-1].start()
    return copies


def load_kernel(gate_ref, up_ref, gate_out, up_out, sems):
    copies = copy_rows(sems.at[0], gate_ref, gate_out)
    copies += copy_rows(sems.at[1], up_ref, up_out)
    for copy in copies:
        copy.wait()


def load(line, *weights):
    return line.call(
        load_kernel,
        weights,
        [pltpu.VMEM(weight.shape, BF16) for weight in weights],
        in_specs=[IN_HBM] * len(weights),
        scratch=[pltpu.SemaphoreType.DMA((len(weights), CUTS))],
        limit=30,
    )


def order_kernel(*refs):
    *piece_refs, out_ref = refs
    pieces = [ref[...].astype(F32) for ref in piece_refs]
    rows = pieces[0].shape[0] // 2
    wa = lax.axis_index("wa")
    slots = []
    for slot in range(len(pieces)):
        at = wa ^ slot
        piece = pieces[0]
        for other in range(1, len(pieces)):
            piece = jnp.where(at == other, pieces[other], piece)
        slots.append(piece)
    out_ref[...] = joined(
        *(slot[:rows] for slot in slots), *(slot[rows:] for slot in slots)
    ).astype(BF16)


def order_rows(line, pieces):
    rows, width = pieces[0].shape
    return line.call(order_kernel, pieces, [shaped(4 * rows, width)])[0]


def forward_kernel(begin, near, far, xy_ref, gate_ref, up_ref, down_ref, keep_ref, send_ref):
    there = pl.ds(begin, keep_ref.shape[1])
    group = xy_ref.shape[0] // 2
    rows = group // 4
    x, y = xy_ref[:group], xy_ref[group:]
    gate = jnp.dot(x, gate_ref[:, there], preferred_element_type=F32)
    up = jnp.dot(x, up_ref[:, there], preferred_element_type=F32)
    dh = lax.dot_general(y, down_ref[there], NT, preferred_element_type=F32)

    def slots(*which):
        cuts = [slice(slot * rows, (slot + 1) * rows) for slot in which]
        return joined(*(part[cut] for cut in cuts for part in (gate, up, dh)))

    keep_ref[...] = slots(0, far)
    send_ref[...] = slots(near, near ^ far).astype(BF16)


def forward(line, begin, columns, axes, xy, gate, up, down):
    rows = 6 * (xy.shape[0] // 8)
    return line.call(
        functools.partial(forward_kernel, begin, *axes),
        (xy, gate, up, down),
        [shaped(rows, columns, F32), shaped(rows, columns)],
    )


def halve_kernel(keep_ref, received_ref, own_ref, send_ref):
    total = keep_ref[...] + received_ref[...].astype(F32)
    half = own_ref.shape[0]
    own_ref[...] = total[:half]
    send_ref[...] = total[half:].astype(BF16)


def halve(line, keep, received):
    shape = (keep.shape[0] // 2, keep.shape[1])
    return line.call(halve_kernel, (keep, received), [shaped(*shape, F32), shaped(*shape)])


def middle_kernel(own_ref, received_ref, out_ref):
    total = own_ref[...] + received_ref[...].astype(F32)
    rows = total.shape[0] // 3
    hidden, d_gate, d_up = pointwise(total[:rows], total[rows : 2 * rows], total[2 * rows :])
    out_ref[...] = joined(d_gate, d_up, hidden).astype(BF16)


def middle(line, own, received):
    return line.call(middle_kernel, (own, received), [shaped(*own.shape)])[0]


def join_kernel(first_ref, second_ref, out_ref):
    out_ref[...] = joined(first_ref[...], second_ref[...]).astype(BF16)


def join(line, first, second):
    rows = first.shape[0] + second.shape[0]
    return line.call(join_kernel, (first, second), [shaped(rows, first.shape[1])])[0]


def stack_kernel(axes, *refs):
    out_ref = refs[-1]
    begin = 0
    for at, (near, far) in enumerate(axes):
        mine, other = refs[2 * at][...].astype(F32), refs[2 * at + 1][...].astype(F32)
        columns = mine.shape[1]
        half, rows = mine.shape[0] // 2, mine.shape[0] // 6
        slots = {0: mine[:half], near: mine[half:]}
        slots |= {far: other[:half], near ^ far: other[half:]}
        cuts = [slots[slot][k * rows : (k + 1) * rows] for k in range(3) for slot in range(4)]
        out_ref[:, begin : begin + columns] = joined(*cuts).astype(BF16)
        begin += columns


def stack(line, axes, blocks):
    rows = 2 * blocks[0][0].shape[0]
    columns = sum(mine.shape[1] for mine, _ in blocks)
    return line.call(
        functools.partial(stack_kernel, axes),
        [block for pair in blocks for block in pair],
        [shaped(rows, columns)],
    )[0]


def input_grad_kernel(begin, stack_ref, gate_ref, up_ref, *refs):
    there = pl.ds(begin, stack_ref.shape[1])
    group = stack_ref.shape[0] // 3
    grad = lax.dot_general(
        stack_ref[:group], gate_ref[:, there], NT, preferred_element_type=F32
    ) + lax.dot_general(
        stack_ref[group : 2 * group], up_ref[:, there], NT, preferred_element_type=F32
    )
    refs[-1][...] = grad + refs[0][...] if len(refs) > 1 else grad


def input_grad(line, begin, stacked, gate_weight, up_weight, start):
    shape = (stacked.shape[0] // 3, gate_weight.shape[0])
    return line.call(
        functools.partial(input_grad_kernel, begin),
        (stacked, gate_weight, up_weight, *start),
        [shaped(*shape, F32)],
    )


def factors_kernel(mine_ref, other_ref, xt_ref, y_all_ref):
    group = mine_ref.shape[0] // 2
    first = lax.axis_index("row") == 0
    x, y = mine_ref[:group], mine_ref[group:]
    x_other, y_other = other_ref[:group], other_ref[group:]
    y_all_ref[:group] = jnp.where(first, y, y_other)
    y_all_ref[group:] = jnp.where(first, y_other, y)
    x_all = jnp.concatenate([jnp.where(first, x, x_other), jnp.where(first, x_other, x)], axis=0)
    xt_ref[...] = x_all.T


def factors(line, xy, other):
    rows, width = xy.shape
    return line.call(factors_kernel, (xy, other), [shaped(width, rows), shaped(rows, width)])


def weight_grad_kernel(parts, xt_ref, y_ref, *refs):
    mine_refs, other_refs = refs[:parts], refs[parts : 2 * parts]
    *outs, both, gate, up, down, sems = refs[2 * parts :]
    group = y_ref.shape[0] // 2
    first = lax.axis_index("row") == 0
    copies = []

    def send(at, source, target):
        copies.append(pltpu.make_async_copy(source, target, sems.at[at, len(copies) // 3]))
        copies[-1].start()

    begin = 0
    for mine_ref, other_ref in zip(mine_refs, other_refs):
        columns = mine_ref.shape[1]
        for start in range(0, columns, TILE):
            size = min(TILE, columns - start)
            source, here = pl.ds(start, size), pl.ds(begin + start, size)
            for at in range(3):
                cut = slice(at * group, (at + 1) * group)
                mine, other = mine_ref[cut, source], other_ref[cut, source]
                both[at, :group, here] = jnp.where(first, mine, other)
                both[at, group:, here] = jnp.where(first, other, mine)
            gate[:, here] = jnp.dot(
                xt_ref[...], both[0, :, here], preferred_element_type=F32
            ).astype(BF16)
            send(0, gate.at[:, here], outs[0].at[:, here])
            up[:, here] = jnp.dot(
                xt_ref[...], both[1, :, here], preferred_element_type=F32
            ).astype(BF16)
            send(1, up.at[:, here], outs[1].at[:, here])
            down[here, :] = lax.dot_general(
                both[2, :, here], y_ref[...], TN, preferred_element_type=F32
            ).astype(BF16)
            send(2, down.at[here], outs[2].at[here])
        begin += columns
    for copy in copies:
        copy.wait()


def weight_grad(line, xt, y, mine, other):
    width = xt.shape[0]
    hidden_width = sum(m.shape[1] for m in mine)
    shapes = [(width, hidden_width), (width, hidden_width), (hidden_width, width)]
    steps = sum(pl.cdiv(m.shape[1], TILE) for m in mine)
    return line.call(
        functools.partial(weight_grad_kernel, len(mine)),
        (xt, y, *mine, *other),
        [shaped(*shape) for shape in shapes],
        out_specs=[IN_HBM] * 3,
        scratch=[
            pltpu.VMEM((3, y.shape[0], hidden_width), BF16),
            *(pltpu.VMEM(shape, BF16) for shape in shapes),
            pltpu.SemaphoreType.DMA((3, steps)),
        ],
        limit=40,
    )


def last_kernel(grad_ref, *out_refs):
    grad = grad_ref[...]
    rows = out_refs[0].shape[0]
    cuts = [grad[slot * rows : (slot + 1) * rows] for slot in range(len(out_refs))]
    wa = lax.axis_index("wa")
    for step, out_ref in enumerate(out_refs):
        at = wa ^ step
        piece = cuts[0]
        for slot in range(1, len(cuts)):
            piece = jnp.where(at == slot, cuts[slot], piece)
        out_ref[...] = piece.astype(out_ref.dtype)


def last_pieces(line, parts, grad):
    shape = (grad.shape[0] // parts, grad.shape[1])
    return line.call(
        last_kernel, (grad,), [shaped(*shape, F32)] + [shaped(*shape)] * (parts - 1)
    )


def total_kernel(own_ref, *refs):
    total = own_ref[...]
    for ref in refs[:-1]:
        total = total + ref[...].astype(F32)
    refs[-1][...] = total.astype(BF16)


def total(line, own, received):
    return line.call(total_kernel, (own, *received), [shaped(*own.shape)])[0]


def swap(value, axis, size, step):
    return lax.ppermute(value, axis, [(at, at ^ step) for at in range(size)])


def fast_body(n_wa, n_ha, n_row, tokens, cotangent, gate_weight, up_weight, down_weight):
    hidden_width = gate_weight.shape[1]
    tiles = hidden_width // LANES
    ends = [-(-tiles * (at + 1) // CHUNKS) * LANES for at in range(CHUNKS)]
    chunks = [(begin, end - begin) for begin, end in zip([0] + ends, ends)]
    axes = [((1, 2), (2, 1))[at % 2] for at in range(CHUNKS)]
    line = Line()

    both = jnp.concatenate([tokens, cotangent], axis=0)
    pieces = [both] + [swap(both, "ha", n_ha, step) for step in range(1, n_ha)]
    gate, up = load(Line(), gate_weight, up_weight)
    xy = order_rows(line, pieces)
    xy_other = swap(xy, "row", n_row, 1)

    kept, got = [], []
    for at, ((begin, columns), axis) in enumerate(zip(chunks, axes)):
        keep, send = forward(line, begin, columns, axis, xy, gate, up, down_weight)
        kept.append(keep)
        got.append(swap(send, "wa", n_wa, axis[0]))
    for at, (_, far) in enumerate(axes):
        kept[at], send = halve(line, kept[at], got[at])
        got[at] = swap(send, "wa", n_wa, far)
    order = [1, 0, 3, 2]
    for at in order:
        kept[at] = middle(line, kept[at], got[at])
        got[at] = swap(kept[at], "wa", n_wa, axes[at][0])
    for at in [1, 0, 3, 2]:
        far = axes[at][1]
        kept[at] = join(line, kept[at], got[at])
        got[at] = swap(kept[at], "wa", n_wa, far)

    xt, y_all = factors(line, xy, xy_other)
    mine, other, grad = [], [], ()
    for at in range(0, CHUNKS, 2):
        pair = slice(at, at + 2)
        mine.append(stack(line, axes[pair], list(zip(kept, got))[pair]))
        other.append(swap(mine[-1], "row", n_row, 1))
        grad = input_grad(line, chunks[at][0], mine[-1], gate, up, grad)
    own, *sends = last_pieces(line, n_ha, grad[0])
    received = [swap(sent, "ha", n_ha, k + 1) for k, sent in enumerate(sends)]
    grads = weight_grad(line, xt, y_all, mine, other)
    return (total(line, own, received), *grads)


def plain_body(tokens, cotangent, gate_weight, up_weight, down_weight):
    hidden_width = gate_weight.shape[1]
    x = lax.all_gather(tokens, "ha", axis=0, tiled=True)
    y = lax.all_gather(cotangent, "ha", axis=0, tiled=True)
    gate_part = jnp.dot(x, gate_weight, preferred_element_type=F32)
    up_part = jnp.dot(x, up_weight, preferred_element_type=F32)
    dh_part = lax.dot_general(y, down_weight, NT, preferred_element_type=F32)
    summed = lax.psum(jnp.concatenate([gate_part, up_part, dh_part], axis=1), "wa")
    hidden, d_gate, d_up = pointwise(
        summed[:, :hidden_width],
        summed[:, hidden_width : 2 * hidden_width],
        summed[:, 2 * hidden_width :],
    )
    partial = lax.dot_general(
        d_gate, gate_weight, NT, preferred_element_type=F32
    ) + lax.dot_general(d_up, up_weight, NT, preferred_element_type=F32)
    grad_tokens = lax.psum_scatter(partial, "ha", scatter_dimension=0, tiled=True)
    grads = (
        lax.dot_general(x, d_gate, TN, preferred_element_type=F32),
        lax.dot_general(x, d_up, TN, preferred_element_type=F32),
        lax.dot_general(hidden, y, TN, preferred_element_type=F32),
    )
    return (
        grad_tokens.astype(BF16),
        *(lax.psum(g.astype(BF16), "row").astype(BF16) for g in grads),
    )


def solution(mesh):
    n_wa, n_ha, n_row = (mesh.shape[name] for name in ("wa", "ha", "row"))

    def body(tokens, cotangent, gate_weight, up_weight, down_weight):
        width, hidden_width = gate_weight.shape
        fits = (
            n_wa == n_ha == 4
            and n_row == 2
            and width % LANES == 0
            and hidden_width % LANES == 0
            and hidden_width >= LANES * CHUNKS
            and width % (16 * CUTS) == 0
            and (tokens.shape[0] * n_ha) % 16 == 0
        )
        if fits:
            return fast_body(
                n_wa, n_ha, n_row, tokens, cotangent, gate_weight, up_weight, down_weight
            )
        return plain_body(tokens, cotangent, gate_weight, up_weight, down_weight)

    return jax.shard_map(
        body,
        mesh=mesh,
        in_specs=(
            P(("row", "ha"), "wa"),
            P(("row", "ha"), "wa"),
            P("wa", "ha"),
            P("wa", "ha"),
            P("ha", "wa"),
        ),
        out_specs=(P(("row", "ha"), "wa"), P("wa", "ha"), P("wa", "ha"), P("ha", "wa")),
        check_vma=False,
    )
```

```python
import functools

import jax
import jax.numpy as jnp
from jax import lax
from jax.experimental import pallas as pl
from jax.experimental.pallas import tpu as pltpu
from jax.sharding import PartitionSpec as P

BF16 = jnp.bfloat16
F32 = jnp.float32
NT = (((1,), (1,)), ((), ()))
TN = (((0,), (0,)), ((), ()))
LANES = 128
CHUNKS = 4
TILE = 256
CUTS = 4
MIB = 1024 * 1024
IN_VMEM = pl.BlockSpec(memory_space=pltpu.VMEM)
IN_HBM = pl.BlockSpec(memory_space=pl.ANY)


def shaped(rows, columns, dtype=BF16):
    return jax.ShapeDtypeStruct((rows, columns), dtype)


def joined(*blocks):
    return jnp.concatenate([block.astype(F32) for block in blocks], axis=0)


def pointwise(gate_sum, up_sum, dh_sum):
    sig = jax.nn.sigmoid(gate_sum)
    active = gate_sum * sig
    hidden = (active * up_sum).astype(BF16)
    d_up = (dh_sum * active).astype(BF16)
    d_gate = (dh_sum * up_sum * sig * (1.0 + gate_sum * (1.0 - sig))).astype(BF16)
    return (hidden, d_gate, d_up)


class Line:
    def __init__(self):
        self.token = ()

    def call(
        self,
        kernel,
        args,
        out_shape,
        in_specs=None,
        out_specs=None,
        scratch=(),
        aliases=None,
        limit=4,
    ):
        count, outs, tokens = len(args), len(out_shape), len(self.token)

        def body(*refs):
            rest = refs[count + tokens :]
            rest[outs][...] = jnp.zeros_like(rest[outs])
            kernel(*refs[:count], *rest[:outs], *rest[outs + 1 :])

        *results, token = pl.pallas_call(
            body,
            in_specs=(in_specs or [IN_VMEM] * count) + [IN_VMEM] * tokens,
            out_specs=(out_specs or [IN_VMEM] * outs) + [IN_VMEM],
            out_shape=[*out_shape, shaped(8, LANES, F32)],
            scratch_shapes=list(scratch),
            input_output_aliases=aliases or {},
            cost_estimate=pl.CostEstimate(flops=1, bytes_accessed=1, transcendentals=0),
            compiler_params=pltpu.CompilerParams(vmem_limit_bytes=limit * MIB),
            name=getattr(kernel, "func", kernel).__name__,
        )(*args, *self.token)
        self.token = (token,)
        return results


def copy_rows(sems, source, target, begin=0):
    rows = target.shape[0] // CUTS
    copies = []
    for cut in range(CUTS):
        there, here = pl.ds(begin + cut * rows, rows), pl.ds(cut * rows, rows)
        copies.append(pltpu.make_async_copy(source.at[there], target.at[here], sems.at[cut]))
        copies[-1].start()
    return copies


def load_kernel(gate_ref, up_ref, gate_out, up_out, sems):
    copies = copy_rows(sems.at[0], gate_ref, gate_out)
    copies += copy_rows(sems.at[1], up_ref, up_out)
    for copy in copies:
        copy.wait()


def load(line, *weights):
    return line.call(
        load_kernel,
        weights,
        [pltpu.VMEM(weight.shape, BF16) for weight in weights],
        in_specs=[IN_HBM] * len(weights),
        scratch=[pltpu.SemaphoreType.DMA((len(weights), CUTS))],
        limit=30,
    )


def order_kernel(*refs):
    *piece_refs, out_ref = refs
    pieces = [ref[...].astype(F32) for ref in piece_refs]
    rows = pieces[0].shape[0] // 2
    wa = lax.axis_index("wa")
    slots = []
    for slot in range(len(pieces)):
        at = wa ^ slot
        piece = pieces[0]
        for other in range(1, len(pieces)):
            piece = jnp.where(at == other, pieces[other], piece)
        slots.append(piece)
    out_ref[...] = joined(
        *(slot[:rows] for slot in slots), *(slot[rows:] for slot in slots)
    ).astype(BF16)


def order_rows(line, pieces):
    rows, width = pieces[0].shape
    return line.call(order_kernel, pieces, [shaped(4 * rows, width)])[0]


def forward_kernel(begin, near, far, xy_ref, gate_ref, up_ref, down_ref, keep_ref, send_ref):
    there = pl.ds(begin, keep_ref.shape[1])
    group = xy_ref.shape[0] // 2
    rows = group // 4
    x, y = xy_ref[:group], xy_ref[group:]
    gate = jnp.dot(x, gate_ref[:, there], preferred_element_type=F32)
    up = jnp.dot(x, up_ref[:, there], preferred_element_type=F32)
    dh = lax.dot_general(y, down_ref[there], NT, preferred_element_type=F32)

    def slots(*which):
        cuts = [slice(slot * rows, (slot + 1) * rows) for slot in which]
        return joined(*(part[cut] for cut in cuts for part in (gate, up, dh)))

    keep_ref[...] = slots(0, far)
    send_ref[...] = slots(near, near ^ far).astype(BF16)


def forward(line, begin, columns, axes, xy, gate, up, down):
    rows = 6 * (xy.shape[0] // 8)
    return line.call(
        functools.partial(forward_kernel, begin, *axes),
        (xy, gate, up, down),
        [shaped(rows, columns, F32), shaped(rows, columns)],
    )


def halve_kernel(keep_ref, received_ref, own_ref, send_ref):
    total = keep_ref[...] + received_ref[...].astype(F32)
    half = own_ref.shape[0]
    own_ref[...] = total[:half]
    send_ref[...] = total[half:].astype(BF16)


def halve(line, keep, received):
    shape = (keep.shape[0] // 2, keep.shape[1])
    return line.call(halve_kernel, (keep, received), [shaped(*shape, F32), shaped(*shape)])


def middle_kernel(own_ref, received_ref, out_ref):
    total = own_ref[...] + received_ref[...].astype(F32)
    rows = total.shape[0] // 3
    hidden, d_gate, d_up = pointwise(total[:rows], total[rows : 2 * rows], total[2 * rows :])
    out_ref[...] = joined(d_gate, d_up, hidden).astype(BF16)


def middle(line, own, received):
    return line.call(middle_kernel, (own, received), [shaped(*own.shape)])[0]


def join_kernel(first_ref, second_ref, out_ref):
    out_ref[...] = joined(first_ref[...], second_ref[...]).astype(BF16)


def join(line, first, second):
    rows = first.shape[0] + second.shape[0]
    return line.call(join_kernel, (first, second), [shaped(rows, first.shape[1])])[0]


def stack_kernel(axes, *refs):
    out_ref = refs[-1]
    begin = 0
    for at, (near, far) in enumerate(axes):
        mine, other = refs[2 * at][...].astype(F32), refs[2 * at + 1][...].astype(F32)
        columns = mine.shape[1]
        half, rows = mine.shape[0] // 2, mine.shape[0] // 6
        slots = {0: mine[:half], near: mine[half:]}
        slots |= {far: other[:half], near ^ far: other[half:]}
        cuts = [slots[slot][k * rows : (k + 1) * rows] for k in range(3) for slot in range(4)]
        out_ref[:, begin : begin + columns] = joined(*cuts).astype(BF16)
        begin += columns
    if begin < out_ref.shape[1]:
        out_ref[:, begin:] = jnp.zeros((out_ref.shape[0], out_ref.shape[1] - begin), BF16)


def stack(line, axes, blocks, columns):
    rows = 2 * blocks[0][0].shape[0]
    return line.call(
        functools.partial(stack_kernel, axes),
        [block for pair in blocks for block in pair],
        [shaped(rows, columns)],
    )[0]


def input_grad_kernel(begin, mine_ref, gate_ref, up_ref, grad_ref):
    grad_ref[...] = input_grad_part(begin, mine_ref, gate_ref, up_ref, 0, grad_ref.shape[1])


def input_grad_part(begin, mine_ref, gate_ref, up_ref, start, size):
    group = mine_ref.shape[0] // 3
    columns = min(mine_ref.shape[1], gate_ref.shape[1] - begin)
    here, there, used = pl.ds(start, size), pl.ds(begin, columns), pl.ds(0, columns)
    return lax.dot_general(
        mine_ref[:group, used], gate_ref[here, there], NT, preferred_element_type=F32
    ) + lax.dot_general(
        mine_ref[group : 2 * group, used], up_ref[here, there], NT, preferred_element_type=F32
    )


def input_grad(line, begin, mine, gate, up):
    return line.call(
        functools.partial(input_grad_kernel, begin),
        (mine, gate, up),
        [shaped(mine.shape[0] // 3, gate.shape[0], F32)],
    )[0]


def factors_kernel(mine_ref, other_ref, xt_ref, y_all_ref):
    group = mine_ref.shape[0] // 2
    first = lax.axis_index("row") == 0
    x, y = mine_ref[:group], mine_ref[group:]
    x_other, y_other = other_ref[:group], other_ref[group:]
    y_all_ref[:group] = jnp.where(first, y, y_other)
    y_all_ref[group:] = jnp.where(first, y_other, y)
    x_all = jnp.concatenate([jnp.where(first, x, x_other), jnp.where(first, x_other, x)], axis=0)
    xt_ref[...] = x_all.T


def factors(line, xy, other):
    rows, width = xy.shape
    return line.call(factors_kernel, (xy, other), [shaped(width, rows), shaped(rows, width)])


class Writer:
    def __init__(self, begin, xt_ref, y_ref, mine_ref, other_ref, outs, scratch):
        self.begin, self.xt_ref, self.y_ref, self.outs = begin, xt_ref, y_ref, outs
        self.both, self.gate, self.up, self.down, self.sems = scratch
        self.mine_ref, self.other_ref = mine_ref, other_ref
        columns = min(mine_ref.shape[1], outs[0].shape[1] - begin)
        self.tiles = [(at, min(TILE, columns - at)) for at in range(0, columns, TILE)]
        self.copies = []

    def send(self, at, source, target):
        step = len(self.copies) // 3
        self.copies.append(pltpu.make_async_copy(source, target, self.sems.at[at, step]))
        self.copies[-1].start()

    def tile(self, start, size):
        group = self.y_ref.shape[0] // 2
        first = lax.axis_index("row") == 0
        here, there = pl.ds(start, size), pl.ds(self.begin + start, size)
        for at in range(3):
            cut = slice(at * group, (at + 1) * group)
            mine, other = self.mine_ref[cut, here], self.other_ref[cut, here]
            self.both[at, :group, here] = jnp.where(first, mine, other)
            self.both[at, group:, here] = jnp.where(first, other, mine)
        for at, grad in enumerate((self.gate, self.up)):
            grad[:, here] = jnp.dot(
                self.xt_ref[...], self.both[at, :, here], preferred_element_type=F32
            ).astype(BF16)
            self.send(at, grad.at[:, here], self.outs[at].at[:, there])
        self.down[here, :] = lax.dot_general(
            self.both[2, :, here], self.y_ref[...], TN, preferred_element_type=F32
        ).astype(BF16)
        self.send(2, self.down.at[here], self.outs[2].at[there])

    def wait(self):
        for copy in self.copies:
            copy.wait()


def first_grads_kernel(begins, *refs):
    xt_ref, y_ref, mine_ref, other_ref, start_ref, last_ref, gate_ref, up_ref, *refs = refs
    *outs, grad_ref = refs[:4]
    writer = Writer(begins[0], xt_ref, y_ref, mine_ref, other_ref, outs, refs[4:])
    width = grad_ref.shape[1]
    pieces = [(at, min(TILE, width - at)) for at in range(0, width, TILE)]
    for step in range(max(len(pieces), len(writer.tiles))):
        if step < len(writer.tiles):
            writer.tile(*writer.tiles[step])
        if step < len(pieces):
            here = pl.ds(*pieces[step])
            grad_ref[:, here] = start_ref[:, here] + input_grad_part(
                begins[1], last_ref, gate_ref, up_ref, *pieces[step]
            )
    writer.wait()


def grad_shapes(width, hidden_width):
    return [(width, hidden_width), (width, hidden_width), (hidden_width, width)]


def writer_scratch(width, rows, columns):
    return [
        pltpu.VMEM((3, rows, columns), BF16),
        *(pltpu.VMEM(shape, BF16) for shape in grad_shapes(width, columns)),
        pltpu.SemaphoreType.DMA((3, pl.cdiv(columns, TILE))),
    ]


def first_grads(line, begins, xt, y, mine, other, start, last, gate_weight, up_weight):
    width, hidden_width = gate_weight.shape
    shapes = [shaped(*shape) for shape in grad_shapes(width, hidden_width)]
    return line.call(
        functools.partial(first_grads_kernel, begins),
        (xt, y, mine, other, start, last, gate_weight, up_weight),
        shapes + [shaped(*start.shape, F32)],
        out_specs=[IN_HBM] * 3 + [IN_VMEM],
        scratch=writer_scratch(width, y.shape[0], mine.shape[1]),
        limit=24,
    )


def weight_grad_kernel(begin, xt_ref, y_ref, mine_ref, other_ref, *refs):
    writer = Writer(begin, xt_ref, y_ref, mine_ref, other_ref, refs[3:6], refs[6:])
    for tile in writer.tiles:
        writer.tile(*tile)
    writer.wait()


def weight_grad(line, begin, xt, y, mine, other, grads):
    return line.call(
        functools.partial(weight_grad_kernel, begin),
        (xt, y, mine, other, *grads),
        [shaped(*grad.shape) for grad in grads],
        in_specs=[IN_VMEM] * 4 + [IN_HBM] * 3,
        out_specs=[IN_HBM] * 3,
        scratch=writer_scratch(xt.shape[0], y.shape[0], mine.shape[1]),
        aliases={4 + at: at for at in range(3)},
        limit=24,
    )


def last_kernel(grad_ref, *out_refs):
    grad = grad_ref[...]
    rows = out_refs[0].shape[0]
    cuts = [grad[slot * rows : (slot + 1) * rows] for slot in range(len(out_refs))]
    wa = lax.axis_index("wa")
    for step, out_ref in enumerate(out_refs):
        at = wa ^ step
        piece = cuts[0]
        for slot in range(1, len(cuts)):
            piece = jnp.where(at == slot, cuts[slot], piece)
        out_ref[...] = piece.astype(out_ref.dtype)


def last_pieces(line, parts, grad):
    shape = (grad.shape[0] // parts, grad.shape[1])
    return line.call(
        last_kernel, (grad,), [shaped(*shape, F32)] + [shaped(*shape)] * (parts - 1)
    )


def total_kernel(own_ref, *refs):
    total = own_ref[...]
    for ref in refs[:-1]:
        total = total + ref[...].astype(F32)
    refs[-1][...] = total.astype(BF16)


def total(line, own, received):
    return line.call(total_kernel, (own, *received), [shaped(*own.shape)])[0]


def swap(value, axis, size, step):
    return lax.ppermute(value, axis, [(at, at ^ step) for at in range(size)])


def fast_body(n_wa, n_ha, n_row, tokens, cotangent, gate_weight, up_weight, down_weight):
    hidden_width = gate_weight.shape[1]
    tiles = hidden_width // LANES
    ends = [-(-tiles * (at + 1) // CHUNKS) * LANES for at in range(CHUNKS)]
    chunks = [(begin, end - begin) for begin, end in zip([0] + ends, ends)]
    axes = [((1, 2), (2, 1))[at % 2] for at in range(CHUNKS)]
    line = Line()

    both = jnp.concatenate([tokens, cotangent], axis=0)
    pieces = [both] + [swap(both, "ha", n_ha, step) for step in range(1, n_ha)]
    gate, up = load(Line(), gate_weight, up_weight)
    xy = order_rows(line, pieces)
    xy_other = swap(xy, "row", n_row, 1)

    kept, got = [], []
    for at, ((begin, columns), axis) in enumerate(zip(chunks, axes)):
        keep, send = forward(line, begin, columns, axis, xy, gate, up, down_weight)
        kept.append(keep)
        got.append(swap(send, "wa", n_wa, axis[0]))
    for at, (_, far) in enumerate(axes):
        kept[at], send = halve(line, kept[at], got[at])
        got[at] = swap(send, "wa", n_wa, far)
    order = [1, 0, 3, 2]
    for at in order:
        kept[at] = middle(line, kept[at], got[at])
        got[at] = swap(kept[at], "wa", n_wa, axes[at][0])
    for at in [1, 0, 3, 2]:
        far = axes[at][1]
        kept[at] = join(line, kept[at], got[at])
        got[at] = swap(kept[at], "wa", n_wa, far)

    xt, y_all = factors(line, xy, xy_other)
    mine, other = [], []
    widths = [sum(c for _, c in chunks[at : at + 2]) for at in range(0, CHUNKS, 2)]
    widest = max(widths)
    begins = [chunks[at][0] for at in range(0, CHUNKS, 2)]
    for at in range(0, CHUNKS, 2):
        pair = slice(at, at + 2)
        mine.append(stack(line, axes[pair], list(zip(kept, got))[pair], widest))
        other.append(swap(mine[-1], "row", n_row, 1))
        if at == 0:
            grad = input_grad(line, begins[0], mine[0], gate, up)
    *grads, grad = first_grads(line, begins, xt, y_all, mine[0], other[0], grad, mine[1], gate, up)
    own, *sends = last_pieces(line, n_ha, grad)
    received = [swap(sent, "ha", n_ha, k + 1) for k, sent in enumerate(sends)]
    grads = weight_grad(line, begins[1], xt, y_all, mine[1], other[1], grads)
    return (total(line, own, received), *grads)


def plain_body(tokens, cotangent, gate_weight, up_weight, down_weight):
    hidden_width = gate_weight.shape[1]
    x = lax.all_gather(tokens, "ha", axis=0, tiled=True)
    y = lax.all_gather(cotangent, "ha", axis=0, tiled=True)
    gate_part = jnp.dot(x, gate_weight, preferred_element_type=F32)
    up_part = jnp.dot(x, up_weight, preferred_element_type=F32)
    dh_part = lax.dot_general(y, down_weight, NT, preferred_element_type=F32)
    summed = lax.psum(jnp.concatenate([gate_part, up_part, dh_part], axis=1), "wa")
    hidden, d_gate, d_up = pointwise(
        summed[:, :hidden_width],
        summed[:, hidden_width : 2 * hidden_width],
        summed[:, 2 * hidden_width :],
    )
    partial = lax.dot_general(
        d_gate, gate_weight, NT, preferred_element_type=F32
    ) + lax.dot_general(d_up, up_weight, NT, preferred_element_type=F32)
    grad_tokens = lax.psum_scatter(partial, "ha", scatter_dimension=0, tiled=True)
    grads = (
        lax.dot_general(x, d_gate, TN, preferred_element_type=F32),
        lax.dot_general(x, d_up, TN, preferred_element_type=F32),
        lax.dot_general(hidden, y, TN, preferred_element_type=F32),
    )
    return (
        grad_tokens.astype(BF16),
        *(lax.psum(g.astype(BF16), "row").astype(BF16) for g in grads),
    )


def solution(mesh):
    n_wa, n_ha, n_row = (mesh.shape[name] for name in ("wa", "ha", "row"))

    def body(tokens, cotangent, gate_weight, up_weight, down_weight):
        width, hidden_width = gate_weight.shape
        fits = (
            n_wa == n_ha == 4
            and n_row == 2
            and width % LANES == 0
            and hidden_width % LANES == 0
            and hidden_width >= LANES * CHUNKS
            and width % (16 * CUTS) == 0
            and (tokens.shape[0] * n_ha) % 16 == 0
        )
        if fits:
            return fast_body(
                n_wa, n_ha, n_row, tokens, cotangent, gate_weight, up_weight, down_weight
            )
        return plain_body(tokens, cotangent, gate_weight, up_weight, down_weight)

    return jax.shard_map(
        body,
        mesh=mesh,
        in_specs=(
            P(("row", "ha"), "wa"),
            P(("row", "ha"), "wa"),
            P("wa", "ha"),
            P("wa", "ha"),
            P("ha", "wa"),
        ),
        out_specs=(P(("row", "ha"), "wa"), P("wa", "ha"), P("wa", "ha"), P("ha", "wa")),
        check_vma=False,
    )
```

```python
import functools

import jax
import jax.numpy as jnp
from jax import lax
from jax.experimental import pallas as pl
from jax.experimental.pallas import tpu as pltpu
from jax.sharding import PartitionSpec as P

BF16 = jnp.bfloat16
F32 = jnp.float32
NT = (((1,), (1,)), ((), ()))
TN = (((0,), (0,)), ((), ()))
LANES = 128
CHUNKS = 4
TILE = 256
CUTS = 4
MIB = 1024 * 1024
IN_VMEM = pl.BlockSpec(memory_space=pltpu.VMEM)
IN_HBM = pl.BlockSpec(memory_space=pl.ANY)


def shaped(rows, columns, dtype=BF16):
    return jax.ShapeDtypeStruct((rows, columns), dtype)


def joined(*blocks):
    return jnp.concatenate([block.astype(F32) for block in blocks], axis=0)


def pointwise(gate_sum, up_sum, dh_sum):
    sig = jax.nn.sigmoid(gate_sum)
    active = gate_sum * sig
    hidden = (active * up_sum).astype(BF16)
    d_up = (dh_sum * active).astype(BF16)
    d_gate = (dh_sum * up_sum * sig * (1.0 + gate_sum * (1.0 - sig))).astype(BF16)
    return (hidden, d_gate, d_up)


class Line:
    def __init__(self):
        self.token = ()

    def call(
        self,
        kernel,
        args,
        out_shape,
        in_specs=None,
        out_specs=None,
        scratch=(),
        aliases=None,
        limit=4,
    ):
        count, outs, tokens = len(args), len(out_shape), len(self.token)

        def body(*refs):
            rest = refs[count + tokens :]
            rest[outs][...] = jnp.zeros_like(rest[outs])
            kernel(*refs[:count], *rest[:outs], *rest[outs + 1 :])

        *results, token = pl.pallas_call(
            body,
            in_specs=(in_specs or [IN_VMEM] * count) + [IN_VMEM] * tokens,
            out_specs=(out_specs or [IN_VMEM] * outs) + [IN_VMEM],
            out_shape=[*out_shape, shaped(8, LANES, F32)],
            scratch_shapes=list(scratch),
            input_output_aliases=aliases or {},
            cost_estimate=pl.CostEstimate(flops=1, bytes_accessed=1, transcendentals=0),
            compiler_params=pltpu.CompilerParams(vmem_limit_bytes=limit * MIB),
            name=getattr(kernel, "func", kernel).__name__,
        )(*args, *self.token)
        self.token = (token,)
        return results


def copy_rows(sems, source, target, begin=0):
    rows = target.shape[0] // CUTS
    copies = []
    for cut in range(CUTS):
        there, here = pl.ds(begin + cut * rows, rows), pl.ds(cut * rows, rows)
        copies.append(pltpu.make_async_copy(source.at[there], target.at[here], sems.at[cut]))
        copies[-1].start()
    return copies


def load_kernel(gate_ref, up_ref, gate_out, up_out, sems):
    copies = copy_rows(sems.at[0], gate_ref, gate_out)
    copies += copy_rows(sems.at[1], up_ref, up_out)
    for copy in copies:
        copy.wait()


def load(line, *weights):
    return line.call(
        load_kernel,
        weights,
        [pltpu.VMEM(weight.shape, BF16) for weight in weights],
        in_specs=[IN_HBM] * len(weights),
        scratch=[pltpu.SemaphoreType.DMA((len(weights), CUTS))],
        limit=30,
    )


def order_kernel(*refs):
    *piece_refs, out_ref = refs
    pieces = [ref[...].astype(F32) for ref in piece_refs]
    rows = pieces[0].shape[0] // 2
    wa = lax.axis_index("wa")
    slots = []
    for slot in range(len(pieces)):
        at = wa ^ slot
        piece = pieces[0]
        for other in range(1, len(pieces)):
            piece = jnp.where(at == other, pieces[other], piece)
        slots.append(piece)
    out_ref[...] = joined(
        *(slot[:rows] for slot in slots), *(slot[rows:] for slot in slots)
    ).astype(BF16)


def order_rows(line, pieces):
    rows, width = pieces[0].shape
    return line.call(order_kernel, pieces, [shaped(4 * rows, width)])[0]


def forward_kernel(begin, near, far, xy_ref, gate_ref, up_ref, down_ref, keep_ref, send_ref):
    there = pl.ds(begin, keep_ref.shape[1])
    group = xy_ref.shape[0] // 2
    rows = group // 4
    x, y = xy_ref[:group], xy_ref[group:]
    gate = jnp.dot(x, gate_ref[:, there], preferred_element_type=F32)
    up = jnp.dot(x, up_ref[:, there], preferred_element_type=F32)
    dh = lax.dot_general(y, down_ref[there], NT, preferred_element_type=F32)

    def slots(*which):
        cuts = [slice(slot * rows, (slot + 1) * rows) for slot in which]
        return joined(*(part[cut] for cut in cuts for part in (gate, up, dh)))

    keep_ref[...] = slots(0, far)
    send_ref[...] = slots(near, near ^ far).astype(BF16)


def forward(line, begin, columns, axes, xy, gate, up, down):
    rows = 6 * (xy.shape[0] // 8)
    return line.call(
        functools.partial(forward_kernel, begin, *axes),
        (xy, gate, up, down),
        [shaped(rows, columns, F32), shaped(rows, columns)],
    )


def halve_kernel(keep_ref, received_ref, own_ref, send_ref):
    total = keep_ref[...] + received_ref[...].astype(F32)
    half = own_ref.shape[0]
    own_ref[...] = total[:half]
    send_ref[...] = total[half:].astype(BF16)


def halve(line, keep, received):
    shape = (keep.shape[0] // 2, keep.shape[1])
    return line.call(halve_kernel, (keep, received), [shaped(*shape, F32), shaped(*shape)])


def middle_kernel(own_ref, received_ref, out_ref):
    total = own_ref[...] + received_ref[...].astype(F32)
    rows = total.shape[0] // 3
    hidden, d_gate, d_up = pointwise(total[:rows], total[rows : 2 * rows], total[2 * rows :])
    out_ref[...] = joined(d_gate, d_up, hidden).astype(BF16)


def middle(line, own, received):
    return line.call(middle_kernel, (own, received), [shaped(*own.shape)])[0]


def join_kernel(first_ref, second_ref, out_ref):
    out_ref[...] = joined(first_ref[...], second_ref[...]).astype(BF16)


def join(line, first, second):
    rows = first.shape[0] + second.shape[0]
    return line.call(join_kernel, (first, second), [shaped(rows, first.shape[1])])[0]


def stack_kernel(axes, *refs):
    out_ref = refs[-1]
    begin = 0
    for at, (near, far) in enumerate(axes):
        mine, other = refs[2 * at][...].astype(F32), refs[2 * at + 1][...].astype(F32)
        columns = mine.shape[1]
        half, rows = mine.shape[0] // 2, mine.shape[0] // 6
        slots = {0: mine[:half], near: mine[half:]}
        slots |= {far: other[:half], near ^ far: other[half:]}
        cuts = [slots[slot][k * rows : (k + 1) * rows] for k in range(3) for slot in range(4)]
        out_ref[:, begin : begin + columns] = joined(*cuts).astype(BF16)
        begin += columns
    if begin < out_ref.shape[1]:
        out_ref[:, begin:] = jnp.zeros((out_ref.shape[0], out_ref.shape[1] - begin), BF16)


def stack(line, axes, blocks, columns):
    rows = 2 * blocks[0][0].shape[0]
    return line.call(
        functools.partial(stack_kernel, axes),
        [block for pair in blocks for block in pair],
        [shaped(rows, columns)],
    )[0]


def input_grad_kernel(begin, mine_ref, gate_ref, up_ref, grad_ref):
    grad_ref[...] = input_grad_part(begin, mine_ref, gate_ref, up_ref, 0, grad_ref.shape[1])


def input_grad_part(begin, mine_ref, gate_ref, up_ref, start, size):
    group = mine_ref.shape[0] // 3
    columns = min(mine_ref.shape[1], gate_ref.shape[1] - begin)
    here, there, used = pl.ds(start, size), pl.ds(begin, columns), pl.ds(0, columns)
    return lax.dot_general(
        mine_ref[:group, used], gate_ref[here, there], NT, preferred_element_type=F32
    ) + lax.dot_general(
        mine_ref[group : 2 * group, used], up_ref[here, there], NT, preferred_element_type=F32
    )


def input_grad(line, begin, mine, gate, up):
    return line.call(
        functools.partial(input_grad_kernel, begin),
        (mine, gate, up),
        [shaped(mine.shape[0] // 3, gate.shape[0], F32)],
    )[0]


def factors_kernel(mine_ref, other_ref, xt_ref, y_all_ref):
    group = mine_ref.shape[0] // 2
    first = lax.axis_index("row") == 0
    x, y = mine_ref[:group], mine_ref[group:]
    x_other, y_other = other_ref[:group], other_ref[group:]
    y_all_ref[:group] = jnp.where(first, y, y_other)
    y_all_ref[group:] = jnp.where(first, y_other, y)
    x_all = jnp.concatenate([jnp.where(first, x, x_other), jnp.where(first, x_other, x)], axis=0)
    xt_ref[...] = x_all.T


def factors(line, xy, other):
    rows, width = xy.shape
    return line.call(factors_kernel, (xy, other), [shaped(width, rows), shaped(rows, width)])


class Writer:
    def __init__(self, begin, xt_ref, y_ref, mine_ref, other_ref, outs, scratch):
        self.begin, self.xt_ref, self.y_ref, self.outs = begin, xt_ref, y_ref, outs
        self.both, self.gate, self.up, self.down, self.sems = scratch
        self.mine_ref, self.other_ref = mine_ref, other_ref
        columns = min(mine_ref.shape[1], outs[0].shape[1] - begin)
        self.tiles = [(at, min(TILE, columns - at)) for at in range(0, columns, TILE)]
        self.copies = []

    def send(self, at, source, target):
        step = len(self.copies) // 3
        self.copies.append(pltpu.make_async_copy(source, target, self.sems.at[at, step]))
        self.copies[-1].start()

    def tile(self, start, size):
        group = self.y_ref.shape[0] // 2
        first = lax.axis_index("row") == 0
        here, there = pl.ds(start, size), pl.ds(self.begin + start, size)
        for at in range(3):
            cut = slice(at * group, (at + 1) * group)
            mine, other = self.mine_ref[cut, here], self.other_ref[cut, here]
            self.both[at, :group, here] = jnp.where(first, mine, other)
            self.both[at, group:, here] = jnp.where(first, other, mine)
        width = self.y_ref.shape[1]
        blocks = [pl.ds(at, min(TILE, width - at)) for at in range(0, width, TILE)]
        for at, grad in enumerate((self.gate, self.up)):
            rows = self.both[at, :, here]
            for block in blocks:
                grad[block, here] = jnp.dot(
                    self.xt_ref[block], rows, preferred_element_type=F32
                ).astype(BF16)
            self.send(at, grad.at[:, here], self.outs[at].at[:, there])
        hidden = self.both[2, :, here].T
        for block in blocks:
            self.down[here, block] = jnp.dot(
                hidden, self.y_ref[:, block], preferred_element_type=F32
            ).astype(BF16)
        self.send(2, self.down.at[here], self.outs[2].at[there])

    def wait(self):
        for copy in self.copies:
            copy.wait()


def first_grads_kernel(begins, *refs):
    xt_ref, y_ref, mine_ref, other_ref, start_ref, last_ref, gate_ref, up_ref, *refs = refs
    *outs, grad_ref = refs[:4]
    writer = Writer(begins[0], xt_ref, y_ref, mine_ref, other_ref, outs, refs[4:])
    width = grad_ref.shape[1]
    pieces = [(at, min(TILE, width - at)) for at in range(0, width, TILE)]
    for step in range(max(len(pieces), len(writer.tiles))):
        if step < len(writer.tiles):
            writer.tile(*writer.tiles[step])
        if step < len(pieces):
            here = pl.ds(*pieces[step])
            grad_ref[:, here] = start_ref[:, here] + input_grad_part(
                begins[1], last_ref, gate_ref, up_ref, *pieces[step]
            )
    writer.wait()


def grad_shapes(width, hidden_width):
    return [(width, hidden_width), (width, hidden_width), (hidden_width, width)]


def writer_scratch(width, rows, columns):
    return [
        pltpu.VMEM((3, rows, columns), BF16),
        *(pltpu.VMEM(shape, BF16) for shape in grad_shapes(width, columns)),
        pltpu.SemaphoreType.DMA((3, pl.cdiv(columns, TILE))),
    ]


def first_grads(line, begins, xt, y, mine, other, start, last, gate_weight, up_weight):
    width, hidden_width = gate_weight.shape
    shapes = [shaped(*shape) for shape in grad_shapes(width, hidden_width)]
    return line.call(
        functools.partial(first_grads_kernel, begins),
        (xt, y, mine, other, start, last, gate_weight, up_weight),
        shapes + [shaped(*start.shape, F32)],
        out_specs=[IN_HBM] * 3 + [IN_VMEM],
        scratch=writer_scratch(width, y.shape[0], mine.shape[1]),
        limit=24,
    )


def weight_grad_kernel(begin, xt_ref, y_ref, mine_ref, other_ref, *refs):
    writer = Writer(begin, xt_ref, y_ref, mine_ref, other_ref, refs[3:6], refs[6:])
    for tile in writer.tiles:
        writer.tile(*tile)
    writer.wait()


def weight_grad(line, begin, xt, y, mine, other, grads):
    return line.call(
        functools.partial(weight_grad_kernel, begin),
        (xt, y, mine, other, *grads),
        [shaped(*grad.shape) for grad in grads],
        in_specs=[IN_VMEM] * 4 + [IN_HBM] * 3,
        out_specs=[IN_HBM] * 3,
        scratch=writer_scratch(xt.shape[0], y.shape[0], mine.shape[1]),
        aliases={4 + at: at for at in range(3)},
        limit=24,
    )


def last_kernel(grad_ref, *out_refs):
    grad = grad_ref[...]
    rows = out_refs[0].shape[0]
    cuts = [grad[slot * rows : (slot + 1) * rows] for slot in range(len(out_refs))]
    wa = lax.axis_index("wa")
    for step, out_ref in enumerate(out_refs):
        at = wa ^ step
        piece = cuts[0]
        for slot in range(1, len(cuts)):
            piece = jnp.where(at == slot, cuts[slot], piece)
        out_ref[...] = piece.astype(out_ref.dtype)


def last_pieces(line, parts, grad):
    shape = (grad.shape[0] // parts, grad.shape[1])
    return line.call(
        last_kernel, (grad,), [shaped(*shape, F32)] + [shaped(*shape)] * (parts - 1)
    )


def total_kernel(own_ref, *refs):
    total = own_ref[...]
    for ref in refs[:-1]:
        total = total + ref[...].astype(F32)
    refs[-1][...] = total.astype(BF16)


def total(line, own, received):
    return line.call(total_kernel, (own, *received), [shaped(*own.shape)])[0]


def swap(value, axis, size, step):
    return lax.ppermute(value, axis, [(at, at ^ step) for at in range(size)])


def fast_body(n_wa, n_ha, n_row, tokens, cotangent, gate_weight, up_weight, down_weight):
    hidden_width = gate_weight.shape[1]
    tiles = hidden_width // LANES
    ends = [-(-tiles * (at + 1) // CHUNKS) * LANES for at in range(CHUNKS)]
    chunks = [(begin, end - begin) for begin, end in zip([0] + ends, ends)]
    axes = [((1, 2), (2, 1))[at % 2] for at in range(CHUNKS)]
    line = Line()

    both = jnp.concatenate([tokens, cotangent], axis=0)
    pieces = [both] + [swap(both, "ha", n_ha, step) for step in range(1, n_ha)]
    gate, up = load(Line(), gate_weight, up_weight)
    xy = order_rows(line, pieces)
    xy_other = swap(xy, "row", n_row, 1)

    kept, got = [], []
    for at, ((begin, columns), axis) in enumerate(zip(chunks, axes)):
        keep, send = forward(line, begin, columns, axis, xy, gate, up, down_weight)
        kept.append(keep)
        got.append(swap(send, "wa", n_wa, axis[0]))
    for at, (_, far) in enumerate(axes):
        kept[at], send = halve(line, kept[at], got[at])
        got[at] = swap(send, "wa", n_wa, far)
    order = [1, 0, 3, 2]
    for at in order:
        kept[at] = middle(line, kept[at], got[at])
        got[at] = swap(kept[at], "wa", n_wa, axes[at][0])
    for at in [1, 0, 3, 2]:
        far = axes[at][1]
        kept[at] = join(line, kept[at], got[at])
        got[at] = swap(kept[at], "wa", n_wa, far)

    xt, y_all = factors(line, xy, xy_other)
    mine, other = [], []
    widths = [sum(c for _, c in chunks[at : at + 2]) for at in range(0, CHUNKS, 2)]
    widest = max(widths)
    begins = [chunks[at][0] for at in range(0, CHUNKS, 2)]
    for at in range(0, CHUNKS, 2):
        pair = slice(at, at + 2)
        mine.append(stack(line, axes[pair], list(zip(kept, got))[pair], widest))
        other.append(swap(mine[-1], "row", n_row, 1))
        if at == 0:
            grad = input_grad(line, begins[0], mine[0], gate, up)
    *grads, grad = first_grads(line, begins, xt, y_all, mine[0], other[0], grad, mine[1], gate, up)
    own, *sends = last_pieces(line, n_ha, grad)
    received = [swap(sent, "ha", n_ha, k + 1) for k, sent in enumerate(sends)]
    grads = weight_grad(line, begins[1], xt, y_all, mine[1], other[1], grads)
    return (total(line, own, received), *grads)


def plain_body(tokens, cotangent, gate_weight, up_weight, down_weight):
    hidden_width = gate_weight.shape[1]
    x = lax.all_gather(tokens, "ha", axis=0, tiled=True)
    y = lax.all_gather(cotangent, "ha", axis=0, tiled=True)
    gate_part = jnp.dot(x, gate_weight, preferred_element_type=F32)
    up_part = jnp.dot(x, up_weight, preferred_element_type=F32)
    dh_part = lax.dot_general(y, down_weight, NT, preferred_element_type=F32)
    summed = lax.psum(jnp.concatenate([gate_part, up_part, dh_part], axis=1), "wa")
    hidden, d_gate, d_up = pointwise(
        summed[:, :hidden_width],
        summed[:, hidden_width : 2 * hidden_width],
        summed[:, 2 * hidden_width :],
    )
    partial = lax.dot_general(
        d_gate, gate_weight, NT, preferred_element_type=F32
    ) + lax.dot_general(d_up, up_weight, NT, preferred_element_type=F32)
    grad_tokens = lax.psum_scatter(partial, "ha", scatter_dimension=0, tiled=True)
    grads = (
        lax.dot_general(x, d_gate, TN, preferred_element_type=F32),
        lax.dot_general(x, d_up, TN, preferred_element_type=F32),
        lax.dot_general(hidden, y, TN, preferred_element_type=F32),
    )
    return (
        grad_tokens.astype(BF16),
        *(lax.psum(g.astype(BF16), "row").astype(BF16) for g in grads),
    )


def solution(mesh):
    n_wa, n_ha, n_row = (mesh.shape[name] for name in ("wa", "ha", "row"))

    def body(tokens, cotangent, gate_weight, up_weight, down_weight):
        width, hidden_width = gate_weight.shape
        fits = (
            n_wa == n_ha == 4
            and n_row == 2
            and width % LANES == 0
            and hidden_width % LANES == 0
            and hidden_width >= LANES * CHUNKS
            and width % (16 * CUTS) == 0
            and (tokens.shape[0] * n_ha) % 16 == 0
        )
        if fits:
            return fast_body(
                n_wa, n_ha, n_row, tokens, cotangent, gate_weight, up_weight, down_weight
            )
        return plain_body(tokens, cotangent, gate_weight, up_weight, down_weight)

    return jax.shard_map(
        body,
        mesh=mesh,
        in_specs=(
            P(("row", "ha"), "wa"),
            P(("row", "ha"), "wa"),
            P("wa", "ha"),
            P("wa", "ha"),
            P("ha", "wa"),
        ),
        out_specs=(P(("row", "ha"), "wa"), P("wa", "ha"), P("wa", "ha"), P("ha", "wa")),
        check_vma=False,
    )
```

```python
import functools

import jax
import jax.numpy as jnp
from jax import lax
from jax.experimental import pallas as pl
from jax.experimental.pallas import tpu as pltpu
from jax.sharding import PartitionSpec as P

BF16 = jnp.bfloat16
F32 = jnp.float32
NT = (((1,), (1,)), ((), ()))
TN = (((0,), (0,)), ((), ()))
LANES = 128
CHUNKS = 4
TILE = 256
CUTS = 4
MIB = 1024 * 1024
IN_VMEM = pl.BlockSpec(memory_space=pltpu.VMEM)
IN_HBM = pl.BlockSpec(memory_space=pl.ANY)


def shaped(rows, columns, dtype=BF16):
    return jax.ShapeDtypeStruct((rows, columns), dtype)


def joined(*blocks):
    return jnp.concatenate([block.astype(F32) for block in blocks], axis=0)


def pointwise(gate_sum, up_sum, dh_sum):
    sig = jax.nn.sigmoid(gate_sum)
    active = gate_sum * sig
    hidden = (active * up_sum).astype(BF16)
    d_up = (dh_sum * active).astype(BF16)
    d_gate = (dh_sum * up_sum * sig * (1.0 + gate_sum * (1.0 - sig))).astype(BF16)
    return (hidden, d_gate, d_up)


class Line:
    def __init__(self):
        self.token = ()

    def call(
        self,
        kernel,
        args,
        out_shape,
        in_specs=None,
        out_specs=None,
        scratch=(),
        aliases=None,
        limit=4,
    ):
        count, outs, tokens = len(args), len(out_shape), len(self.token)

        def body(*refs):
            rest = refs[count + tokens :]
            rest[outs][...] = jnp.zeros_like(rest[outs])
            kernel(*refs[:count], *rest[:outs], *rest[outs + 1 :])

        *results, token = pl.pallas_call(
            body,
            in_specs=(in_specs or [IN_VMEM] * count) + [IN_VMEM] * tokens,
            out_specs=(out_specs or [IN_VMEM] * outs) + [IN_VMEM],
            out_shape=[*out_shape, shaped(8, LANES, F32)],
            scratch_shapes=list(scratch),
            input_output_aliases=aliases or {},
            cost_estimate=pl.CostEstimate(flops=1, bytes_accessed=1, transcendentals=0),
            compiler_params=pltpu.CompilerParams(vmem_limit_bytes=limit * MIB),
            name=getattr(kernel, "func", kernel).__name__,
        )(*args, *self.token)
        self.token = (token,)
        return results


def copy_rows(sems, source, target, begin=0):
    rows = target.shape[0] // CUTS
    copies = []
    for cut in range(CUTS):
        there, here = pl.ds(begin + cut * rows, rows), pl.ds(cut * rows, rows)
        copies.append(pltpu.make_async_copy(source.at[there], target.at[here], sems.at[cut]))
        copies[-1].start()
    return copies


def load_kernel(gate_ref, up_ref, gate_out, up_out, sems):
    copies = copy_rows(sems.at[0], gate_ref, gate_out)
    copies += copy_rows(sems.at[1], up_ref, up_out)
    for copy in copies:
        copy.wait()


def load(line, *weights):
    return line.call(
        load_kernel,
        weights,
        [pltpu.VMEM(weight.shape, BF16) for weight in weights],
        in_specs=[IN_HBM] * len(weights),
        scratch=[pltpu.SemaphoreType.DMA((len(weights), CUTS))],
        limit=30,
    )


def order_kernel(*refs):
    *piece_refs, out_ref = refs
    pieces = [ref[...].astype(F32) for ref in piece_refs]
    rows = pieces[0].shape[0] // 2
    wa = lax.axis_index("wa")
    slots = []
    for slot in range(len(pieces)):
        at = wa ^ slot
        piece = pieces[0]
        for other in range(1, len(pieces)):
            piece = jnp.where(at == other, pieces[other], piece)
        slots.append(piece)
    out_ref[...] = joined(
        *(slot[:rows] for slot in slots), *(slot[rows:] for slot in slots)
    ).astype(BF16)


def order_rows(line, pieces):
    rows, width = pieces[0].shape
    return line.call(order_kernel, pieces, [shaped(4 * rows, width)])[0]


def forward_kernel(begin, near, far, xy_ref, gate_ref, up_ref, down_ref, keep_ref, send_ref):
    there = pl.ds(begin, keep_ref.shape[1])
    group = xy_ref.shape[0] // 2
    rows = group // 4
    x, y = xy_ref[:group], xy_ref[group:]
    gate = jnp.dot(x, gate_ref[:, there], preferred_element_type=F32)
    up = jnp.dot(x, up_ref[:, there], preferred_element_type=F32)
    dh = lax.dot_general(y, down_ref[there], NT, preferred_element_type=F32)

    def slots(*which):
        cuts = [slice(slot * rows, (slot + 1) * rows) for slot in which]
        return joined(*(part[cut] for cut in cuts for part in (gate, up, dh)))

    keep_ref[...] = slots(0, far)
    send_ref[...] = slots(near, near ^ far).astype(BF16)


def forward(line, begin, columns, axes, xy, gate, up, down):
    rows = 6 * (xy.shape[0] // 8)
    return line.call(
        functools.partial(forward_kernel, begin, *axes),
        (xy, gate, up, down),
        [shaped(rows, columns, F32), shaped(rows, columns)],
    )


def halve_kernel(keep_ref, received_ref, own_ref, send_ref):
    total = keep_ref[...] + received_ref[...].astype(F32)
    half = own_ref.shape[0]
    own_ref[...] = total[:half]
    send_ref[...] = total[half:].astype(BF16)


def halve(line, keep, received):
    shape = (keep.shape[0] // 2, keep.shape[1])
    return line.call(halve_kernel, (keep, received), [shaped(*shape, F32), shaped(*shape)])


def middle_kernel(own_ref, received_ref, out_ref):
    total = own_ref[...] + received_ref[...].astype(F32)
    rows = total.shape[0] // 3
    hidden, d_gate, d_up = pointwise(total[:rows], total[rows : 2 * rows], total[2 * rows :])
    out_ref[...] = joined(d_gate, d_up, hidden).astype(BF16)


def middle(line, own, received):
    return line.call(middle_kernel, (own, received), [shaped(*own.shape)])[0]


def join_kernel(first_ref, second_ref, out_ref):
    out_ref[...] = joined(first_ref[...], second_ref[...]).astype(BF16)


def join(line, first, second):
    rows = first.shape[0] + second.shape[0]
    return line.call(join_kernel, (first, second), [shaped(rows, first.shape[1])])[0]


def stack_kernel(axes, *refs):
    out_ref = refs[-1]
    begin = 0
    for at, (near, far) in enumerate(axes):
        mine, other = refs[2 * at][...].astype(F32), refs[2 * at + 1][...].astype(F32)
        columns = mine.shape[1]
        half, rows = mine.shape[0] // 2, mine.shape[0] // 6
        slots = {0: mine[:half], near: mine[half:]}
        slots |= {far: other[:half], near ^ far: other[half:]}
        cuts = [slots[slot][k * rows : (k + 1) * rows] for k in range(3) for slot in range(4)]
        out_ref[:, begin : begin + columns] = joined(*cuts).astype(BF16)
        begin += columns


def stack(line, axes, blocks):
    rows = 2 * blocks[0][0].shape[0]
    columns = sum(mine.shape[1] for mine, _ in blocks)
    return line.call(
        functools.partial(stack_kernel, axes),
        [block for pair in blocks for block in pair],
        [shaped(rows, columns)],
    )[0]


def input_grad_kernel(begin, stack_ref, gate_ref, up_ref, *refs):
    there = pl.ds(begin, stack_ref.shape[1])
    group = stack_ref.shape[0] // 3
    grad = lax.dot_general(
        stack_ref[:group], gate_ref[:, there], NT, preferred_element_type=F32
    ) + lax.dot_general(
        stack_ref[group : 2 * group], up_ref[:, there], NT, preferred_element_type=F32
    )
    refs[-1][...] = grad + refs[0][...] if len(refs) > 1 else grad


def input_grad(line, begin, stacked, gate_weight, up_weight, start):
    shape = (stacked.shape[0] // 3, gate_weight.shape[0])
    return line.call(
        functools.partial(input_grad_kernel, begin),
        (stacked, gate_weight, up_weight, *start),
        [shaped(*shape, F32)],
    )


def factors_kernel(mine_ref, other_ref, xt_ref, y_all_ref):
    group = mine_ref.shape[0] // 2
    first = lax.axis_index("row") == 0
    x, y = mine_ref[:group], mine_ref[group:]
    x_other, y_other = other_ref[:group], other_ref[group:]
    y_all_ref[:group] = jnp.where(first, y, y_other)
    y_all_ref[group:] = jnp.where(first, y_other, y)
    x_all = jnp.concatenate([jnp.where(first, x, x_other), jnp.where(first, x_other, x)], axis=0)
    xt_ref[...] = x_all.T


def factors(line, xy, other):
    rows, width = xy.shape
    return line.call(factors_kernel, (xy, other), [shaped(width, rows), shaped(rows, width)])


class Writer:
    def __init__(self, begin, xt_ref, y_ref, mine_ref, other_ref, outs, scratch):
        self.begin, self.xt_ref, self.y_ref, self.outs = begin, xt_ref, y_ref, outs
        self.both, self.gate, self.up, self.down, self.sems = scratch
        self.mine_ref, self.other_ref = mine_ref, other_ref
        columns = min(mine_ref.shape[1], outs[0].shape[1] - begin)
        self.tiles = [(at, min(TILE, columns - at)) for at in range(0, columns, TILE)]
        self.copies = []

    def send(self, at, source, target):
        step = len(self.copies) // 3
        self.copies.append(pltpu.make_async_copy(source, target, self.sems.at[at, step]))
        self.copies[-1].start()

    def tile(self, start, size):
        group = self.y_ref.shape[0] // 2
        first = lax.axis_index("row") == 0
        here, there = pl.ds(start, size), pl.ds(self.begin + start, size)
        for at in range(3):
            cut = slice(at * group, (at + 1) * group)
            mine, other = self.mine_ref[cut, here], self.other_ref[cut, here]
            self.both[at, :group, here] = jnp.where(first, mine, other)
            self.both[at, group:, here] = jnp.where(first, other, mine)
        width = self.y_ref.shape[1]
        blocks = [pl.ds(at, min(TILE, width - at)) for at in range(0, width, TILE)]
        for at, grad in enumerate((self.gate, self.up)):
            rows = self.both[at, :, here]
            for block in blocks:
                grad[block, here] = jnp.dot(
                    self.xt_ref[block], rows, preferred_element_type=F32
                ).astype(BF16)
            self.send(at, grad.at[:, here], self.outs[at].at[:, there])
        hidden = self.both[2, :, here].T
        for block in blocks:
            self.down[here, block] = jnp.dot(
                hidden, self.y_ref[:, block], preferred_element_type=F32
            ).astype(BF16)
        self.send(2, self.down.at[here], self.outs[2].at[there])

    def wait(self):
        for copy in self.copies:
            copy.wait()


def grad_shapes(width, hidden_width):
    return [(width, hidden_width), (width, hidden_width), (hidden_width, width)]


def writer_scratch(width, rows, columns):
    return [
        pltpu.VMEM((3, rows, columns), BF16),
        *(pltpu.VMEM(shape, BF16) for shape in grad_shapes(width, columns)),
        pltpu.SemaphoreType.DMA((3, pl.cdiv(columns, TILE))),
    ]


def weight_grad_kernel(begin, held, xt_ref, y_ref, mine_ref, other_ref, _, *refs):
    outs, scratch = refs[held : held + 3], refs[held + 3 :]
    writer = Writer(begin, xt_ref, y_ref, mine_ref, other_ref, outs, scratch)
    for tile in writer.tiles:
        writer.tile(*tile)
    writer.wait()


def weight_grad(line, begin, hidden_width, xt, y, mine, other, grads, after):
    shapes = grad_shapes(xt.shape[0], hidden_width)
    return line.call(
        functools.partial(weight_grad_kernel, begin, len(grads)),
        (xt, y, mine, other, after, *grads),
        [shaped(*shape) for shape in shapes],
        in_specs=[IN_VMEM] * 5 + [IN_HBM] * len(grads),
        out_specs=[IN_HBM] * 3,
        scratch=writer_scratch(xt.shape[0], y.shape[0], mine.shape[1]),
        aliases={5 + at: at for at in range(len(grads))},
        limit=24,
    )


def last_kernel(grad_ref, keep_ref, send_ref):
    grad = grad_ref[...]
    rows = keep_ref.shape[0] // 2
    cuts = [grad[slot * rows : (slot + 1) * rows] for slot in range(4)]
    wa = lax.axis_index("wa")
    pieces = []
    for step in range(4):
        at = wa ^ step
        piece = cuts[0]
        for slot in range(1, len(cuts)):
            piece = jnp.where(at == slot, cuts[slot], piece)
        pieces.append(piece)
    keep_ref[...] = joined(*pieces[:2])
    send_ref[...] = joined(*pieces[2:]).astype(BF16)


def last_pieces(line, grad):
    shape = (grad.shape[0] // 2, grad.shape[1])
    return line.call(last_kernel, (grad,), [shaped(*shape, F32), shaped(*shape)])


def total_kernel(own_ref, *refs):
    total = own_ref[...]
    for ref in refs[:-1]:
        total = total + ref[...].astype(F32)
    refs[-1][...] = total.astype(BF16)


def total(line, own, received):
    return line.call(total_kernel, (own, *received), [shaped(*own.shape)])[0]


def swap(value, axis, size, step):
    return lax.ppermute(value, axis, [(at, at ^ step) for at in range(size)])


def fast_body(n_wa, n_ha, n_row, tokens, cotangent, gate_weight, up_weight, down_weight):
    hidden_width = gate_weight.shape[1]
    tiles = hidden_width // LANES
    ends = [-(-tiles * (at + 1) // CHUNKS) * LANES for at in range(CHUNKS)]
    chunks = [(begin, end - begin) for begin, end in zip([0] + ends, ends)]
    axes = [((1, 2), (2, 1))[at % 2] for at in range(CHUNKS)]
    line = Line()

    both = jnp.concatenate([tokens, cotangent], axis=0)
    pieces = [both] + [swap(both, "ha", n_ha, step) for step in range(1, n_ha)]
    gate, up = load(Line(), gate_weight, up_weight)
    xy = order_rows(line, pieces)
    xy_other = swap(xy, "row", n_row, 1)

    kept, got = [], []
    for at, ((begin, columns), axis) in enumerate(zip(chunks, axes)):
        keep, send = forward(line, begin, columns, axis, xy, gate, up, down_weight)
        kept.append(keep)
        got.append(swap(send, "wa", n_wa, axis[0]))
    for at, (_, far) in enumerate(axes):
        kept[at], send = halve(line, kept[at], got[at])
        got[at] = swap(send, "wa", n_wa, far)
    order = [1, 0, 3, 2]
    for at in order:
        kept[at] = middle(line, kept[at], got[at])
        got[at] = swap(kept[at], "wa", n_wa, axes[at][0])
    for at in [1, 0, 3, 2]:
        far = axes[at][1]
        kept[at] = join(line, kept[at], got[at])
        got[at] = swap(kept[at], "wa", n_wa, far)

    xt, y_all = factors(line, xy, xy_other)
    mine, other, grad = [], [], ()
    for at in range(0, CHUNKS, 2):
        pair = slice(at, at + 2)
        mine.append(stack(line, axes[pair], list(zip(kept, got))[pair]))
        other.append(swap(mine[-1], "row", n_row, 1))
        grad = input_grad(line, chunks[at][0], mine[-1], gate, up, grad)
    keep, send = last_pieces(line, grad[0])
    received = swap(send, "ha", n_ha, 2)
    grads = weight_grad(line, 0, hidden_width, xt, y_all, mine[0], other[0], (), other[1])
    keep, send = halve(line, keep, received)
    received = swap(send, "ha", n_ha, 1)
    grads = weight_grad(
        line, mine[0].shape[1], hidden_width, xt, y_all, mine[1], other[1], grads, other[0]
    )
    return (total(line, keep, [received]), *grads)


def plain_body(tokens, cotangent, gate_weight, up_weight, down_weight):
    hidden_width = gate_weight.shape[1]
    x = lax.all_gather(tokens, "ha", axis=0, tiled=True)
    y = lax.all_gather(cotangent, "ha", axis=0, tiled=True)
    gate_part = jnp.dot(x, gate_weight, preferred_element_type=F32)
    up_part = jnp.dot(x, up_weight, preferred_element_type=F32)
    dh_part = lax.dot_general(y, down_weight, NT, preferred_element_type=F32)
    summed = lax.psum(jnp.concatenate([gate_part, up_part, dh_part], axis=1), "wa")
    hidden, d_gate, d_up = pointwise(
        summed[:, :hidden_width],
        summed[:, hidden_width : 2 * hidden_width],
        summed[:, 2 * hidden_width :],
    )
    partial = lax.dot_general(
        d_gate, gate_weight, NT, preferred_element_type=F32
    ) + lax.dot_general(d_up, up_weight, NT, preferred_element_type=F32)
    grad_tokens = lax.psum_scatter(partial, "ha", scatter_dimension=0, tiled=True)
    grads = (
        lax.dot_general(x, d_gate, TN, preferred_element_type=F32),
        lax.dot_general(x, d_up, TN, preferred_element_type=F32),
        lax.dot_general(hidden, y, TN, preferred_element_type=F32),
    )
    return (
        grad_tokens.astype(BF16),
        *(lax.psum(g.astype(BF16), "row").astype(BF16) for g in grads),
    )


def solution(mesh):
    n_wa, n_ha, n_row = (mesh.shape[name] for name in ("wa", "ha", "row"))

    def body(tokens, cotangent, gate_weight, up_weight, down_weight):
        width, hidden_width = gate_weight.shape
        fits = (
            n_wa == n_ha == 4
            and n_row == 2
            and width % LANES == 0
            and hidden_width % LANES == 0
            and hidden_width >= LANES * CHUNKS
            and width % (16 * CUTS) == 0
            and (tokens.shape[0] * n_ha) % 16 == 0
        )
        if fits:
            return fast_body(
                n_wa, n_ha, n_row, tokens, cotangent, gate_weight, up_weight, down_weight
            )
        return plain_body(tokens, cotangent, gate_weight, up_weight, down_weight)

    return jax.shard_map(
        body,
        mesh=mesh,
        in_specs=(
            P(("row", "ha"), "wa"),
            P(("row", "ha"), "wa"),
            P("wa", "ha"),
            P("wa", "ha"),
            P("ha", "wa"),
        ),
        out_specs=(P(("row", "ha"), "wa"), P("wa", "ha"), P("wa", "ha"), P("ha", "wa")),
        check_vma=False,
    )
```

```python
import functools

import jax
import jax.numpy as jnp
from jax import lax
from jax.experimental import pallas as pl
from jax.experimental.pallas import tpu as pltpu
from jax.sharding import PartitionSpec as P

BF16 = jnp.bfloat16
F32 = jnp.float32
NT = (((1,), (1,)), ((), ()))
TN = (((0,), (0,)), ((), ()))
LANES = 128
CHUNKS = 4
TILE = 256
CUTS = 4
MIB = 1024 * 1024
IN_VMEM = pl.BlockSpec(memory_space=pltpu.VMEM)
IN_HBM = pl.BlockSpec(memory_space=pl.ANY)


def shaped(rows, columns, dtype=BF16):
    return jax.ShapeDtypeStruct((rows, columns), dtype)


def joined(*blocks):
    return jnp.concatenate([block.astype(F32) for block in blocks], axis=0)


def pointwise(gate_sum, up_sum, dh_sum):
    sig = jax.nn.sigmoid(gate_sum)
    active = gate_sum * sig
    hidden = (active * up_sum).astype(BF16)
    d_up = (dh_sum * active).astype(BF16)
    d_gate = (dh_sum * up_sum * sig * (1.0 + gate_sum * (1.0 - sig))).astype(BF16)
    return (hidden, d_gate, d_up)


class Line:
    def __init__(self):
        self.token = ()

    def call(
        self,
        kernel,
        args,
        out_shape,
        in_specs=None,
        out_specs=None,
        scratch=(),
        aliases=None,
        limit=4,
    ):
        count, outs, tokens = len(args), len(out_shape), len(self.token)

        def body(*refs):
            rest = refs[count + tokens :]
            rest[outs][...] = jnp.zeros_like(rest[outs])
            kernel(*refs[:count], *rest[:outs], *rest[outs + 1 :])

        *results, token = pl.pallas_call(
            body,
            in_specs=(in_specs or [IN_VMEM] * count) + [IN_VMEM] * tokens,
            out_specs=(out_specs or [IN_VMEM] * outs) + [IN_VMEM],
            out_shape=[*out_shape, shaped(8, LANES, F32)],
            scratch_shapes=list(scratch),
            input_output_aliases=aliases or {},
            cost_estimate=pl.CostEstimate(flops=1, bytes_accessed=1, transcendentals=0),
            compiler_params=pltpu.CompilerParams(vmem_limit_bytes=limit * MIB),
            name=getattr(kernel, "func", kernel).__name__,
        )(*args, *self.token)
        self.token = (token,)
        return results


def copy_rows(sems, source, target, begin=0):
    rows = target.shape[0] // CUTS
    copies = []
    for cut in range(CUTS):
        there, here = pl.ds(begin + cut * rows, rows), pl.ds(cut * rows, rows)
        copies.append(pltpu.make_async_copy(source.at[there], target.at[here], sems.at[cut]))
        copies[-1].start()
    return copies


def load_kernel(gate_ref, up_ref, gate_out, up_out, sems):
    copies = copy_rows(sems.at[0], gate_ref, gate_out)
    copies += copy_rows(sems.at[1], up_ref, up_out)
    for copy in copies:
        copy.wait()


def load(line, *weights):
    return line.call(
        load_kernel,
        weights,
        [pltpu.VMEM(weight.shape, BF16) for weight in weights],
        in_specs=[IN_HBM] * len(weights),
        scratch=[pltpu.SemaphoreType.DMA((len(weights), CUTS))],
        limit=30,
    )


def order_kernel(*refs):
    *piece_refs, out_ref = refs
    pieces = [ref[...].astype(F32) for ref in piece_refs]
    rows = pieces[0].shape[0] // 2
    wa = lax.axis_index("wa")
    slots = []
    for slot in range(len(pieces)):
        at = wa ^ slot
        piece = pieces[0]
        for other in range(1, len(pieces)):
            piece = jnp.where(at == other, pieces[other], piece)
        slots.append(piece)
    out_ref[...] = joined(
        *(slot[:rows] for slot in slots), *(slot[rows:] for slot in slots)
    ).astype(BF16)


def order_rows(line, pieces):
    rows, width = pieces[0].shape
    return line.call(order_kernel, pieces, [shaped(4 * rows, width)])[0]


def forward_kernel(begin, near, far, xy_ref, gate_ref, up_ref, down_ref, keep_ref, send_ref):
    there = pl.ds(begin, keep_ref.shape[1])
    group = xy_ref.shape[0] // 2
    rows = group // 4
    x, y = xy_ref[:group], xy_ref[group:]
    gate = jnp.dot(x, gate_ref[:, there], preferred_element_type=F32)
    up = jnp.dot(x, up_ref[:, there], preferred_element_type=F32)
    dh = lax.dot_general(y, down_ref[there], NT, preferred_element_type=F32)

    def slots(*which):
        cuts = [slice(slot * rows, (slot + 1) * rows) for slot in which]
        return joined(*(part[cut] for cut in cuts for part in (gate, up, dh)))

    keep_ref[...] = slots(0, far)
    send_ref[...] = slots(near, near ^ far).astype(BF16)


def forward(line, begin, columns, axes, xy, gate, up, down):
    rows = 6 * (xy.shape[0] // 8)
    return line.call(
        functools.partial(forward_kernel, begin, *axes),
        (xy, gate, up, down),
        [shaped(rows, columns, F32), shaped(rows, columns)],
    )


def halve_kernel(keep_ref, received_ref, own_ref, send_ref):
    total = keep_ref[...] + received_ref[...].astype(F32)
    half = own_ref.shape[0]
    own_ref[...] = total[:half]
    send_ref[...] = total[half:].astype(BF16)


def halve(line, keep, received):
    shape = (keep.shape[0] // 2, keep.shape[1])
    return line.call(halve_kernel, (keep, received), [shaped(*shape, F32), shaped(*shape)])


def middle_kernel(own_ref, received_ref, out_ref):
    total = own_ref[...] + received_ref[...].astype(F32)
    rows = total.shape[0] // 3
    hidden, d_gate, d_up = pointwise(total[:rows], total[rows : 2 * rows], total[2 * rows :])
    out_ref[...] = joined(d_gate, d_up, hidden).astype(BF16)


def middle(line, own, received):
    return line.call(middle_kernel, (own, received), [shaped(*own.shape)])[0]


def join_kernel(first_ref, second_ref, out_ref):
    out_ref[...] = joined(first_ref[...], second_ref[...]).astype(BF16)


def join(line, first, second):
    rows = first.shape[0] + second.shape[0]
    return line.call(join_kernel, (first, second), [shaped(rows, first.shape[1])])[0]


def stack_kernel(axes, ahead, *refs):
    *refs, out_ref = refs
    begin = 0
    for ref in refs[2:]:
        out_ref[:, begin : begin + ref.shape[1]] = ref[...]
        begin += ref.shape[1]
    near, far = axes
    mine, other = refs[0][...].astype(F32), refs[1][...].astype(F32)
    half, rows = mine.shape[0] // 2, mine.shape[0] // 6
    slots = {0: mine[:half], near: mine[half:]}
    slots |= {far: other[:half], near ^ far: other[half:]}
    cuts = [slots[slot][k * rows : (k + 1) * rows] for k in range(3) for slot in range(4)]
    out_ref[:, begin:] = joined(*cuts).astype(BF16)


def stack(line, axes, mine, other, ahead):
    rows = 2 * mine.shape[0]
    columns = mine.shape[1] + sum(block.shape[1] for block in ahead)
    return line.call(
        functools.partial(stack_kernel, axes, len(ahead)),
        (mine, other, *ahead),
        [shaped(rows, columns)],
    )[0]


def input_grad_kernel(begin, columns, stack_ref, gate_ref, up_ref, *refs):
    there = pl.ds(begin, columns)
    here = pl.ds(stack_ref.shape[1] - columns, columns)
    group = stack_ref.shape[0] // 3
    grad = lax.dot_general(
        stack_ref[:group, here], gate_ref[:, there], NT, preferred_element_type=F32
    ) + lax.dot_general(
        stack_ref[group : 2 * group, here], up_ref[:, there], NT, preferred_element_type=F32
    )
    refs[-1][...] = grad + refs[0][...] if len(refs) > 1 else grad


def input_grad(line, begin, columns, stacked, gate_weight, up_weight, start):
    shape = (stacked.shape[0] // 3, gate_weight.shape[0])
    return line.call(
        functools.partial(input_grad_kernel, begin, columns),
        (stacked, gate_weight, up_weight, *start),
        [shaped(*shape, F32)],
    )


def factors_kernel(mine_ref, other_ref, xt_ref, y_all_ref):
    group = mine_ref.shape[0] // 2
    first = lax.axis_index("row") == 0
    x, y = mine_ref[:group], mine_ref[group:]
    x_other, y_other = other_ref[:group], other_ref[group:]
    y_all_ref[:group] = jnp.where(first, y, y_other)
    y_all_ref[group:] = jnp.where(first, y_other, y)
    x_all = jnp.concatenate([jnp.where(first, x, x_other), jnp.where(first, x_other, x)], axis=0)
    xt_ref[...] = x_all.T


def factors(line, xy, other):
    rows, width = xy.shape
    return line.call(factors_kernel, (xy, other), [shaped(width, rows), shaped(rows, width)])


def weight_grad_kernel(parts, xt_ref, y_ref, *refs):
    mine_refs, other_refs = refs[:parts], refs[parts : 2 * parts]
    *outs, both, gate, up, down, sems = refs[2 * parts :]
    group = y_ref.shape[0] // 2
    first = lax.axis_index("row") == 0
    copies = []

    def send(at, source, target):
        copies.append(pltpu.make_async_copy(source, target, sems.at[at, len(copies) // 3]))
        copies[-1].start()

    width = y_ref.shape[1]
    blocks = [pl.ds(at, min(TILE, width - at)) for at in range(0, width, TILE)]
    begin = 0
    for mine_ref, other_ref in zip(mine_refs, other_refs):
        columns = mine_ref.shape[1]
        for start in range(0, columns, TILE):
            size = min(TILE, columns - start)
            source, here = pl.ds(start, size), pl.ds(begin + start, size)
            for at in range(3):
                cut = slice(at * group, (at + 1) * group)
                mine, other = mine_ref[cut, source], other_ref[cut, source]
                both[at, :group, here] = jnp.where(first, mine, other)
                both[at, group:, here] = jnp.where(first, other, mine)
            for at, grad in enumerate((gate, up)):
                rows = both[at, :, here]
                for block in blocks:
                    grad[block, here] = jnp.dot(
                        xt_ref[block], rows, preferred_element_type=F32
                    ).astype(BF16)
                send(at, grad.at[:, here], outs[at].at[:, here])
            hidden = both[2, :, here].T
            for block in blocks:
                down[here, block] = jnp.dot(
                    hidden, y_ref[:, block], preferred_element_type=F32
                ).astype(BF16)
            send(2, down.at[here], outs[2].at[here])
        begin += columns
    for copy in copies:
        copy.wait()


def weight_grad(line, xt, y, mine, other):
    width = xt.shape[0]
    hidden_width = sum(m.shape[1] for m in mine)
    shapes = [(width, hidden_width), (width, hidden_width), (hidden_width, width)]
    steps = sum(pl.cdiv(m.shape[1], TILE) for m in mine)
    return line.call(
        functools.partial(weight_grad_kernel, len(mine)),
        (xt, y, *mine, *other),
        [shaped(*shape) for shape in shapes],
        out_specs=[IN_HBM] * 3,
        scratch=[
            pltpu.VMEM((3, y.shape[0], hidden_width), BF16),
            *(pltpu.VMEM(shape, BF16) for shape in shapes),
            pltpu.SemaphoreType.DMA((3, steps)),
        ],
        limit=40,
    )


def last_kernel(grad_ref, *out_refs):
    grad = grad_ref[...]
    rows = out_refs[0].shape[0]
    cuts = [grad[slot * rows : (slot + 1) * rows] for slot in range(len(out_refs))]
    wa = lax.axis_index("wa")
    for step, out_ref in enumerate(out_refs):
        at = wa ^ step
        piece = cuts[0]
        for slot in range(1, len(cuts)):
            piece = jnp.where(at == slot, cuts[slot], piece)
        out_ref[...] = piece.astype(out_ref.dtype)


def last_pieces(line, parts, grad):
    shape = (grad.shape[0] // parts, grad.shape[1])
    return line.call(
        last_kernel, (grad,), [shaped(*shape, F32)] + [shaped(*shape)] * (parts - 1)
    )


def total_kernel(own_ref, *refs):
    total = own_ref[...]
    for ref in refs[:-1]:
        total = total + ref[...].astype(F32)
    refs[-1][...] = total.astype(BF16)


def total(line, own, received):
    return line.call(total_kernel, (own, *received), [shaped(*own.shape)])[0]


def swap(value, axis, size, step):
    return lax.ppermute(value, axis, [(at, at ^ step) for at in range(size)])


def fast_body(n_wa, n_ha, n_row, tokens, cotangent, gate_weight, up_weight, down_weight):
    hidden_width = gate_weight.shape[1]
    tiles = hidden_width // LANES
    ends = [-(-tiles * (at + 1) // CHUNKS) * LANES for at in range(CHUNKS)]
    chunks = [(begin, end - begin) for begin, end in zip([0] + ends, ends)]
    axes = [((1, 2), (2, 1))[at % 2] for at in range(CHUNKS)]
    line = Line()

    both = jnp.concatenate([tokens, cotangent], axis=0)
    pieces = [both] + [swap(both, "ha", n_ha, step) for step in range(1, n_ha)]
    gate, up = load(Line(), gate_weight, up_weight)
    xy = order_rows(line, pieces)
    xy_other = swap(xy, "row", n_row, 1)

    kept, got = [], []
    for at, ((begin, columns), axis) in enumerate(zip(chunks, axes)):
        keep, send = forward(line, begin, columns, axis, xy, gate, up, down_weight)
        kept.append(keep)
        got.append(swap(send, "wa", n_wa, axis[0]))
    for at, (_, far) in enumerate(axes):
        kept[at], send = halve(line, kept[at], got[at])
        got[at] = swap(send, "wa", n_wa, far)
    order = [1, 0, 3, 2]
    for at in order:
        kept[at] = middle(line, kept[at], got[at])
        got[at] = swap(kept[at], "wa", n_wa, axes[at][0])
    for at in [1, 0, 3, 2]:
        far = axes[at][1]
        kept[at] = join(line, kept[at], got[at])
        got[at] = swap(kept[at], "wa", n_wa, far)

    xt, y_all = factors(line, xy, xy_other)
    mine, other, ahead, grad = [], [], [], ()
    for at, (begin, columns) in enumerate(chunks):
        stacked = stack(line, axes[at], kept[at], got[at], ahead)
        if at in [1, 3]:
            mine.append(stacked)
            other.append(swap(stacked, "row", n_row, 1))
            ahead = []
        else:
            ahead = [stacked]
        grad = input_grad(line, begin, columns, stacked, gate, up, grad)
    own, *sends = last_pieces(line, n_ha, grad[0])
    received = [swap(sent, "ha", n_ha, k + 1) for k, sent in enumerate(sends)]
    grads = weight_grad(line, xt, y_all, mine, other)
    return (total(line, own, received), *grads)


def plain_body(tokens, cotangent, gate_weight, up_weight, down_weight):
    hidden_width = gate_weight.shape[1]
    x = lax.all_gather(tokens, "ha", axis=0, tiled=True)
    y = lax.all_gather(cotangent, "ha", axis=0, tiled=True)
    gate_part = jnp.dot(x, gate_weight, preferred_element_type=F32)
    up_part = jnp.dot(x, up_weight, preferred_element_type=F32)
    dh_part = lax.dot_general(y, down_weight, NT, preferred_element_type=F32)
    summed = lax.psum(jnp.concatenate([gate_part, up_part, dh_part], axis=1), "wa")
    hidden, d_gate, d_up = pointwise(
        summed[:, :hidden_width],
        summed[:, hidden_width : 2 * hidden_width],
        summed[:, 2 * hidden_width :],
    )
    partial = lax.dot_general(
        d_gate, gate_weight, NT, preferred_element_type=F32
    ) + lax.dot_general(d_up, up_weight, NT, preferred_element_type=F32)
    grad_tokens = lax.psum_scatter(partial, "ha", scatter_dimension=0, tiled=True)
    grads = (
        lax.dot_general(x, d_gate, TN, preferred_element_type=F32),
        lax.dot_general(x, d_up, TN, preferred_element_type=F32),
        lax.dot_general(hidden, y, TN, preferred_element_type=F32),
    )
    return (
        grad_tokens.astype(BF16),
        *(lax.psum(g.astype(BF16), "row").astype(BF16) for g in grads),
    )


def solution(mesh):
    n_wa, n_ha, n_row = (mesh.shape[name] for name in ("wa", "ha", "row"))

    def body(tokens, cotangent, gate_weight, up_weight, down_weight):
        width, hidden_width = gate_weight.shape
        fits = (
            n_wa == n_ha == 4
            and n_row == 2
            and width % LANES == 0
            and hidden_width % LANES == 0
            and hidden_width >= LANES * CHUNKS
            and width % (16 * CUTS) == 0
            and (tokens.shape[0] * n_ha) % 16 == 0
        )
        if fits:
            return fast_body(
                n_wa, n_ha, n_row, tokens, cotangent, gate_weight, up_weight, down_weight
            )
        return plain_body(tokens, cotangent, gate_weight, up_weight, down_weight)

    return jax.shard_map(
        body,
        mesh=mesh,
        in_specs=(
            P(("row", "ha"), "wa"),
            P(("row", "ha"), "wa"),
            P("wa", "ha"),
            P("wa", "ha"),
            P("ha", "wa"),
        ),
        out_specs=(P(("row", "ha"), "wa"), P("wa", "ha"), P("wa", "ha"), P("ha", "wa")),
        check_vma=False,
    )
```

```python
import functools

import jax
import jax.numpy as jnp
from jax import lax
from jax.experimental import pallas as pl
from jax.experimental.pallas import tpu as pltpu
from jax.sharding import PartitionSpec as P

BF16 = jnp.bfloat16
F32 = jnp.float32
NT = (((1,), (1,)), ((), ()))
TN = (((0,), (0,)), ((), ()))
LANES = 128
CHUNKS = 4
TILE = 256
CUTS = 4
MIB = 1024 * 1024
IN_VMEM = pl.BlockSpec(memory_space=pltpu.VMEM)
IN_HBM = pl.BlockSpec(memory_space=pl.ANY)


def shaped(rows, columns, dtype=BF16):
    return jax.ShapeDtypeStruct((rows, columns), dtype)


def joined(*blocks):
    return jnp.concatenate([block.astype(F32) for block in blocks], axis=0)


def pointwise(gate_sum, up_sum, dh_sum):
    sig = jax.nn.sigmoid(gate_sum)
    active = gate_sum * sig
    hidden = (active * up_sum).astype(BF16)
    d_up = (dh_sum * active).astype(BF16)
    d_gate = (dh_sum * up_sum * sig * (1.0 + gate_sum * (1.0 - sig))).astype(BF16)
    return (hidden, d_gate, d_up)


class Line:
    def __init__(self):
        self.token = ()

    def call(
        self,
        kernel,
        args,
        out_shape,
        in_specs=None,
        out_specs=None,
        scratch=(),
        aliases=None,
        limit=4,
    ):
        count, outs, tokens = len(args), len(out_shape), len(self.token)

        def body(*refs):
            rest = refs[count + tokens :]
            rest[outs][...] = jnp.zeros_like(rest[outs])
            kernel(*refs[:count], *rest[:outs], *rest[outs + 1 :])

        *results, token = pl.pallas_call(
            body,
            in_specs=(in_specs or [IN_VMEM] * count) + [IN_VMEM] * tokens,
            out_specs=(out_specs or [IN_VMEM] * outs) + [IN_VMEM],
            out_shape=[*out_shape, shaped(8, LANES, F32)],
            scratch_shapes=list(scratch),
            input_output_aliases=aliases or {},
            cost_estimate=pl.CostEstimate(flops=1, bytes_accessed=1, transcendentals=0),
            compiler_params=pltpu.CompilerParams(vmem_limit_bytes=limit * MIB),
            name=getattr(kernel, "func", kernel).__name__,
        )(*args, *self.token)
        self.token = (token,)
        return results


def copy_rows(sems, source, target, begin=0):
    rows = target.shape[0] // CUTS
    copies = []
    for cut in range(CUTS):
        there, here = pl.ds(begin + cut * rows, rows), pl.ds(cut * rows, rows)
        copies.append(pltpu.make_async_copy(source.at[there], target.at[here], sems.at[cut]))
        copies[-1].start()
    return copies


def load_kernel(gate_ref, up_ref, gate_out, up_out, sems):
    copies = copy_rows(sems.at[0], gate_ref, gate_out)
    copies += copy_rows(sems.at[1], up_ref, up_out)
    for copy in copies:
        copy.wait()


def load(line, *weights):
    return line.call(
        load_kernel,
        weights,
        [pltpu.VMEM(weight.shape, BF16) for weight in weights],
        in_specs=[IN_HBM] * len(weights),
        scratch=[pltpu.SemaphoreType.DMA((len(weights), CUTS))],
        limit=30,
    )


def turned(value, row):
    return (1 - row) * value + row * (((value & 1) << 1) | (value >> 1))


def order_kernel(*refs):
    *piece_refs, out_ref = refs
    pieces = [ref[...].astype(F32) for ref in piece_refs]
    rows = pieces[0].shape[0] // 2
    wa, row = lax.axis_index("wa"), lax.axis_index("row")
    slots = []
    for slot in range(len(pieces)):
        at = wa ^ turned(slot, row)
        piece = pieces[0]
        for other in range(1, len(pieces)):
            piece = jnp.where(at == other, pieces[other], piece)
        slots.append(piece)
    out_ref[...] = joined(
        *(slot[:rows] for slot in slots), *(slot[rows:] for slot in slots)
    ).astype(BF16)


def order_rows(line, pieces):
    rows, width = pieces[0].shape
    return line.call(order_kernel, pieces, [shaped(4 * rows, width)])[0]


def forward_kernel(begin, near, far, xy_ref, gate_ref, up_ref, down_ref, keep_ref, send_ref):
    there = pl.ds(begin, keep_ref.shape[1])
    group = xy_ref.shape[0] // 2
    rows = group // 4
    x, y = xy_ref[:group], xy_ref[group:]
    gate = jnp.dot(x, gate_ref[:, there], preferred_element_type=F32)
    up = jnp.dot(x, up_ref[:, there], preferred_element_type=F32)
    dh = lax.dot_general(y, down_ref[there], NT, preferred_element_type=F32)

    def slots(*which):
        cuts = [slice(slot * rows, (slot + 1) * rows) for slot in which]
        return joined(*(part[cut] for cut in cuts for part in (gate, up, dh)))

    keep_ref[...] = slots(0, far)
    send_ref[...] = slots(near, near ^ far).astype(BF16)


def forward(line, begin, columns, axes, xy, gate, up, down):
    rows = 6 * (xy.shape[0] // 8)
    return line.call(
        functools.partial(forward_kernel, begin, *axes),
        (xy, gate, up, down),
        [shaped(rows, columns, F32), shaped(rows, columns)],
    )


def halve_kernel(keep_ref, received_ref, own_ref, send_ref):
    total = keep_ref[...] + received_ref[...].astype(F32)
    half = own_ref.shape[0]
    own_ref[...] = total[:half]
    send_ref[...] = total[half:].astype(BF16)


def halve(line, keep, received):
    shape = (keep.shape[0] // 2, keep.shape[1])
    return line.call(halve_kernel, (keep, received), [shaped(*shape, F32), shaped(*shape)])


def middle_kernel(own_ref, received_ref, out_ref):
    total = own_ref[...] + received_ref[...].astype(F32)
    rows = total.shape[0] // 3
    hidden, d_gate, d_up = pointwise(total[:rows], total[rows : 2 * rows], total[2 * rows :])
    out_ref[...] = joined(d_gate, d_up, hidden).astype(BF16)


def middle(line, own, received):
    return line.call(middle_kernel, (own, received), [shaped(*own.shape)])[0]


def join_kernel(first_ref, second_ref, out_ref):
    out_ref[...] = joined(first_ref[...], second_ref[...]).astype(BF16)


def join(line, first, second):
    rows = first.shape[0] + second.shape[0]
    return line.call(join_kernel, (first, second), [shaped(rows, first.shape[1])])[0]


def stack_kernel(axes, *refs):
    out_ref = refs[-1]
    begin = 0
    for at, (near, far) in enumerate(axes):
        mine, other = refs[2 * at][...].astype(F32), refs[2 * at + 1][...].astype(F32)
        columns = mine.shape[1]
        half, rows = mine.shape[0] // 2, mine.shape[0] // 6
        slots = {0: mine[:half], near: mine[half:]}
        slots |= {far: other[:half], near ^ far: other[half:]}
        cuts = [slots[slot][k * rows : (k + 1) * rows] for k in range(3) for slot in range(4)]
        out_ref[:, begin : begin + columns] = joined(*cuts).astype(BF16)
        begin += columns


def stack(line, axes, blocks):
    rows = 2 * blocks[0][0].shape[0]
    columns = sum(mine.shape[1] for mine, _ in blocks)
    return line.call(
        functools.partial(stack_kernel, axes),
        [block for pair in blocks for block in pair],
        [shaped(rows, columns)],
    )[0]


def input_grad_kernel(begin, stack_ref, gate_ref, up_ref, *refs):
    there = pl.ds(begin, stack_ref.shape[1])
    group = stack_ref.shape[0] // 3
    grad = lax.dot_general(
        stack_ref[:group], gate_ref[:, there], NT, preferred_element_type=F32
    ) + lax.dot_general(
        stack_ref[group : 2 * group], up_ref[:, there], NT, preferred_element_type=F32
    )
    refs[-1][...] = grad + refs[0][...] if len(refs) > 1 else grad


def input_grad(line, begin, stacked, gate_weight, up_weight, start):
    shape = (stacked.shape[0] // 3, gate_weight.shape[0])
    return line.call(
        functools.partial(input_grad_kernel, begin),
        (stacked, gate_weight, up_weight, *start),
        [shaped(*shape, F32)],
    )


def factors_kernel(mine_ref, other_ref, xt_ref, y_all_ref):
    group = mine_ref.shape[0] // 2
    first = lax.axis_index("row") == 0
    x, y = mine_ref[:group], mine_ref[group:]
    x_other, y_other = other_ref[:group], other_ref[group:]
    y_all_ref[:group] = jnp.where(first, y, y_other)
    y_all_ref[group:] = jnp.where(first, y_other, y)
    x_all = jnp.concatenate([jnp.where(first, x, x_other), jnp.where(first, x_other, x)], axis=0)
    xt_ref[...] = x_all.T


def factors(line, xy, other):
    rows, width = xy.shape
    return line.call(factors_kernel, (xy, other), [shaped(width, rows), shaped(rows, width)])


class Writer:
    def __init__(self, begin, xt_ref, y_ref, mine_ref, other_ref, outs, scratch):
        self.begin, self.xt_ref, self.y_ref, self.outs = begin, xt_ref, y_ref, outs
        self.both, self.gate, self.up, self.down, self.sems = scratch
        self.mine_ref, self.other_ref = mine_ref, other_ref
        columns = min(mine_ref.shape[1], outs[0].shape[1] - begin)
        self.tiles = [(at, min(TILE, columns - at)) for at in range(0, columns, TILE)]
        self.copies = []

    def send(self, at, source, target):
        step = len(self.copies) // 3
        self.copies.append(pltpu.make_async_copy(source, target, self.sems.at[at, step]))
        self.copies[-1].start()

    def tile(self, start, size):
        group = self.y_ref.shape[0] // 2
        first = lax.axis_index("row") == 0
        here, there = pl.ds(start, size), pl.ds(self.begin + start, size)
        for at in range(3):
            cut = slice(at * group, (at + 1) * group)
            mine, other = self.mine_ref[cut, here], self.other_ref[cut, here]
            self.both[at, :group, here] = jnp.where(first, mine, other)
            self.both[at, group:, here] = jnp.where(first, other, mine)
        width = self.y_ref.shape[1]
        blocks = [pl.ds(at, min(TILE, width - at)) for at in range(0, width, TILE)]
        for at, grad in enumerate((self.gate, self.up)):
            rows = self.both[at, :, here]
            for block in blocks:
                grad[block, here] = jnp.dot(
                    self.xt_ref[block], rows, preferred_element_type=F32
                ).astype(BF16)
            self.send(at, grad.at[:, here], self.outs[at].at[:, there])
        hidden = self.both[2, :, here].T
        for block in blocks:
            self.down[here, block] = jnp.dot(
                hidden, self.y_ref[:, block], preferred_element_type=F32
            ).astype(BF16)
        self.send(2, self.down.at[here], self.outs[2].at[there])

    def wait(self):
        for copy in self.copies:
            copy.wait()


def grad_shapes(width, hidden_width):
    return [(width, hidden_width), (width, hidden_width), (hidden_width, width)]


def writer_scratch(width, rows, columns):
    return [
        pltpu.VMEM((3, rows, columns), BF16),
        *(pltpu.VMEM(shape, BF16) for shape in grad_shapes(width, columns)),
        pltpu.SemaphoreType.DMA((3, pl.cdiv(columns, TILE))),
    ]


def weight_grad_kernel(begin, held, xt_ref, y_ref, mine_ref, other_ref, _, *refs):
    outs, scratch = refs[held : held + 3], refs[held + 3 :]
    writer = Writer(begin, xt_ref, y_ref, mine_ref, other_ref, outs, scratch)
    for tile in writer.tiles:
        writer.tile(*tile)
    writer.wait()


def weight_grad(line, begin, hidden_width, xt, y, mine, other, grads, after):
    shapes = grad_shapes(xt.shape[0], hidden_width)
    return line.call(
        functools.partial(weight_grad_kernel, begin, len(grads)),
        (xt, y, mine, other, after, *grads),
        [shaped(*shape) for shape in shapes],
        in_specs=[IN_VMEM] * 5 + [IN_HBM] * len(grads),
        out_specs=[IN_HBM] * 3,
        scratch=writer_scratch(xt.shape[0], y.shape[0], mine.shape[1]),
        aliases={5 + at: at for at in range(len(grads))},
        limit=24,
    )


def last_kernel(grad_ref, keep_ref, send_ref):
    grad = grad_ref[...]
    rows = keep_ref.shape[0] // 2
    cuts = [grad[slot * rows : (slot + 1) * rows] for slot in range(4)]
    wa, row = lax.axis_index("wa"), lax.axis_index("row")
    pieces = []
    for step in range(4):
        at = turned(wa ^ step, row)
        piece = cuts[0]
        for slot in range(1, len(cuts)):
            piece = jnp.where(at == slot, cuts[slot], piece)
        pieces.append(piece)
    keep_ref[...] = joined(*pieces[:2])
    send_ref[...] = joined(*pieces[2:]).astype(BF16)


def last_pieces(line, grad):
    shape = (grad.shape[0] // 2, grad.shape[1])
    return line.call(last_kernel, (grad,), [shaped(*shape, F32), shaped(*shape)])


def total_kernel(own_ref, *refs):
    total = own_ref[...]
    for ref in refs[:-1]:
        total = total + ref[...].astype(F32)
    refs[-1][...] = total.astype(BF16)


def total(line, own, received):
    return line.call(total_kernel, (own, *received), [shaped(*own.shape)])[0]


def swap(value, axis, size, step):
    return lax.ppermute(value, axis, [(at, at ^ step) for at in range(size)])


def exchange(value, n_wa, n_row, step):
    pairs = [
        (at * n_row + row, (at ^ turned(step, row)) * n_row + row)
        for at in range(n_wa)
        for row in range(n_row)
    ]
    return lax.ppermute(value, ("wa", "row"), pairs)


def fast_body(n_wa, n_ha, n_row, tokens, cotangent, gate_weight, up_weight, down_weight):
    hidden_width = gate_weight.shape[1]
    tiles = hidden_width // LANES
    ends = [-(-tiles * (at + 1) // CHUNKS) * LANES for at in range(CHUNKS)]
    chunks = [(begin, end - begin) for begin, end in zip([0] + ends, ends)]
    axes = [((1, 2), (2, 1))[at % 2] for at in range(CHUNKS)]
    line = Line()

    both = jnp.concatenate([tokens, cotangent], axis=0)
    pieces = [both] + [swap(both, "ha", n_ha, step) for step in range(1, n_ha)]
    gate, up = load(Line(), gate_weight, up_weight)
    xy = order_rows(line, pieces)
    xy_other = swap(xy, "row", n_row, 1)

    kept, got = [], []
    for at, ((begin, columns), axis) in enumerate(zip(chunks, axes)):
        keep, send = forward(line, begin, columns, axis, xy, gate, up, down_weight)
        kept.append(keep)
        got.append(exchange(send, n_wa, n_row, axis[0]))
    for at, (_, far) in enumerate(axes):
        kept[at], send = halve(line, kept[at], got[at])
        got[at] = exchange(send, n_wa, n_row, far)
    order = [1, 0, 3, 2]
    for at in order:
        kept[at] = middle(line, kept[at], got[at])
        got[at] = exchange(kept[at], n_wa, n_row, axes[at][0])
    for at in [1, 0, 3, 2]:
        far = axes[at][1]
        kept[at] = join(line, kept[at], got[at])
        got[at] = exchange(kept[at], n_wa, n_row, far)

    xt, y_all = factors(line, xy, xy_other)
    mine, other, grad = [], [], ()
    for at in range(0, CHUNKS, 2):
        pair = slice(at, at + 2)
        mine.append(stack(line, axes[pair], list(zip(kept, got))[pair]))
        other.append(swap(mine[-1], "row", n_row, 1))
        grad = input_grad(line, chunks[at][0], mine[-1], gate, up, grad)
    keep, send = last_pieces(line, grad[0])
    received = swap(send, "ha", n_ha, 2)
    grads = weight_grad(line, 0, hidden_width, xt, y_all, mine[0], other[0], (), other[1])
    keep, send = halve(line, keep, received)
    received = swap(send, "ha", n_ha, 1)
    grads = weight_grad(
        line, mine[0].shape[1], hidden_width, xt, y_all, mine[1], other[1], grads, other[0]
    )
    return (total(line, keep, [received]), *grads)


def plain_body(tokens, cotangent, gate_weight, up_weight, down_weight):
    hidden_width = gate_weight.shape[1]
    x = lax.all_gather(tokens, "ha", axis=0, tiled=True)
    y = lax.all_gather(cotangent, "ha", axis=0, tiled=True)
    gate_part = jnp.dot(x, gate_weight, preferred_element_type=F32)
    up_part = jnp.dot(x, up_weight, preferred_element_type=F32)
    dh_part = lax.dot_general(y, down_weight, NT, preferred_element_type=F32)
    summed = lax.psum(jnp.concatenate([gate_part, up_part, dh_part], axis=1), "wa")
    hidden, d_gate, d_up = pointwise(
        summed[:, :hidden_width],
        summed[:, hidden_width : 2 * hidden_width],
        summed[:, 2 * hidden_width :],
    )
    partial = lax.dot_general(
        d_gate, gate_weight, NT, preferred_element_type=F32
    ) + lax.dot_general(d_up, up_weight, NT, preferred_element_type=F32)
    grad_tokens = lax.psum_scatter(partial, "ha", scatter_dimension=0, tiled=True)
    grads = (
        lax.dot_general(x, d_gate, TN, preferred_element_type=F32),
        lax.dot_general(x, d_up, TN, preferred_element_type=F32),
        lax.dot_general(hidden, y, TN, preferred_element_type=F32),
    )
    return (
        grad_tokens.astype(BF16),
        *(lax.psum(g.astype(BF16), "row").astype(BF16) for g in grads),
    )


def solution(mesh):
    n_wa, n_ha, n_row = (mesh.shape[name] for name in ("wa", "ha", "row"))

    def body(tokens, cotangent, gate_weight, up_weight, down_weight):
        width, hidden_width = gate_weight.shape
        fits = (
            n_wa == n_ha == 4
            and n_row == 2
            and width % LANES == 0
            and hidden_width % LANES == 0
            and hidden_width >= LANES * CHUNKS
            and width % (16 * CUTS) == 0
            and (tokens.shape[0] * n_ha) % 16 == 0
        )
        if fits:
            return fast_body(
                n_wa, n_ha, n_row, tokens, cotangent, gate_weight, up_weight, down_weight
            )
        return plain_body(tokens, cotangent, gate_weight, up_weight, down_weight)

    return jax.shard_map(
        body,
        mesh=mesh,
        in_specs=(
            P(("row", "ha"), "wa"),
            P(("row", "ha"), "wa"),
            P("wa", "ha"),
            P("wa", "ha"),
            P("ha", "wa"),
        ),
        out_specs=(P(("row", "ha"), "wa"), P("wa", "ha"), P("wa", "ha"), P("ha", "wa")),
        check_vma=False,
    )
```

```python
import functools

import jax
import jax.numpy as jnp
from jax import lax
from jax.experimental import pallas as pl
from jax.experimental.pallas import tpu as pltpu
from jax.sharding import PartitionSpec as P

BF16 = jnp.bfloat16
F32 = jnp.float32
NT = (((1,), (1,)), ((), ()))
TN = (((0,), (0,)), ((), ()))
LANES = 128
CHUNKS = 4
TILE = 256
CUTS = 4
MIB = 1024 * 1024
IN_VMEM = pl.BlockSpec(memory_space=pltpu.VMEM)
IN_HBM = pl.BlockSpec(memory_space=pl.ANY)


def shaped(rows, columns, dtype=BF16):
    return jax.ShapeDtypeStruct((rows, columns), dtype)


def joined(*blocks):
    return jnp.concatenate([block.astype(F32) for block in blocks], axis=0)


def pointwise(gate_sum, up_sum, dh_sum):
    sig = jax.nn.sigmoid(gate_sum)
    active = gate_sum * sig
    hidden = (active * up_sum).astype(BF16)
    d_up = (dh_sum * active).astype(BF16)
    d_gate = (dh_sum * up_sum * sig * (1.0 + gate_sum * (1.0 - sig))).astype(BF16)
    return (hidden, d_gate, d_up)


class Line:
    def __init__(self):
        self.token = ()

    def call(
        self,
        kernel,
        args,
        out_shape,
        in_specs=None,
        out_specs=None,
        scratch=(),
        aliases=None,
        limit=4,
    ):
        count, outs, tokens = len(args), len(out_shape), len(self.token)

        def body(*refs):
            rest = refs[count + tokens :]
            rest[outs][...] = jnp.zeros_like(rest[outs])
            kernel(*refs[:count], *rest[:outs], *rest[outs + 1 :])

        *results, token = pl.pallas_call(
            body,
            in_specs=(in_specs or [IN_VMEM] * count) + [IN_VMEM] * tokens,
            out_specs=(out_specs or [IN_VMEM] * outs) + [IN_VMEM],
            out_shape=[*out_shape, shaped(8, LANES, F32)],
            scratch_shapes=list(scratch),
            input_output_aliases=aliases or {},
            cost_estimate=pl.CostEstimate(flops=1, bytes_accessed=1, transcendentals=0),
            compiler_params=pltpu.CompilerParams(vmem_limit_bytes=limit * MIB),
            name=getattr(kernel, "func", kernel).__name__,
        )(*args, *self.token)
        self.token = (token,)
        return results


def copy_rows(sems, source, target, begin=0):
    rows = target.shape[0] // CUTS
    copies = []
    for cut in range(CUTS):
        there, here = pl.ds(begin + cut * rows, rows), pl.ds(cut * rows, rows)
        copies.append(pltpu.make_async_copy(source.at[there], target.at[here], sems.at[cut]))
        copies[-1].start()
    return copies


def load_kernel(gate_ref, up_ref, gate_out, up_out, sems):
    copies = copy_rows(sems.at[0], gate_ref, gate_out)
    copies += copy_rows(sems.at[1], up_ref, up_out)
    for copy in copies:
        copy.wait()


def load(line, *weights):
    return line.call(
        load_kernel,
        weights,
        [pltpu.VMEM(weight.shape, BF16) for weight in weights],
        in_specs=[IN_HBM] * len(weights),
        scratch=[pltpu.SemaphoreType.DMA((len(weights), CUTS))],
        limit=30,
    )


def order_kernel(*refs):
    *piece_refs, out_ref = refs
    pieces = [ref[...].astype(F32) for ref in piece_refs]
    rows = pieces[0].shape[0] // 2
    wa = lax.axis_index("wa")
    slots = []
    for slot in range(len(pieces)):
        at = wa ^ slot
        piece = pieces[0]
        for other in range(1, len(pieces)):
            piece = jnp.where(at == other, pieces[other], piece)
        slots.append(piece)
    out_ref[...] = joined(
        *(slot[:rows] for slot in slots), *(slot[rows:] for slot in slots)
    ).astype(BF16)


def order_rows(line, pieces):
    rows, width = pieces[0].shape
    return line.call(order_kernel, pieces, [shaped(4 * rows, width)])[0]


def forward_kernel(begin, near, far, xy_ref, gate_ref, up_ref, down_ref, keep_ref, send_ref):
    there = pl.ds(begin, keep_ref.shape[1])
    group = xy_ref.shape[0] // 2
    rows = group // 4
    x, y = xy_ref[:group], xy_ref[group:]
    gate = jnp.dot(x, gate_ref[:, there], preferred_element_type=F32)
    up = jnp.dot(x, up_ref[:, there], preferred_element_type=F32)
    dh = lax.dot_general(y, down_ref[there], NT, preferred_element_type=F32)

    def slots(*which):
        cuts = [slice(slot * rows, (slot + 1) * rows) for slot in which]
        return joined(*(part[cut] for cut in cuts for part in (gate, up, dh)))

    keep_ref[...] = slots(0, far)
    send_ref[...] = slots(near, near ^ far).astype(BF16)


def forward(line, begin, columns, axes, xy, gate, up, down):
    rows = 6 * (xy.shape[0] // 8)
    return line.call(
        functools.partial(forward_kernel, begin, *axes),
        (xy, gate, up, down),
        [shaped(rows, columns, F32), shaped(rows, columns)],
    )


def halve_kernel(keep_ref, received_ref, own_ref, send_ref):
    total = keep_ref[...] + received_ref[...].astype(F32)
    half = own_ref.shape[0]
    own_ref[...] = total[:half]
    send_ref[...] = total[half:].astype(BF16)


def halve(line, keep, received):
    shape = (keep.shape[0] // 2, keep.shape[1])
    return line.call(halve_kernel, (keep, received), [shaped(*shape, F32), shaped(*shape)])


def middle_kernel(own_ref, received_ref, out_ref):
    total = own_ref[...] + received_ref[...].astype(F32)
    rows = total.shape[0] // 3
    hidden, d_gate, d_up = pointwise(total[:rows], total[rows : 2 * rows], total[2 * rows :])
    out_ref[...] = joined(d_gate, d_up, hidden).astype(BF16)


def middle(line, own, received):
    return line.call(middle_kernel, (own, received), [shaped(*own.shape)])[0]


def join_kernel(first_ref, second_ref, out_ref):
    out_ref[...] = joined(first_ref[...], second_ref[...]).astype(BF16)


def join(line, first, second):
    rows = first.shape[0] + second.shape[0]
    return line.call(join_kernel, (first, second), [shaped(rows, first.shape[1])])[0]


def stack_kernel(axes, *refs):
    out_ref = refs[-1]
    begin = 0
    for at, (near, far) in enumerate(axes):
        mine, other = refs[2 * at][...].astype(F32), refs[2 * at + 1][...].astype(F32)
        columns = mine.shape[1]
        half, rows = mine.shape[0] // 2, mine.shape[0] // 6
        slots = {0: mine[:half], near: mine[half:]}
        slots |= {far: other[:half], near ^ far: other[half:]}
        cuts = [slots[slot][k * rows : (k + 1) * rows] for k in range(3) for slot in range(4)]
        out_ref[:, begin : begin + columns] = joined(*cuts).astype(BF16)
        begin += columns


def stack(line, axes, blocks):
    rows = 2 * blocks[0][0].shape[0]
    columns = sum(mine.shape[1] for mine, _ in blocks)
    return line.call(
        functools.partial(stack_kernel, axes),
        [block for pair in blocks for block in pair],
        [shaped(rows, columns)],
    )[0]


def input_grad_kernel(begin, stack_ref, gate_ref, up_ref, *refs):
    there = pl.ds(begin, stack_ref.shape[1])
    group = stack_ref.shape[0] // 3
    grad = lax.dot_general(
        stack_ref[:group], gate_ref[:, there], NT, preferred_element_type=F32
    ) + lax.dot_general(
        stack_ref[group : 2 * group], up_ref[:, there], NT, preferred_element_type=F32
    )
    refs[-1][...] = grad + refs[0][...] if len(refs) > 1 else grad


def input_grad(line, begin, stacked, gate_weight, up_weight, start):
    shape = (stacked.shape[0] // 3, gate_weight.shape[0])
    return line.call(
        functools.partial(input_grad_kernel, begin),
        (stacked, gate_weight, up_weight, *start),
        [shaped(*shape, F32)],
    )


def factors_kernel(mine_ref, other_ref, xt_ref, y_all_ref):
    group = mine_ref.shape[0] // 2
    first = lax.axis_index("row") == 0
    x, y = mine_ref[:group], mine_ref[group:]
    x_other, y_other = other_ref[:group], other_ref[group:]
    y_all_ref[:group] = jnp.where(first, y, y_other)
    y_all_ref[group:] = jnp.where(first, y_other, y)
    x_all = jnp.concatenate([jnp.where(first, x, x_other), jnp.where(first, x_other, x)], axis=0)
    xt_ref[...] = x_all.T


def factors(line, xy, other):
    rows, width = xy.shape
    return line.call(factors_kernel, (xy, other), [shaped(width, rows), shaped(rows, width)])


class Writer:
    def __init__(self, begin, xt_ref, y_ref, mine_ref, other_ref, outs, scratch):
        self.begin, self.xt_ref, self.y_ref, self.outs = begin, xt_ref, y_ref, outs
        self.both, self.gate, self.up, self.down, self.sems = scratch
        self.mine_ref, self.other_ref = mine_ref, other_ref
        columns = min(mine_ref.shape[1], outs[0].shape[1] - begin)
        self.tiles = [(at, min(TILE, columns - at)) for at in range(0, columns, TILE)]
        self.copies = []

    def send(self, at, source, target):
        step = len(self.copies) // 3
        self.copies.append(pltpu.make_async_copy(source, target, self.sems.at[at, step]))
        self.copies[-1].start()

    def tile(self, start, size):
        group = self.y_ref.shape[0] // 2
        first = lax.axis_index("row") == 0
        here, there = pl.ds(start, size), pl.ds(self.begin + start, size)
        for at in range(3):
            cut = slice(at * group, (at + 1) * group)
            mine, other = self.mine_ref[cut, here], self.other_ref[cut, here]
            self.both[at, :group, here] = jnp.where(first, mine, other)
            self.both[at, group:, here] = jnp.where(first, other, mine)
        width = self.y_ref.shape[1]
        blocks = [pl.ds(at, min(TILE, width - at)) for at in range(0, width, TILE)]
        for at, grad in enumerate((self.gate, self.up)):
            rows = self.both[at, :, here]
            for block in blocks:
                grad[block, here] = jnp.dot(
                    self.xt_ref[block], rows, preferred_element_type=F32
                ).astype(BF16)
            self.send(at, grad.at[:, here], self.outs[at].at[:, there])
        hidden = self.both[2, :, here].T
        for block in blocks:
            self.down[here, block] = jnp.dot(
                hidden, self.y_ref[:, block], preferred_element_type=F32
            ).astype(BF16)
        self.send(2, self.down.at[here], self.outs[2].at[there])

    def wait(self):
        for copy in self.copies:
            copy.wait()


def grad_shapes(width, hidden_width):
    return [(width, hidden_width), (width, hidden_width), (hidden_width, width)]


def writer_scratch(width, rows, columns):
    return [
        pltpu.VMEM((3, rows, columns), BF16),
        *(pltpu.VMEM(shape, BF16) for shape in grad_shapes(width, columns)),
        pltpu.SemaphoreType.DMA((3, pl.cdiv(columns, TILE))),
    ]


def weight_grad_kernel(begin, held, xt_ref, y_ref, mine_ref, other_ref, _, *refs):
    outs, scratch = refs[held : held + 3], refs[held + 3 :]
    writer = Writer(begin, xt_ref, y_ref, mine_ref, other_ref, outs, scratch)
    for tile in writer.tiles:
        writer.tile(*tile)
    writer.wait()


def weight_grad(line, begin, hidden_width, xt, y, mine, other, grads, after):
    shapes = grad_shapes(xt.shape[0], hidden_width)
    return line.call(
        functools.partial(weight_grad_kernel, begin, len(grads)),
        (xt, y, mine, other, after, *grads),
        [shaped(*shape) for shape in shapes],
        in_specs=[IN_VMEM] * 5 + [IN_HBM] * len(grads),
        out_specs=[IN_HBM] * 3,
        scratch=writer_scratch(xt.shape[0], y.shape[0], mine.shape[1]),
        aliases={5 + at: at for at in range(len(grads))},
        limit=24,
    )


def last_kernel(grad_ref, keep_ref, send_ref):
    grad = grad_ref[...]
    rows = keep_ref.shape[0] // 2
    cuts = [grad[slot * rows : (slot + 1) * rows] for slot in range(4)]
    wa = lax.axis_index("wa")
    pieces = []
    for step in range(4):
        at = wa ^ step
        piece = cuts[0]
        for slot in range(1, len(cuts)):
            piece = jnp.where(at == slot, cuts[slot], piece)
        pieces.append(piece)
    keep_ref[...] = joined(*pieces[:2])
    send_ref[...] = joined(*pieces[2:]).astype(BF16)


def last_pieces(line, grad):
    shape = (grad.shape[0] // 2, grad.shape[1])
    return line.call(last_kernel, (grad,), [shaped(*shape, F32), shaped(*shape)])


def total_kernel(own_ref, *refs):
    total = own_ref[...]
    for ref in refs[:-1]:
        total = total + ref[...].astype(F32)
    refs[-1][...] = total.astype(BF16)


def total(line, own, received):
    return line.call(total_kernel, (own, *received), [shaped(*own.shape)])[0]


def swap(value, axis, size, step):
    return lax.ppermute(value, axis, [(at, at ^ step) for at in range(size)])


def fast_body(n_wa, n_ha, n_row, tokens, cotangent, gate_weight, up_weight, down_weight):
    hidden_width = gate_weight.shape[1]
    tiles = hidden_width // LANES
    ends = [-(-tiles * (at + 1) // CHUNKS) * LANES for at in range(CHUNKS)]
    chunks = [(begin, end - begin) for begin, end in zip([0] + ends, ends)]
    axes = [((1, 2), (2, 1))[at % 2] for at in range(CHUNKS)]
    line = Line()

    both = jnp.concatenate([tokens, cotangent], axis=0)
    pieces = [both] + [swap(both, "ha", n_ha, step) for step in range(1, n_ha)]
    gate, up = load(Line(), gate_weight, up_weight)
    xy = order_rows(line, pieces)
    xy_other = swap(xy, "row", n_row, 1)

    kept, got = [], []
    for at, ((begin, columns), axis) in enumerate(zip(chunks, axes)):
        keep, send = forward(line, begin, columns, axis, xy, gate, up, down_weight)
        kept.append(keep)
        got.append(swap(send, "wa", n_wa, axis[0]))
    for at, (_, far) in enumerate(axes):
        kept[at], send = halve(line, kept[at], got[at])
        got[at] = swap(send, "wa", n_wa, far)
    order = [1, 0, 3, 2]
    for at in order:
        kept[at] = middle(line, kept[at], got[at])
        got[at] = swap(kept[at], "wa", n_wa, axes[at][0])
    for at in [1, 0, 3, 2]:
        far = axes[at][1]
        kept[at] = join(line, kept[at], got[at])
        got[at] = swap(kept[at], "wa", n_wa, far)

    mine, other, grad = [], [], ()
    for at in range(0, CHUNKS, 2):
        pair = slice(at, at + 2)
        mine.append(stack(line, axes[pair], list(zip(kept, got))[pair]))
        other.append(swap(mine[-1], "row", n_row, 1))
        grad = input_grad(line, chunks[at][0], mine[-1], gate, up, grad)
    keep, send = last_pieces(line, grad[0])
    received = swap(send, "ha", n_ha, 2)
    xt, y_all = factors(line, xy, xy_other)
    grads = weight_grad(line, 0, hidden_width, xt, y_all, mine[0], other[0], (), other[1])
    keep, send = halve(line, keep, received)
    received = swap(send, "ha", n_ha, 1)
    grads = weight_grad(
        line, mine[0].shape[1], hidden_width, xt, y_all, mine[1], other[1], grads, other[0]
    )
    return (total(line, keep, [received]), *grads)


def plain_body(tokens, cotangent, gate_weight, up_weight, down_weight):
    hidden_width = gate_weight.shape[1]
    x = lax.all_gather(tokens, "ha", axis=0, tiled=True)
    y = lax.all_gather(cotangent, "ha", axis=0, tiled=True)
    gate_part = jnp.dot(x, gate_weight, preferred_element_type=F32)
    up_part = jnp.dot(x, up_weight, preferred_element_type=F32)
    dh_part = lax.dot_general(y, down_weight, NT, preferred_element_type=F32)
    summed = lax.psum(jnp.concatenate([gate_part, up_part, dh_part], axis=1), "wa")
    hidden, d_gate, d_up = pointwise(
        summed[:, :hidden_width],
        summed[:, hidden_width : 2 * hidden_width],
        summed[:, 2 * hidden_width :],
    )
    partial = lax.dot_general(
        d_gate, gate_weight, NT, preferred_element_type=F32
    ) + lax.dot_general(d_up, up_weight, NT, preferred_element_type=F32)
    grad_tokens = lax.psum_scatter(partial, "ha", scatter_dimension=0, tiled=True)
    grads = (
        lax.dot_general(x, d_gate, TN, preferred_element_type=F32),
        lax.dot_general(x, d_up, TN, preferred_element_type=F32),
        lax.dot_general(hidden, y, TN, preferred_element_type=F32),
    )
    return (
        grad_tokens.astype(BF16),
        *(lax.psum(g.astype(BF16), "row").astype(BF16) for g in grads),
    )


def solution(mesh):
    n_wa, n_ha, n_row = (mesh.shape[name] for name in ("wa", "ha", "row"))

    def body(tokens, cotangent, gate_weight, up_weight, down_weight):
        width, hidden_width = gate_weight.shape
        fits = (
            n_wa == n_ha == 4
            and n_row == 2
            and width % LANES == 0
            and hidden_width % LANES == 0
            and hidden_width >= LANES * CHUNKS
            and width % (16 * CUTS) == 0
            and (tokens.shape[0] * n_ha) % 16 == 0
        )
        if fits:
            return fast_body(
                n_wa, n_ha, n_row, tokens, cotangent, gate_weight, up_weight, down_weight
            )
        return plain_body(tokens, cotangent, gate_weight, up_weight, down_weight)

    return jax.shard_map(
        body,
        mesh=mesh,
        in_specs=(
            P(("row", "ha"), "wa"),
            P(("row", "ha"), "wa"),
            P("wa", "ha"),
            P("wa", "ha"),
            P("ha", "wa"),
        ),
        out_specs=(P(("row", "ha"), "wa"), P("wa", "ha"), P("wa", "ha"), P("ha", "wa")),
        check_vma=False,
    )
```
